32 devices in a mesh: fsdp: 32 (over z, y, x, core).
Axes of the slice: x: 2, y: 2, z: 4, core: 2. Of those that a mesh axis runs over, the one named last changes fastest.
Arguments:
- tokens: bfloat16 [128, 128, 512], P('fsdp'), may hold values from -6 to 6
- norm1_gain: float32 [512], P('fsdp'), may hold values from 0.5 to 1.5
- norm1_bias: float32 [512], P('fsdp'), may hold values from -1 to 1
- qkv1_weight: float32 [786432], P('fsdp'), may hold values from -0.25 to 0.25
- query1_bias: float32 [512], P('fsdp'), may hold values from -1 to 1
- value1_bias: float32 [512], P('fsdp'), may hold values from -1 to 1
- proj1_weight: float32 [262144], P('fsdp'), may hold values from -1.5 to 1.5
- proj1_bias: float32 [512], P('fsdp'), may hold values from -1 to 1
- norm2_gain: float32 [512], P('fsdp'), may hold values from 0.5 to 1.5
- norm2_bias: float32 [512], P('fsdp'), may hold values from -1 to 1
- hidden_weight: float32 [1048576], P('fsdp'), may hold values from -0.25 to 0.25
- hidden_bias: float32 [2048], P('fsdp'), may hold values from -1 to 1
- output_weight: float32 [1048576], P('fsdp'), may hold values from -0.25 to 0.25
- output_bias: float32 [512], P('fsdp'), may hold values from -1 to 1
- norm3_gain: float32 [512], P('fsdp'), may hold values from 0.5 to 1.5
- norm3_bias: float32 [512], P('fsdp'), may hold values from -1 to 1
- qkv2_weight: float32 [786432], P('fsdp'), may hold values from -0.25 to 0.25
- query2_bias: float32 [512], P('fsdp'), may hold values from -1 to 1
- value2_bias: float32 [512], P('fsdp'), may hold values from -1 to 1
- proj2_weight: float32 [262144], P('fsdp'), may hold values from -1.5 to 1.5
- proj2_bias: float32 [512], P('fsdp'), may hold values from -1 to 1
- norm4_gain: float32 [512], P('fsdp'), may hold values from 0.5 to 1.5
- norm4_bias: float32 [512], P('fsdp'), may hold values from -1 to 1
- router_weight: float32 [2048], P('fsdp'), may hold values from -0.25 to 0.25
- expert_in_weight: float32 [4194304], P('fsdp'), may hold values from -0.25 to 0.25
- expert_in_bias: float32 [8192], P('fsdp'), may hold values from -1 to 1
- expert_out_weight: float32 [4194304], P('fsdp'), may hold values from -0.75 to 0.75
- expert_out_bias: float32 [2048], P('fsdp'), may hold values from -1 to 1
- routes: int32 [128, 128, 2], P('fsdp'), may hold values from 0 to 3, as said below
- priority: int32 [64, 256], P('fsdp'), may hold values from 0 to 255, each once within a row
- cotangent: bfloat16 [128, 128, 512], P('fsdp'), may hold values from -6 to 6
Outputs:
- activations: bfloat16 [128, 128, 512], P('fsdp')
- input_grad: bfloat16 [128, 128, 512], P('fsdp')
- norm1_gain_grad: float32 [512], P('fsdp')
- norm1_bias_grad: float32 [512], P('fsdp')
- qkv1_weight_grad: float32 [786432], P('fsdp')
- query1_bias_grad: float32 [512], P('fsdp')
- value1_bias_grad: float32 [512], P('fsdp')
- proj1_weight_grad: float32 [262144], P('fsdp')
- proj1_bias_grad: float32 [512], P('fsdp')
- norm2_gain_grad: float32 [512], P('fsdp')
- norm2_bias_grad: float32 [512], P('fsdp')
- hidden_weight_grad: float32 [1048576], P('fsdp')
- hidden_bias_grad: float32 [2048], P('fsdp')
- output_weight_grad: float32 [1048576], P('fsdp')
- output_bias_grad: float32 [512], P('fsdp')
- norm3_gain_grad: float32 [512], P('fsdp')
- norm3_bias_grad: float32 [512], P('fsdp')
- qkv2_weight_grad: float32 [786432], P('fsdp')
- query2_bias_grad: float32 [512], P('fsdp')
- value2_bias_grad: float32 [512], P('fsdp')
- proj2_weight_grad: float32 [262144], P('fsdp')
- proj2_bias_grad: float32 [512], P('fsdp')
- norm4_gain_grad: float32 [512], P('fsdp')
- norm4_bias_grad: float32 [512], P('fsdp')
- router_weight_grad: float32 [2048], P('fsdp')
- expert_in_weight_grad: float32 [4194304], P('fsdp')
- expert_in_bias_grad: float32 [8192], P('fsdp')
- expert_out_weight_grad: float32 [4194304], P('fsdp')
- expert_out_bias_grad: float32 [2048], P('fsdp')
The draws below stay inside these ranges and needn't reach their ends.
Inputs may be any that keep to these rules, and one draw needn't show every extreme that they name: `routes`: the two experts of a token differ. `priority`: each row, one group of 256 tokens, holds every rank once.
All inputs are finite; a program needn't handle non-finite values.
Results may differ from the reference program's by a relative error of at most 0.028.
Values may be sent and summed in bfloat16 or wider, within the bound.
A program may use at most 256 MiB of HBM per device.

```python
import math
import jax
import jax.numpy as jnp
from jax import lax

D = 512
HEADS = 8
HEAD_DIM = 64
FF = 2048
EXP_FF = 2048
EXPERTS = 4
PATCH = 128
GROUP = 256
CAP = 160
IMAGES = 128
NGROUPS = 64


def draw_routes(key, part):
    key = jax.random.fold_in(key, 11)
    subkeys = jax.random.split(key, 5)
    shape_rows = (IMAGES, PATCH)
    favoured = jax.random.randint(subkeys[0], (NGROUPS, 1), 0, EXPERTS, dtype=jnp.int32)
    favoured = jnp.broadcast_to(favoured, (NGROUPS, GROUP)).reshape(IMAGES, PATCH)
    holds_favoured = jax.random.randint(subkeys[1], shape_rows, 0, 1000, dtype=jnp.int32) < 700
    other_one = jax.random.randint(subkeys[2], shape_rows, 0, EXPERTS - 1, dtype=jnp.int32)
    other_two = jax.random.randint(subkeys[3], shape_rows, 0, EXPERTS - 2, dtype=jnp.int32)
    other_two = other_two + (other_two >= other_one).astype(jnp.int32)
    first_other = (favoured + 1 + other_one) % EXPERTS
    second_other = (favoured + 1 + other_two) % EXPERTS
    swapped = jax.random.randint(subkeys[4], shape_rows, 0, 2, dtype=jnp.int32) == 1
    first_expert = jnp.where(holds_favoured, jnp.where(swapped, first_other, favoured), first_other)
    second_expert = jnp.where(holds_favoured, jnp.where(swapped, favoured, first_other), second_other)
    return jnp.stack([first_expert, second_expert], -1).astype(jnp.int32)


def block_scale(rng, shape, cuts, least, largest):
    factor_of = 1.0
    for position, parts in cuts:
        heights = jax.random.uniform(jax.random.fold_in(jax.random.fold_in(rng, 6), position), (parts,), jnp.float32, least / len(cuts), largest / len(cuts))
        factor_of = factor_of * jnp.repeat(jnp.exp(heights), shape[position] // parts).reshape((-1,) + (1,) * (len(shape) - 1 - position))
    return factor_of


def gaussian(rng, extent, spread, reach, pieces=(), kind=jnp.bfloat16):
    values = spread * jax.random.normal(rng, extent, jnp.float32)
    if pieces:
        values = values * block_scale(rng, extent, pieces, -0.22, 0.18)
    return jnp.clip(values, -reach, reach).astype(kind)


def setup_inputs(seed: int = 0) -> dict:
    key_of = jax.random.split(jax.random.key(seed), 32)
    return {
        "tokens": gaussian(key_of[0], (IMAGES, PATCH, D), 1.0, 6.0, ((0, 32),)),
        "norm1_gain": jnp.clip(1.0 + 0.1 * jax.random.normal(key_of[1], (D,), jnp.float32), 0.5, 1.5),
        "norm1_bias": gaussian(key_of[2], (D,), 0.2, 1.0, ((0, 32),), jnp.float32),
        "qkv1_weight": gaussian(key_of[3], (3 * D * D,), D ** -0.5, 0.25, ((0, 32),), jnp.float32),
        "query1_bias": gaussian(key_of[4], (D,), 0.2, 1.0, ((0, 32),), jnp.float32),
        "value1_bias": gaussian(key_of[5], (D,), 0.2, 1.0, ((0, 32),), jnp.float32),
        "proj1_weight": gaussian(key_of[6], (D * D,), (D // 32) ** -0.5, 1.5, ((0, 32),), jnp.float32),
        "proj1_bias": gaussian(key_of[7], (D,), 0.2, 1.0, ((0, 32),), jnp.float32),
        "norm2_gain": jnp.clip(1.0 + 0.1 * jax.random.normal(key_of[8], (D,), jnp.float32), 0.5, 1.5),
        "norm2_bias": gaussian(key_of[9], (D,), 0.2, 1.0, ((0, 32),), jnp.float32),
        "hidden_weight": gaussian(key_of[10], (D * FF,), D ** -0.5, 0.25, ((0, 32),), jnp.float32),
        "hidden_bias": gaussian(key_of[11], (FF,), 0.2, 1.0, ((0, 32),), jnp.float32),
        "output_weight": gaussian(key_of[12], (FF * D,), (FF // 4) ** -0.5, 0.25, ((0, 32),), jnp.float32),
        "output_bias": gaussian(key_of[13], (D,), 0.2, 1.0, ((0, 32),), jnp.float32),
        "norm3_gain": jnp.clip(1.0 + 0.1 * jax.random.normal(key_of[14], (D,), jnp.float32), 0.5, 1.5),
        "norm3_bias": gaussian(key_of[15], (D,), 0.2, 1.0, ((0, 32),), jnp.float32),
        "qkv2_weight": gaussian(key_of[16], (3 * D * D,), D ** -0.5, 0.25, ((0, 32),), jnp.float32),
        "query2_bias": gaussian(key_of[17], (D,), 0.2, 1.0, ((0, 32),), jnp.float32),
        "value2_bias": gaussian(key_of[18], (D,), 0.2, 1.0, ((0, 32),), jnp.float32),
        "proj2_weight": gaussian(key_of[19], (D * D,), (D // 32) ** -0.5, 1.5, ((0, 32),), jnp.float32),
        "proj2_bias": gaussian(key_of[20], (D,), 0.2, 1.0, ((0, 32),), jnp.float32),
        "norm4_gain": jnp.clip(1.0 + 0.1 * jax.random.normal(key_of[21], (D,), jnp.float32), 0.5, 1.5),
        "norm4_bias": gaussian(key_of[22], (D,), 0.2, 1.0, ((0, 32),), jnp.float32),
        "router_weight": gaussian(key_of[23], (D * EXPERTS,), D ** -0.5, 0.25, ((0, 32),), jnp.float32),
        "expert_in_weight": gaussian(key_of[24], (EXPERTS * D * EXP_FF,), D ** -0.5, 0.25, ((0, 32),), jnp.float32),
        "expert_in_bias": gaussian(key_of[25], (EXPERTS * EXP_FF,), 0.2, 1.0, ((0, 32),), jnp.float32),
        "expert_out_weight": gaussian(key_of[26], (EXPERTS * EXP_FF * D,), (EXP_FF // 32) ** -0.5, 0.75, ((0, 32),), jnp.float32),
        "expert_out_bias": gaussian(key_of[27], (EXPERTS * D,), 0.2, 1.0, ((0, 32),), jnp.float32),
        "routes": draw_routes(jax.random.fold_in(key_of[31], 71), 0),
        "priority": jax.vmap(lambda own: jax.random.permutation(own, GROUP))(jax.random.split(key_of[29], NGROUPS)).reshape((NGROUPS, GROUP)).astype(jnp.int32),
        "cotangent": gaussian(key_of[30], (IMAGES, PATCH, D), 1.0, 6.0, ((0, 32),)),
    }


@jax.custom_vjp
def low(v):
    return lax.optimization_barrier(v.astype(jnp.bfloat16)).astype(jnp.float32)

@jax.custom_vjp
def low_back(v):
    return v

def low_keep(v):
    return (low(v), None)

def low_pass(kept, grad):
    return (grad,)

def back_keep(v):
    return (v, None)

def back_low(kept, grad):
    return (low(grad),)
low.defvjp(low_keep, low_pass)
low_back.defvjp(back_keep, back_low)

def matmul(left_side, right_side):
    return jnp.dot(left_side, right_side, precision=lax.Precision.HIGHEST)

def layer_norm(values, norm_gain, norm_shift):
    centred = values - lax.optimization_barrier(jnp.mean(values, -1, keepdims=True))
    variance = lax.optimization_barrier(jnp.mean(centred * centred, -1, keepdims=True))
    return centred * lax.rsqrt(variance + 1e-06) * norm_gain + norm_shift

def softmax_last(scores):
    row_max = lax.optimization_barrier(jnp.max(scores, -1, keepdims=True))
    exponent = jnp.exp(scores - row_max)
    return exponent / lax.optimization_barrier(jnp.sum(exponent, -1, keepdims=True))

def slot_numbers(routes, priority):
    row_count = routes.shape[0]
    in_order = jnp.zeros((row_count,), jnp.int32).at[priority].set(jnp.arange(row_count, dtype=jnp.int32))
    ranked = routes[in_order]
    experts_range = jnp.arange(EXPERTS, dtype=jnp.int32)
    first_hot = (ranked[:, 0:1] == experts_range).astype(jnp.int32)
    second_hot = (ranked[:, 1:2] == experts_range).astype(jnp.int32)
    first_pos = lax.optimization_barrier(jnp.sum((jnp.cumsum(first_hot, 0) - first_hot) * first_hot, 1))
    first_total = lax.optimization_barrier(jnp.sum(first_hot, 0))
    second_pos = lax.optimization_barrier(jnp.sum((jnp.cumsum(second_hot, 0) - second_hot + first_total) * second_hot, 1))
    placed = jnp.stack([first_pos, second_pos], 1)[priority]
    slot_ids = routes * CAP + placed
    return jnp.where(placed < CAP, slot_ids, EXPERTS * CAP).astype(jnp.int32)

def attention(normed, qkv_weight, query_bias, value_bias, proj_weight, proj_bias):
    row_count = normed.shape[0]
    packed_bias = jnp.concatenate([query_bias, jnp.zeros_like(query_bias), value_bias])
    packed = low(low_back(matmul(low(normed), qkv_weight.reshape(D, 3 * D)) + packed_bias))
    packed = packed.reshape(row_count // PATCH, PATCH, 3, HEADS, HEAD_DIM)
    score_scale = 1.0 / math.sqrt(HEAD_DIM)
    scores = low_back(jnp.einsum('iqhd,ikhd->ihqk', packed[:, :, 0], packed[:, :, 1], precision=lax.Precision.HIGHEST) * score_scale)
    weights_low = low(softmax_last(scores))
    heads_out = jnp.einsum('ihqk,ikhd->iqhd', weights_low, packed[:, :, 2], precision=lax.Precision.HIGHEST)
    heads_low = low(low_back(heads_out.reshape(row_count, D)))
    return low_back(matmul(heads_low, proj_weight.reshape(D, D)) + proj_bias)

def routed(normed, router_weight, in_weight, in_bias, out_weight, out_bias, route_pair, ranking):
    normed_low = low(normed)
    logits = low_back(matmul(normed_low, router_weight.reshape(D, EXPERTS)))
    probs_all = softmax_last(logits)
    gates = jnp.take_along_axis(probs_all, route_pair, axis=1)
    slot_ids = slot_numbers(route_pair, ranking)
    padded_rows = jnp.zeros((EXPERTS * CAP + 1, D), jnp.float32)
    padded_rows = padded_rows.at[slot_ids[:, 0]].add(normed_low).at[slot_ids[:, 1]].add(normed_low)
    dispatched = padded_rows[:EXPERTS * CAP].reshape(EXPERTS, CAP, D)
    pre_act = low_back(jnp.einsum('ecd,edf->ecf', dispatched, in_weight.reshape(EXPERTS, D, EXP_FF), precision=lax.Precision.HIGHEST) + in_bias.reshape(EXPERTS, 1, EXP_FF))
    hidden = low(jax.nn.gelu(pre_act))
    expert_out = low_back(jnp.einsum('ecf,efd->ecd', hidden, out_weight.reshape(EXPERTS, EXP_FF, D), precision=lax.Precision.HIGHEST) + out_bias.reshape(EXPERTS, 1, D))
    out_table = jnp.concatenate([expert_out.reshape(EXPERTS * CAP, D), jnp.zeros((1, D), jnp.float32)], 0)
    return gates[:, 0:1] * out_table[slot_ids[:, 0]] + gates[:, 1:2] * out_table[slot_ids[:, 1]]

def forward(stream, weights, route_pair, ranking):
    norm1_gain, norm1_bias, qkv1_weight, query1_bias, value1_bias, proj1_weight, proj1_bias, norm2_gain, norm2_bias, hidden_weight, hidden_bias, output_weight, output_bias, norm3_gain, norm3_bias, qkv2_weight, query2_bias, value2_bias, proj2_weight, proj2_bias, norm4_gain, norm4_bias, router_weight, expert_in_weight, expert_in_bias, expert_out_weight, expert_out_bias = [low(weight) for weight in weights]
    stream = stream + attention(layer_norm(stream, norm1_gain, norm1_bias), qkv1_weight, query1_bias, value1_bias, proj1_weight, proj1_bias)
    normed = layer_norm(stream, norm2_gain, norm2_bias)
    pre_act = low_back(matmul(low(normed), hidden_weight.reshape(D, FF)) + hidden_bias)
    stream = stream + low_back(matmul(low(jax.nn.gelu(pre_act)), output_weight.reshape(FF, D)) + output_bias)
    stream = stream + attention(layer_norm(stream, norm3_gain, norm3_bias), qkv2_weight, query2_bias, value2_bias, proj2_weight, proj2_bias)
    return stream + routed(layer_norm(stream, norm4_gain, norm4_bias), router_weight, expert_in_weight, expert_in_bias, expert_out_weight, expert_out_bias, route_pair, ranking)

def reference(tokens, norm1_gain, norm1_bias, qkv1_weight, query1_bias, value1_bias, proj1_weight, proj1_bias, norm2_gain, norm2_bias, hidden_weight, hidden_bias, output_weight, output_bias, norm3_gain, norm3_bias, qkv2_weight, query2_bias, value2_bias, proj2_weight, proj2_bias, norm4_gain, norm4_bias, router_weight, expert_in_weight, expert_in_bias, expert_out_weight, expert_out_bias, routes, priority, cotangent):
    weights = (norm1_gain, norm1_bias, qkv1_weight, query1_bias, value1_bias, proj1_weight, proj1_bias, norm2_gain, norm2_bias, hidden_weight, hidden_bias, output_weight, output_bias, norm3_gain, norm3_bias, qkv2_weight, query2_bias, value2_bias, proj2_weight, proj2_bias, norm4_gain, norm4_bias, router_weight, expert_in_weight, expert_in_bias, expert_out_weight, expert_out_bias)
    streams = tokens.astype(jnp.float32).reshape(NGROUPS, GROUP, D)
    route_groups = routes.reshape(NGROUPS, GROUP, 2)
    cot_groups = cotangent.astype(jnp.float32).reshape(NGROUPS, GROUP, D)

    def group_step(totals, inputs):
        stream, route_pair, ranking, grad_final = inputs

        def group_forward(stream_in, weight_set):
            return forward(stream_in, weight_set, route_pair, ranking)
        result, pullback = jax.vjp(group_forward, stream, weights)
        grad_stream, grad_weights = pullback(grad_final)
        totals = tuple((summed + addend for summed, addend in zip(totals, grad_weights)))
        return (totals, (result.astype(jnp.bfloat16), grad_stream.astype(jnp.bfloat16)))
    zero_sums = tuple((jnp.zeros_like(weight) for weight in weights))
    totals, (results, grads_in) = lax.scan(group_step, zero_sums, (streams, route_groups, priority, cot_groups))
    return (results.reshape(IMAGES, PATCH, D), grads_in.reshape(IMAGES, PATCH, D), totals[0], totals[1], totals[2], totals[3], totals[4], totals[5], totals[6], totals[7], totals[8], totals[9], totals[10], totals[11], totals[12], totals[13], totals[14], totals[15], totals[16], totals[17], totals[18], totals[19], totals[20], totals[21], totals[22], totals[23], totals[24], totals[25], totals[26])
```

```python
import functools
import math
from typing import Any, NamedTuple

import jax
import jax.numpy as jnp
from jax import lax
from jax.experimental import pallas as pl
from jax.experimental.pallas import tpu as pltpu
from jax.sharding import PartitionSpec as P

D = 512
HEADS = 8
HEAD_DIM = 64
FF = 2048
EXP_FF = 2048
EXPERTS = 4
PATCH = 128
GROUP = 256
CAP = 160
SLOTS = EXPERTS * CAP
MESH = pl.DeviceIdType.MESH

(
    NORM1_GAIN,
    NORM1_BIAS,
    QKV1,
    QUERY1,
    VALUE1,
    PROJ1,
    PROJ1_BIAS,
    NORM2_GAIN,
    NORM2_BIAS,
    HIDDEN,
    HIDDEN_BIAS,
    OUTPUT,
    OUTPUT_BIAS,
    NORM3_GAIN,
    NORM3_BIAS,
    QKV2,
    QUERY2,
    VALUE2,
    PROJ2,
    PROJ2_BIAS,
    NORM4_GAIN,
    NORM4_BIAS,
    ROUTER,
    EXPERT_IN,
    EXPERT_IN_BIAS,
    EXPERT_OUT,
    EXPERT_OUT_BIAS,
) = NAMES = tuple(range(27))
BIG = {
    QKV1: (D, 3 * D),
    PROJ1: (D, D),
    HIDDEN: (D, FF),
    OUTPUT: (FF, D),
    QKV2: (D, 3 * D),
    PROJ2: (D, D),
    EXPERT_IN: (EXPERTS * D, EXP_FF),
    EXPERT_OUT: (EXPERTS * EXP_FF, D),
}
SMALL = tuple(name for name in NAMES if name not in BIG)
BIG_NAMES = tuple(BIG)
GAINS = (NORM1_GAIN, NORM1_BIAS, NORM2_GAIN, NORM2_BIAS, NORM3_GAIN, NORM3_BIAS, NORM4_GAIN, NORM4_BIAS)


def norm_forward(values, norm_gain, norm_shift):
    centred = values - jnp.mean(values, -1, keepdims=True)
    variance = jnp.mean(centred * centred, -1, keepdims=True)
    return centred * lax.rsqrt(variance + 1e-06) * norm_gain + norm_shift


def norm_backward(values, norm_gain, norm_shift, grad_normed):
    unused, pullback = jax.vjp(norm_forward, values, norm_gain, norm_shift)
    return pullback(grad_normed)


def gelu_backward(pre_act, grad_act):
    unused, pullback = jax.vjp(jax.nn.gelu, pre_act)
    return pullback(grad_act)[0]


def column_sums(matrix):
    return jnp.sum(matrix.astype(jnp.float32), 0)


def attention_forward(normed, qkv_weight, query_bias, value_bias, proj_weight, proj_bias):
    row_count = normed.shape[0]
    normed_low = normed.astype(jnp.bfloat16)
    packed_bias = jnp.concatenate([query_bias, jnp.zeros_like(query_bias), value_bias]).astype(
        jnp.float32
    )
    packed = jnp.dot(normed_low, qkv_weight, preferred_element_type=jnp.float32) + packed_bias
    packed = packed.astype(jnp.bfloat16).reshape(row_count // PATCH, PATCH, 3, HEADS, HEAD_DIM)
    queries = packed[:, :, 0]
    key_block = packed[:, :, 1]
    values = packed[:, :, 2]
    score_scale = 1.0 / math.sqrt(HEAD_DIM)
    scores = (
        jnp.einsum("iqhd,ikhd->ihqk", queries, key_block, preferred_element_type=jnp.float32)
        * score_scale
    )
    row_max = jnp.max(scores, -1, keepdims=True)
    exponent = jnp.exp(scores - row_max)
    row_total = jnp.sum(exponent, -1, keepdims=True)
    weights_low = (exponent / row_total).astype(jnp.bfloat16)
    logsum = row_max + jnp.log(row_total)
    mixed_heads = jnp.einsum(
        "ihqk,ikhd->iqhd", weights_low, values, preferred_element_type=jnp.float32
    )
    mixed_heads = mixed_heads.reshape(row_count, D).astype(jnp.bfloat16)
    output = jnp.dot(
        mixed_heads, proj_weight, preferred_element_type=jnp.float32
    ) + proj_bias.astype(jnp.float32)
    return (output, (normed_low, queries, key_block, values, logsum, mixed_heads))


def attention_backward(grad_output, saved_state, qkv_weight, proj_weight):
    normed_low, queries, key_block, values, logsum, mixed_heads = saved_state
    row_count = normed_low.shape[0]
    grad_low = grad_output.astype(jnp.bfloat16)
    grad_proj_weight = jnp.einsum(
        "rd,re->de", mixed_heads, grad_low, preferred_element_type=jnp.float32
    )
    grad_proj_bias = column_sums(grad_low)
    grad_mixed = jnp.einsum("re,de->rd", grad_low, proj_weight, preferred_element_type=jnp.float32)
    grad_mixed = grad_mixed.astype(jnp.bfloat16).reshape(row_count // PATCH, PATCH, HEADS, HEAD_DIM)
    score_scale = 1.0 / math.sqrt(HEAD_DIM)
    scores = (
        jnp.einsum("iqhd,ikhd->ihqk", queries, key_block, preferred_element_type=jnp.float32)
        * score_scale
    )
    weights_full = jnp.exp(scores - logsum)
    weights_low = weights_full.astype(jnp.bfloat16)
    grad_weights = jnp.einsum(
        "iqhd,ikhd->ihqk", grad_mixed, values, preferred_element_type=jnp.float32
    )
    grad_values = jnp.einsum(
        "ihqk,iqhd->ikhd", weights_low, grad_mixed, preferred_element_type=jnp.float32
    )
    inner_sum = jnp.sum(grad_weights * weights_full, -1, keepdims=True)
    grad_scores = (weights_full * (grad_weights - inner_sum)).astype(jnp.bfloat16)
    grad_queries = (
        jnp.einsum("ihqk,ikhd->iqhd", grad_scores, key_block, preferred_element_type=jnp.float32)
        * score_scale
    )
    grad_keys = (
        jnp.einsum("ihqk,iqhd->ikhd", grad_scores, queries, preferred_element_type=jnp.float32)
        * score_scale
    )
    grad_packed = (
        jnp.stack([grad_queries, grad_keys, grad_values], 2)
        .reshape(row_count, 3 * D)
        .astype(jnp.bfloat16)
    )
    grad_qkv_weight = jnp.einsum(
        "rd,re->de", normed_low, grad_packed, preferred_element_type=jnp.float32
    )
    grad_query_bias = column_sums(grad_packed[:, :D])
    grad_value_bias = column_sums(grad_packed[:, 2 * D :])
    grad_normed = jnp.einsum(
        "re,de->rd", grad_packed, qkv_weight, preferred_element_type=jnp.float32
    )
    return (
        grad_normed,
        (grad_qkv_weight, grad_query_bias, grad_value_bias, grad_proj_weight, grad_proj_bias),
    )


def feed_forward(normed, in_weight, in_bias, out_weight, out_bias):
    normed_low = normed.astype(jnp.bfloat16)
    pre_act = jnp.dot(normed_low, in_weight, preferred_element_type=jnp.float32) + in_bias.astype(
        jnp.float32
    )
    activation = jax.nn.gelu(pre_act).astype(jnp.bfloat16)
    output = jnp.dot(activation, out_weight, preferred_element_type=jnp.float32) + out_bias.astype(
        jnp.float32
    )
    return (output, (normed_low, pre_act, activation))


def feed_backward(grad_output, saved_state, in_weight, out_weight):
    normed_low, pre_act, activation = saved_state
    grad_low = grad_output.astype(jnp.bfloat16)
    grad_out_weight = jnp.einsum(
        "rf,rd->fd", activation, grad_low, preferred_element_type=jnp.float32
    )
    grad_out_bias = column_sums(grad_low)
    grad_activation = jnp.einsum(
        "rd,fd->rf", grad_low, out_weight, preferred_element_type=jnp.float32
    )
    grad_pre = gelu_backward(pre_act, grad_activation).astype(jnp.bfloat16)
    grad_in_weight = jnp.einsum(
        "rd,rf->df", normed_low, grad_pre, preferred_element_type=jnp.float32
    )
    grad_in_bias = column_sums(grad_pre)
    grad_normed = jnp.einsum("rf,df->rd", grad_pre, in_weight, preferred_element_type=jnp.float32)
    return (grad_normed, (grad_in_weight, grad_in_bias, grad_out_weight, grad_out_bias))


TILE = 512
F32 = jnp.float32
LOW = jnp.bfloat16
ROWS = 512
CHUNK = 64
COUNT = len(BIG_NAMES)
A_QKV1, A_PROJ1, A_HIDDEN, A_OUTPUT, A_QKV2, A_PROJ2, A_IN, A_OUT, A_SMALL = range(COUNT + 1)
VECTORS = (
    NORM1_GAIN,
    NORM1_BIAS,
    QUERY1,
    VALUE1,
    PROJ1_BIAS,
    NORM2_GAIN,
    NORM2_BIAS,
    OUTPUT_BIAS,
    NORM3_GAIN,
    NORM3_BIAS,
    QUERY2,
    VALUE2,
    PROJ2_BIAS,
    NORM4_GAIN,
    NORM4_BIAS,
)
ROW_OF = {name: at for at, name in enumerate(VECTORS)}


def mm(left, right):
    return jnp.dot(left, right, preferred_element_type=F32)


def nt(left, right):
    return lax.dot_general(left, right, (((1,), (1,)), ((), ())), preferred_element_type=F32)


def tn(left, right):
    return lax.dot_general(left, right, (((0,), (0,)), ((), ())), preferred_element_type=F32)


def iota(shape, dimension):
    return lax.broadcasted_iota(jnp.int32, shape, dimension)


def chunks(body, rows=ROWS, init=0, size=CHUNK):
    def step(at, carry):
        return body(pl.ds(pl.multiple_of(at * size, size), size), carry)

    return lax.fori_loop(0, rows // size, step, init)


def normed(values):
    centred = values - jnp.mean(values, -1, keepdims=True)
    scale = lax.rsqrt(jnp.mean(centred * centred, -1, keepdims=True) + 1e-06)
    return centred * scale, scale


SQRT_2_PI = math.sqrt(2.0 / math.pi)


def gelu_parts(pre):
    squared = pre * pre
    bent = jnp.tanh(pre * (SQRT_2_PI + (SQRT_2_PI * 0.044715) * squared))
    return squared, bent, 0.5 + 0.5 * bent


def gelu_low(pre):
    return (pre * gelu_parts(pre)[2]).astype(LOW)


def gelu_and_slope(pre):
    squared, bent, half = gelu_parts(pre)
    slope = half + (0.5 * pre) * (1.0 - bent * bent) * (
        SQRT_2_PI + (3.0 * SQRT_2_PI * 0.044715) * squared
    )
    return (pre * half).astype(LOW), slope


def column_sum(values):
    return jnp.sum(values.astype(F32), 0, keepdims=True)


def place():
    me = lax.axis_index("fsdp")
    return me // 8, (me // 4) % 2, (me // 2) % 2, me % 2


def device(z, y, x, core):
    return (((z * 2 + y) * 2 + x) * 2 + core,)


def partners(z, y, x, core):
    found = [device((z + step) % 4, y, x, core) for step in (1, 2, 3)]
    return found + [device(z, y, 1 - x, core), device(z, 1 - y, x, core), device(z, y, x, 1 - core)]


def greet(devices):
    barrier = pltpu.get_barrier_semaphore()
    for one in devices:
        pl.semaphore_signal(barrier, inc=1, device_id=one, device_id_type=MESH)
    pl.semaphore_wait(barrier, len(devices))


class Link:
    def __init__(self, items, send, recv):
        self.items, self.send, self.recv = items, send, recv
        self.z, self.y, self.x, self.core = place()

    def copy(self, item, message, source, target, to):
        return pltpu.make_async_remote_copy(
            src_ref=source,
            dst_ref=target,
            send_sem=self.send.at[item, message],
            recv_sem=self.recv.at[item, message],
            device_id=to,
            device_id_type=MESH,
        )

    def rows(self, item):
        which, first, rows = self.items[item]
        return which, pl.ds(first, rows)


class Gather(Link):
    messages = 11
    leads = (0, 2, 4, 6, 8)

    def __init__(self, items, shards, wholes, prepare, send, recv, local):
        super().__init__(items, send, recv)
        self.shards, self.wholes, self.prepare, self.local = shards, wholes, prepare, local
        self.ready, self.tick = set(), 0

    def block(self, item, zs, y, x, core):
        which, rows = self.rows(item)
        return self.wholes[which].at[zs, y, x, core, rows]

    def source(self, item):
        which, rows = self.rows(item)
        return self.shards[which].at[rows]

    def own(self, item):
        target = self.block(item, self.z, self.y, self.x, self.core)
        return pltpu.make_async_copy(self.source(item), target, self.local.at[item])

    def along_z(self, item):
        z, y, x, core = self.z, self.y, self.x, self.core
        source = self.source(item)
        target = self.block(item, z, y, x, core)
        return [
            self.copy(item, step - 1, source, target, device((z + step) % 4, y, x, core))
            for step in (1, 2, 3)
        ]

    def same(self, item, message, zs, y, x, core, to):
        part = self.block(item, zs, y, x, core)
        return self.copy(item, message, part, part, to)

    def across(self, item):
        z, y, x, core = self.z, self.y, self.x, self.core
        return [
            self.same(item, 3, slice(None), y, x, core, device(z, y, 1 - x, core)),
            self.same(item, 4, slice(None), y, x, core, device(z, 1 - y, x, core)),
        ]

    def onward(self, item):
        z, y, x, core = self.z, self.y, self.x, self.core
        return [
            self.same(item, 5, pl.ds(0, 2), y, 1 - x, core, device(z, 1 - y, x, core)),
            self.same(item, 6, pl.ds(2, 2), 1 - y, x, core, device(z, y, 1 - x, core)),
        ]

    def pair(self, item, which):
        z, y, x, core = self.z, self.y, self.x, self.core
        ys, xs = ((y, x), (y, 1 - x), (1 - y, x), (1 - y, 1 - x))[which]
        return self.same(item, 7 + which, slice(None), ys, xs, core, device(z, y, x, 1 - core))

    def stage(self, number, item):
        if number == 0:
            self.prepare(item)
            self.own(item).start()
            for one in self.along_z(item):
                one.start()
        elif number == 1:
            self.own(item).wait()
            for one in self.along_z(item):
                one.wait_recv()
            for one in self.across(item):
                one.start()
            self.pair(item, 0).start()
        elif number == 2:
            for one in self.across(item):
                one.wait_recv()
            for one in self.onward(item):
                one.start()
            self.pair(item, 1).start()
            self.pair(item, 2).start()
        elif number == 3:
            for one in self.onward(item):
                one.wait_recv()
            self.pair(item, 3).start()
        else:
            for which in range(4):
                self.pair(item, which).wait_recv()
            self.ready.add(item)

    def step(self):
        if len(self.ready) == len(self.items):
            return False
        for number in reversed(range(5)):
            item = self.tick - self.leads[number]
            if 0 <= item < len(self.items):
                self.stage(number, item)
        self.tick += 1
        return True

    def need(self, which):
        wanted = {at for at, item in enumerate(self.items) if item[0] == which}
        while not wanted <= self.ready:
            self.step()

    def finish(self):
        for item in range(len(self.items)):
            sent = self.along_z(item) + self.across(item) + self.onward(item)
            for one in sent + [self.pair(item, which) for which in range(4)]:
                one.wait_send()


class Scatter(Link):
    messages = 8
    leads = (0, 1, 2, 3, 4, 5)
    slots = 6

    def __init__(self, items, grads, landing, own, landed, pool, halves, sides, ends, give, send, recv, local):
        super().__init__(items, send, recv)
        self.grads, self.landing = grads, landing
        self.own, self.landed, self.pool = own, landed, pool
        self.halves, self.sides, self.ends = halves, sides, ends
        self.give, self.local = give, local
        self.tick, self.made = 0, {}

    def slot(self, kind, item):
        which, first, rows = self.items[item]
        if which == A_SMALL:
            return kind[1]
        return kind[0].at[item % kind[0].shape[0], :, :, :, pl.ds(0, rows)]

    def load_own(self, item):
        which, rows = self.rows(item)
        source = self.grads[which].at[:, :, :, self.core, rows]
        return pltpu.make_async_copy(source, self.slot(self.own, item), self.local.at[item % 2])

    def load_landed(self, item):
        which, rows = self.rows(item)
        source = self.landing[which].at[:, :, :, rows]
        return pltpu.make_async_copy(source, self.slot(self.landed, item), self.local.at[2])

    def pair(self, item):
        which, rows = self.rows(item)
        return self.copy(
            item,
            0,
            self.grads[which].at[:, :, :, 1 - self.core, rows],
            self.landing[which].at[:, :, :, rows],
            device(self.z, self.y, self.x, 1 - self.core),
        )

    def half(self, item):
        which, rows = self.rows(item)
        z, y, x, core = self.z, self.y, self.x, self.core
        found = []
        for at, to in ((0, device(z, y, 1 - x, core)), (1, device(z, 1 - y, x, core))):
            source = self.slot(self.pool, item).at[pl.ds(2 * at, 2), 1 - y, 1 - x]
            target = self.halves[which].at[pl.ds(2 * at, 2), rows]
            found.append(self.copy(item, 1 + at, source, target, to))
        return found

    def side(self, item):
        which, rows = self.rows(item)
        z, y, x, core = self.z, self.y, self.x, self.core
        found = []
        for at, (ys, xs) in enumerate(((y, 1 - x), (1 - y, x))):
            source = self.slot(self.pool, item).at[:, ys, xs]
            target = self.sides[which].at[at, :, rows]
            found.append(self.copy(item, 3 + at, source, target, device(z, ys, xs, core)))
        return found

    def along_z(self, item):
        which, rows = self.rows(item)
        z, y, x, core = self.z, self.y, self.x, self.core
        found = []
        for step in (1, 2, 3):
            to = (z + step) % 4
            source = self.slot(self.pool, item).at[to, y, x]
            target = self.ends[which].at[step - 1, rows]
            found.append(self.copy(item, 4 + step, source, target, device(to, y, x, core)))
        return found

    def sent(self, item):
        for one in self.half(item) + self.side(item) + self.along_z(item):
            one.wait_send()

    def stage(self, number, item):
        which, rows = self.rows(item)
        z, y, x = self.z, self.y, self.x
        pool = self.slot(self.pool, item)
        if number == 0:
            for one in self.made[item]:
                one()
            self.load_own(item).start()
            self.pair(item).start()
        elif number == 1:
            self.pair(item).wait_recv()
            self.load_landed(item).start()
        elif number == 2:
            self.load_own(item).wait()
            self.load_landed(item).wait()
            if item >= self.slots:
                self.sent(item - self.slots)
            own, landed = self.slot(self.own, item), self.slot(self.landed, item)

            def add(at, carry):
                spot = (at // 4, at // 2 % 2, at % 2)
                pool[spot] = own[spot] + landed[spot]
                return carry

            lax.fori_loop(0, 16, add, 0)
            for one in self.half(item):
                one.start()
        elif number == 3:
            for one in self.half(item):
                one.wait_recv()
            for at in range(4):
                spot = (at, 1 - y, x) if at < 2 else (at, y, 1 - x)
                pool[spot] = pool[spot] + self.halves[which][at, rows]
            for one in self.side(item):
                one.start()
        elif number == 4:
            for one in self.side(item):
                one.wait_recv()
            sides = self.sides[which]
            for at in range(4):
                total = pool[at, y, x].astype(F32) + sides[0, at, rows].astype(F32)
                pool[at, y, x] = (total + sides[1, at, rows].astype(F32)).astype(pool.dtype)
            for one in self.along_z(item):
                one.start()
        else:
            for one in self.along_z(item):
                one.wait_recv()
            total = pool[z, y, x].astype(F32)
            for step in range(3):
                total = total + self.ends[which][step, rows].astype(F32)
            self.give(self.items[item], total)

    def step(self):
        count = len(self.items)
        if self.tick >= count + self.leads[-1]:
            return False
        if self.tick < count and self.tick not in self.made:
            return False
        for number in reversed(range(6)):
            item = self.tick - self.leads[number]
            if 0 <= item < count:
                self.stage(number, item)
        self.tick += 1
        return True

    def finish(self):
        count = len(self.items)
        for item in range(count):
            self.pair(item).wait_send()
        for item in range(max(0, count - self.slots), count):
            self.sent(item)


class Ring:
    def __init__(self, slots, semaphores):
        self.slots, self.semaphores = slots, semaphores
        self.count = slots.shape[0]
        self.under_way = [None] * self.count
        self.next = 0

    def copy(self, slot, target):
        return pltpu.make_async_copy(self.slots.at[slot], target, self.semaphores.at[slot])

    def settle(self, slot):
        if self.under_way[slot] is not None:
            self.under_way[slot].wait()
            self.under_way[slot] = None

    def settle_all(self):
        for slot in range(self.count):
            self.settle(slot)

    def put(self, values, target):
        slot, self.next = self.next, (self.next + 1) % self.count
        self.settle(slot)
        self.slots[slot] = values.astype(LOW).reshape(self.slots.shape[1:])
        copy = self.copy(slot, target)
        copy.start()
        self.under_way[slot] = copy

        def wait():
            if self.under_way[slot] is copy:
                self.settle(slot)

        return wait

    def put_at(self, slot, values, target):
        self.slots[slot] = values.astype(LOW).reshape(self.slots.shape[1:])
        self.copy(slot, target).start()

    def note(self, targets):
        for slot, target in enumerate(targets):
            self.under_way[slot] = self.copy(slot, target)


class Inputs(NamedTuple):
    tokens: Any
    cotangent: Any
    info: Any
    small: Any
    shards: Any


class Outputs(NamedTuple):
    activations: Any
    input_grad: Any
    small: Any
    grads: Any
    wholes: Any
    made: Any
    landing: Any


class Scratch(NamedTuple):
    low: Any
    resident: Any
    small_whole: Any
    small_grad: Any
    flat: Any
    vec: Any
    vec_ff: Any
    vec_out: Any
    router: Any
    grad_vec: Any
    grad_ff: Any
    grad_out: Any
    grad_router: Any
    stream: Any
    norm: Any
    packed: Any
    heads: Any
    probs: Any
    side: Any
    slots: Any
    dispatched: Any
    slot_grad: Any
    weight_in: Any
    weight_out: Any
    grad: Any
    table: Any
    wide: Any
    wide2: Any
    thin: Any
    thin2: Any
    grad_packed: Any
    ring_a: Any
    ring_b: Any
    ring_c: Any
    own: Any
    landed: Any
    pool: Any
    own_small: Any
    landed_small: Any
    pool_small: Any
    landing_small: Any
    halves: Any
    sides: Any
    ends: Any
    gather_send: Any
    gather_recv: Any
    gather_local: Any
    scatter_send: Any
    scatter_recv: Any
    scatter_local: Any
    ring_a_sem: Any
    ring_b_sem: Any
    ring_c_sem: Any
    fetch: Any


class Step:
    def __init__(self, plan, inputs, outputs, scratch):
        self.plan, self.i, self.o, self.s = plan, inputs, outputs, scratch
        s = scratch
        wholes = list(s.resident) + list(outputs.wholes) + [s.small_whole]
        made = list(outputs.made) + [s.small_grad]
        self.wholes, self.made = wholes, made
        self.prepared = set()
        self.gather = Gather(
            plan.gather_items,
            list(s.low) + [inputs.small],
            wholes,
            self.prepare,
            s.gather_send,
            s.gather_recv,
            s.gather_local,
        )
        self.scatter = Scatter(
            plan.scatter_items,
            made,
            list(outputs.landing) + [s.landing_small],
            (s.own, s.own_small),
            (s.landed, s.landed_small),
            (s.pool, s.pool_small),
            s.halves,
            s.sides,
            s.ends,
            self.give,
            s.scatter_send,
            s.scatter_recv,
            s.scatter_local,
        )
        self.ring_a = Ring(s.ring_a, s.ring_a_sem)
        self.ring_b = Ring(s.ring_b, s.ring_b_sem)
        self.ring_c = Ring(s.ring_c, s.ring_c_sem)
        self.tiles_made = {}


    def prepare(self, item):
        which = self.plan.gather_items[item][0]
        if which in self.prepared or which == A_SMALL:
            return
        self.prepared.add(which)
        tiles, rows = self.plan.tiles[which], self.plan.rows[which]
        view, low = self.i.shards[which], self.s.low[which]
        for tile in range(tiles):
            for quarter in range(4):
                found = view[pl.ds(4 * tile + quarter, rows, stride=4 * tiles), :]
                low[tile * rows : (tile + 1) * rows, 128 * quarter : 128 * quarter + 128] = found.astype(LOW)

    def give(self, item, total):
        which, first, count = item
        if which == A_SMALL:
            self.o.small[...] = total
            return
        tiles, rows = self.plan.tiles[which], self.plan.rows[which]
        view = self.o.grads[which]
        at = first
        while at < first + count:
            tile, row = at // rows, at % rows
            take = min(rows - row, first + count - at)
            part = total[at - first : at - first + take]
            for quarter in range(4):
                start = 4 * tiles * row + 4 * tile + quarter
                view[pl.ds(start, take, stride=4 * tiles), :] = part[:, 128 * quarter : 128 * quarter + 128]
            at += take


    def breathe(self):
        self.gather.step()
        self.scatter.step()

    def finished(self, which, tile, wait):
        self.tiles_made[which, tile] = wait
        for item, (one, first, rows) in enumerate(self.plan.scatter_items):
            if item in self.scatter.made or one != which:
                continue
            wanted = [(which, tile) for tile in self.plan.made_of(which, first, rows)]
            if all(key in self.tiles_made for key in wanted):
                self.scatter.made[item] = [self.tiles_made[key] for key in wanted]


    def column_tile(self, which, tile):
        rows = self.plan.rows[which]
        return self.wholes[which][:, :, :, :, pl.ds(tile * rows, rows), :].reshape(TILE, TILE)

    def row_tile(self, which, tile):
        return self.wholes[which][tile].reshape(TILE, TILE)

    def fetch(self, expert, out):
        source = self.o.wholes[1 if out else 0].at[expert]
        target = self.s.weight_out if out else self.s.weight_in
        return pltpu.make_async_copy(source, target, self.s.fetch.at[1 if out else 0])

    def in_tile(self, tile):
        return self.s.weight_in[:, :, :, pl.ds(tile * 64, 64), :].reshape(TILE, TILE)

    def out_tile(self, tile):
        return self.s.weight_out[tile // 2, tile % 2].reshape(TILE, TILE)

    def row(self, name):
        at = ROW_OF[name]
        return self.s.vec[at : at + 1, :]

    def keep_row(self, name, values):
        at = ROW_OF[name]
        self.s.grad_vec[at : at + 1, :] = values


    def spread(self, width, first, each):
        lane, column = iota((128, width), 0), iota((128, width), 1)
        return jnp.where(lane == first + column % each, 1.0, 0.0).astype(LOW)

    def spread_router(self, expert):
        lane, column = iota((128, TILE), 0), iota((128, TILE), 1)
        return jnp.where(lane == 64 + 4 * (column % 16) + expert, 1.0, 0.0).astype(LOW)

    def unpack_small(self):
        s = self.s
        s.flat[...] = s.small_whole[...].reshape(256, 128)
        device_row, column = iota((32, TILE), 0), iota((32, TILE), 1)
        found = [s.flat[pl.ds(row, 32, stride=8), :].astype(LOW) for row in (0, 1, 2, 5)]
        mine = device_row == column // 16
        for at in range(len(VECTORS)):
            wide = mm(found[at // 8], self.spread(TILE, at % 8 * 16, 16))
            s.vec[at : at + 1, :] = jnp.sum(jnp.where(mine, wide, 0.0), 0, keepdims=True)
        s.router[...] = jnp.zeros((128, TILE), F32)
        for expert in range(EXPERTS):
            wide = mm(found[2], self.spread_router(expert))
            s.router[expert : expert + 1, :] = jnp.sum(jnp.where(mine, wide, 0.0), 0, keepdims=True)
        wide = mm(found[2], self.spread(FF, 0, 64))
        wide = jnp.where(iota((32, FF), 0) == iota((32, FF), 1) // 64, wide, 0.0)
        s.vec_ff[0:1, :] = jnp.sum(wide, 0, keepdims=True)
        wide = mm(found[3], self.spread(TILE, 0, 64))
        for expert in range(EXPERTS):
            part = jnp.where(device_row == 8 * expert + column // 64, wide, 0.0)
            s.vec_out[expert : expert + 1, :] = jnp.sum(part, 0, keepdims=True)
            for at in range(16):
                row = 8 * (8 * expert + at // 2) + 3 + at % 2
                s.vec_ff[1 + expert : 2 + expert, 128 * at : 128 * at + 128] = s.flat[row : row + 1, :]

    def pack_small(self):
        s = self.s
        device_row, column = iota((32, TILE), 0), iota((32, TILE), 1)
        mine = device_row == column // 16

        def back(values, one_hot):
            high = values.astype(LOW)
            rest = (values - high.astype(F32)).astype(LOW)
            return nt(high, one_hot) + nt(rest, one_hot)

        rows = [jnp.zeros((32, 128), F32) for _ in range(4)]
        for at in range(len(VECTORS)):
            values = jnp.where(mine, s.grad_vec[at : at + 1, :], 0.0)
            rows[at // 8] += back(values, self.spread(TILE, at % 8 * 16, 16))
        for expert in range(EXPERTS):
            values = jnp.where(mine, s.grad_router[expert : expert + 1, :], 0.0)
            rows[2] += back(values, self.spread_router(expert))
        own = iota((32, FF), 0) == iota((32, FF), 1) // 64
        rows[2] += back(jnp.where(own, s.grad_ff[0:1, :], 0.0), self.spread(FF, 0, 64))
        total = jnp.zeros((32, TILE), F32)
        for expert in range(EXPERTS):
            own = device_row == 8 * expert + column // 64
            total += jnp.where(own, s.grad_out[expert : expert + 1, :], 0.0)
        rows[3] = back(total, self.spread(TILE, 0, 64))
        s.flat[...] = jnp.zeros((256, 128), F32)
        for row, values in zip((0, 1, 2, 5), rows):
            s.flat[pl.ds(row, 32, stride=8), :] = values
        for expert in range(EXPERTS):
            for at in range(16):
                row = 8 * (8 * expert + at // 2) + 3 + at % 2
                s.flat[row : row + 1, :] = s.grad_ff[1 + expert : 2 + expert, 128 * at : 128 * at + 128]
        s.small_grad[...] = s.flat[...].reshape(4, 2, 2, 2, 8, 128)
        self.finished(A_SMALL, 0, lambda: None)


    def norm(self, source, target, gain, bias):
        gain, bias = self.row(gain), self.row(bias)

        def body(rows, carry):
            target[rows] = (normed(source[rows].astype(F32))[0] * gain + bias).astype(LOW)
            return carry

        chunks(body)

    def norm_back(self, source, back, gain, bias):
        wide, grad = self.row(gain), self.s.grad

        def body(rows, carry):
            to_gain, to_bias = carry
            unit, scale = normed(source[rows].astype(F32))
            found = back[rows]
            to_gain = to_gain + column_sum(found * unit)
            to_bias = to_bias + column_sum(found)
            found = found * wide
            mean = jnp.mean(found, -1, keepdims=True)
            along = jnp.mean(found * unit, -1, keepdims=True)
            grad[rows] = grad[rows] + scale * (found - mean - unit * along)
            return to_gain, to_bias

        zero = jnp.zeros((1, D), F32)
        to_gain, to_bias = chunks(body, init=(zero, zero))
        self.keep_row(gain, to_gain)
        self.keep_row(bias, to_bias)


    def masks(self):
        first = iota((PATCH, 128), 1) < HEAD_DIM
        return first, jnp.where(first, 1.0, 0.0).astype(LOW), jnp.where(first, 0.0, 1.0).astype(LOW)

    def scores(self, packed, rows, at, masks):
        query = packed[rows, 128 * at : 128 * at + 128]
        keys = packed[rows, D + 128 * at : D + 128 * at + 128]
        values = packed[rows, 2 * D + 128 * at : 2 * D + 128 * at + 128]
        query = jnp.concatenate([query * masks[1], query * masks[2]], 0)
        found = nt(query, keys) * (1.0 / math.sqrt(HEAD_DIM))
        found = jnp.exp(found - jnp.max(found, -1, keepdims=True))
        return query, keys, values, found / jnp.sum(found, -1, keepdims=True)

    def attention(self, block, source, target, names):
        s = self.s
        gain, bias, query, value, proj = names
        qkv_at, proj_at = (A_QKV1, A_PROJ1) if block == 0 else (A_QKV2, A_PROJ2)
        low, packed, heads = s.norm.at[0 if block == 0 else 2], s.packed.at[block], s.heads.at[block]
        self.norm(source, low, gain, bias)
        self.breathe()
        self.gather.need(qkv_at)
        for part in range(3):
            found = mm(low[...], self.column_tile(qkv_at, part))
            if part != 1:
                found = found + self.row(query if part == 0 else value)
            packed[:, part * D : (part + 1) * D] = found.astype(LOW)
        self.breathe()

        def image(number, carry):
            rows = pl.ds(pl.multiple_of(number * PATCH, PATCH), PATCH)
            masks = self.masks()
            for at in range(HEADS // 2):
                unused, unused, values, weights = self.scores(packed, rows, at, masks)
                found = mm(weights.astype(LOW), values)
                found = jnp.where(masks[0], found[:PATCH], found[PATCH:])
                heads[rows, 128 * at : 128 * at + 128] = found.astype(LOW)
            return carry

        lax.fori_loop(0, ROWS // PATCH, image, 0)
        self.breathe()
        self.gather.need(proj_at)
        found = mm(heads[...], self.column_tile(proj_at, 0)) + self.row(proj)
        target[...] = source[...].astype(F32) + found

    def low_and_sums(self, source, target):
        def body(rows, carry):
            found = source[rows].astype(LOW)
            target[rows] = found
            return carry + column_sum(found)

        return chunks(body, init=jnp.zeros((1, D), F32))

    def attention_back(self, block, source, names):
        s = self.s
        gain, bias, query_bias, value_bias, proj_bias = names
        qkv_at, proj_at = (A_QKV1, A_PROJ1) if block == 0 else (A_QKV2, A_PROJ2)
        low, packed, heads = s.norm.at[0 if block == 0 else 2], s.packed.at[block], s.heads.at[block]
        self.keep_row(proj_bias, self.low_and_sums(s.grad, s.thin))
        target = self.made[proj_at]
        self.finished(proj_at, 0, self.ring_a.put(tn(heads[...], s.thin[...]), target))
        s.thin2[...] = nt(s.thin[...], self.column_tile(proj_at, 0)).astype(LOW)
        self.breathe()
        scale = 1.0 / math.sqrt(HEAD_DIM)

        def image(number, carry):
            rows = pl.ds(pl.multiple_of(number * PATCH, PATCH), PATCH)
            masks = self.masks()
            for at in range(HEADS // 2):
                query, keys, values, weights = self.scores(packed, rows, at, masks)
                found = s.thin2[rows, 128 * at : 128 * at + 128]
                found = jnp.concatenate([found * masks[1], found * masks[2]], 0)
                to_weights = nt(found, values)
                to_values = tn(weights.astype(LOW), found)
                inner = jnp.sum(to_weights * weights, -1, keepdims=True)
                to_scores = (weights * (to_weights - inner)).astype(LOW)
                to_query = mm(to_scores, keys) * scale
                to_query = jnp.where(masks[0], to_query[:PATCH], to_query[PATCH:])
                to_keys = tn(to_scores, query) * scale
                for part, one in enumerate((to_query, to_keys, to_values)):
                    s.grad_packed[rows, part * D + 128 * at : part * D + 128 * at + 128] = one.astype(LOW)
            return carry

        lax.fori_loop(0, 2, image, 0)
        self.breathe()
        lax.fori_loop(2, 4, image, 0)
        self.breathe()

        def body(rows, carry):
            return (
                carry[0] + column_sum(s.grad_packed[rows, :D]),
                carry[1] + column_sum(s.grad_packed[rows, 2 * D :]),
            )

        zero = jnp.zeros((1, D), F32)
        to_query, to_value = chunks(body, init=(zero, zero))
        self.keep_row(query_bias, to_query)
        self.keep_row(value_bias, to_value)
        for part in range(3):
            found = s.grad_packed[:, part * D : (part + 1) * D]
            target = self.made[qkv_at].at[:, :, :, :, pl.ds(16 * part, 16)]
            self.finished(qkv_at, part, self.ring_a.put(tn(low[...], found), target))
            back = nt(found, self.column_tile(qkv_at, part))
            s.wide[...] = back if part == 0 else s.wide[...] + back
        self.breathe()
        self.norm_back(source, s.wide, gain, bias)
        self.breathe()


    def feed(self, source, target):
        s = self.s
        low = s.norm.at[1]
        self.norm(source, low, NORM2_GAIN, NORM2_BIAS)
        self.breathe()
        self.gather.need(A_HIDDEN)
        self.gather.need(A_OUTPUT)
        for tile in range(FF // TILE):
            s.wide[...] = mm(low[...], self.column_tile(A_HIDDEN, tile))
            bias = s.vec_ff[0:1, tile * TILE : (tile + 1) * TILE]

            def body(rows, carry, bias=bias):
                s.thin[rows] = gelu_low(s.wide[rows] + bias)
                return carry

            chunks(body)
            found = mm(s.thin[...], self.row_tile(A_OUTPUT, tile))
            if tile == 0:
                target[...] = source[...] + self.row(OUTPUT_BIAS) + found
            else:
                target[...] = target[...] + found
            if tile % 2:
                self.breathe()

    def feed_back(self, source):
        s = self.s
        low = s.norm.at[1]
        self.keep_row(OUTPUT_BIAS, self.low_and_sums(s.grad, s.thin))
        for tile in range(FF // TILE):
            columns = slice(tile * TILE, (tile + 1) * TILE)
            s.wide[...] = mm(low[...], self.column_tile(A_HIDDEN, tile))
            s.wide2[...] = nt(s.thin[...], self.row_tile(A_OUTPUT, tile))
            bias = s.vec_ff[0:1, columns]

            def body(rows, carry, bias=bias):
                active, slope = gelu_and_slope(s.wide[rows] + bias)
                s.thin2[rows] = active
                found = (slope * s.wide2[rows]).astype(LOW)
                s.grad_packed[rows, :TILE] = found
                return carry + column_sum(found)

            s.grad_ff[0:1, columns] = chunks(body, init=jnp.zeros((1, TILE), F32))
            found = tn(s.thin2[...], s.thin[...])
            self.finished(A_OUTPUT, tile, self.ring_b.put(found, self.made[A_OUTPUT].at[tile]))
            to_pre = s.grad_packed[:, :TILE]
            target = self.made[A_HIDDEN].at[:, :, :, :, pl.ds(16 * tile, 16)]
            self.finished(A_HIDDEN, tile, self.ring_a.put(tn(low[...], to_pre), target))
            back = nt(to_pre, self.column_tile(A_HIDDEN, tile))
            if tile == 0:
                s.side[...] = back
            else:
                s.side[...] = s.side[...] + back
            self.breathe()
        self.norm_back(source, s.side, NORM2_GAIN, NORM2_BIAS)
        self.breathe()


    def route(self):
        s = self.s
        lane = iota((ROWS, 128), 1)
        logits = jnp.where(lane < EXPERTS, nt(s.norm[3], s.router[...].astype(LOW)), -1e30)
        found = jnp.exp(logits - jnp.max(logits, -1, keepdims=True))
        s.probs[...] = found / jnp.sum(found, -1, keepdims=True)
        same = iota((GROUP, GROUP), 0) == iota((GROUP, GROUP), 1)

        def upright(row):
            return jnp.sum(jnp.where(same, row, 0.0), 1, keepdims=True)

        lane = iota((GROUP, 128), 1)
        for group in range(ROWS // GROUP):
            rows = slice(group * GROUP, (group + 1) * GROUP)
            first, second, rank = (self.i.info[8 * group + at : 8 * group + at + 1, :] for at in range(3))
            first_up, second_up, rank_up = upright(first), upright(second), upright(rank)
            before = jnp.where(rank_up < rank, 1.0, 0.0)
            place_first = jnp.sum(jnp.where(first_up == first, before, 0.0), 0, keepdims=True)
            place_second = jnp.sum(
                jnp.where(second_up == second, before, 0.0) + jnp.where(first_up == second, 1.0, 0.0),
                0,
                keepdims=True,
            )
            kept = []
            for at, (expert, spot) in enumerate(((first, place_first), (second, place_second))):
                slot = jnp.where(spot < CAP, expert * CAP + spot, -1.0)
                s.slots[2 * group + at : 2 * group + at + 1, :] = slot
                kept.append(upright(slot))
            probs = s.probs[rows]
            gates = [
                jnp.sum(jnp.where(lane == one.astype(jnp.int32), probs, 0.0), -1, keepdims=True)
                for one in (first_up, second_up)
            ]
            columns = [first_up, second_up] + gates + kept
            table = jnp.zeros((GROUP, 128), F32)
            for at, one in enumerate(columns):
                table = jnp.where(lane == at, one, table)
            s.table[rows, :] = table
            slots = pl.ds(group * CAP, CAP)
            given = self.i.cotangent[rows].astype(F32)
            for at, gate in enumerate(gates):
                s.thin[at * GROUP : (at + 1) * GROUP, :] = (gate * given).astype(LOW)
            for expert in range(EXPERTS):
                picks = self.picks(group, expert)
                s.dispatched[expert, slots, :] = mm(picks[0] + picks[1], s.norm[3, rows, :]).astype(LOW)
                s.slot_grad[expert, slots, :] = mm(jnp.concatenate(picks, 1), s.thin[...]).astype(LOW)

    def picks(self, group, expert):
        slot = (iota((CAP, GROUP), 0) + expert * CAP).astype(F32)
        return [
            jnp.where(slot == self.s.slots[2 * group + at : 2 * group + at + 1, :], 1.0, 0.0).astype(LOW)
            for at in range(2)
        ]

    def picks_up(self, group):
        slot = iota((GROUP, SLOTS), 1).astype(F32)
        rows = slice(group * GROUP, (group + 1) * GROUP)
        return [
            jnp.where(slot == self.s.table[rows, 4 + at : 5 + at], 1.0, 0.0).astype(LOW) for at in range(2)
        ]

    def experts_first(self):
        s = self.s
        count = 2 * CAP
        self.fetch(0, False).start()
        for expert in range(EXPERTS):
            self.fetch(expert, False).wait()

            def body(at, carry, expert=expert, half=0):
                tile = 2 * half + at
                columns = pl.ds(pl.multiple_of(tile * TILE, TILE), TILE)
                s.wide[:count] = mm(s.dispatched[expert], self.in_tile(tile))
                bias = s.vec_ff[1 + expert : 2 + expert, columns]

                def part(rows, carry):
                    s.thin[rows] = gelu_low(s.wide[rows] + bias)
                    return carry

                chunks(part, count)
                found = tn(s.thin[:count], s.slot_grad[expert])
                self.ring_c.put_at(at, found, self.made[A_OUT].at[expert, tile // 2, tile % 2])
                return carry

            for half in range(2):
                self.ring_c.settle_all()
                lax.fori_loop(0, 2, functools.partial(body, half=half), 0)
                self.ring_c.note([self.made[A_OUT].at[expert, half, at] for at in range(2)])
            if expert + 1 < EXPERTS:
                self.fetch(expert + 1, False).start()
            s.grad_out[expert : expert + 1, :] = column_sum(s.slot_grad[expert])
            self.finished(A_OUT, expert, self.ring_c.settle_all)
            self.breathe()
            self.breathe()

    def experts_then(self):
        s = self.s
        count = 2 * CAP
        self.fetch(0, False).start()
        self.fetch(0, True).start()
        for expert in range(EXPERTS):
            self.fetch(expert, False).wait()
            self.fetch(expert, True).wait()
            s.wide[:count] = jnp.zeros((count, D), F32)
            s.wide2[:count] = jnp.zeros((count, D), F32)
            for half in range(2):
                self.ring_b.settle_all()

                def body(at, carry, expert=expert, half=half):
                    tile = 2 * half + at
                    columns = pl.ds(pl.multiple_of(tile * TILE, TILE), TILE)
                    out = self.out_tile(tile)
                    s.grad[:count] = mm(s.dispatched[expert], self.in_tile(tile))
                    s.side[:count] = nt(s.slot_grad[expert], out)
                    bias = s.vec_ff[1 + expert : 2 + expert, columns]

                    def part(rows, carry):
                        active, slope = gelu_and_slope(s.grad[rows] + bias)
                        s.thin[rows] = active
                        found = (slope * s.side[rows]).astype(LOW)
                        s.thin2[rows] = found
                        return carry + column_sum(found)

                    s.grad_ff[1 + expert : 2 + expert, columns] = chunks(
                        part, count, jnp.zeros((1, TILE), F32)
                    )
                    s.wide[:count] += mm(s.thin[:count], out)
                    to_pre = s.thin2[:count]
                    found = tn(s.dispatched[expert], to_pre)
                    target = self.made[A_IN].at[expert, :, :, :, pl.ds(tile * 64, 64)]
                    self.ring_b.put_at(at, found, target)
                    s.wide2[:count] += nt(to_pre, self.in_tile(tile))
                    return carry

                lax.fori_loop(0, 2, body, 0)
                self.ring_b.note(
                    [self.made[A_IN].at[expert, :, :, :, pl.ds(tile * 64, 64)] for tile in (2 * half, 2 * half + 1)]
                )
                self.finished(A_IN, (expert, half), self.ring_b.settle_all)
                self.breathe()
            if expert + 1 < EXPERTS:
                self.fetch(expert + 1, False).start()
                self.fetch(expert + 1, True).start()
            s.dispatched[expert] = (s.wide[:count] + s.vec_out[expert : expert + 1, :]).astype(LOW)
            s.slot_grad[expert] = s.wide2[:count].astype(LOW)

    def combine(self):
        s = self.s
        lane = iota((GROUP, 128), 1)
        for group in range(ROWS // GROUP):
            rows = slice(group * GROUP, (group + 1) * GROUP)
            slots = pl.ds(group * CAP, CAP)
            picks = self.picks_up(group)
            out = s.dispatched[:, slots, :].reshape(SLOTS, D)
            picked = [mm(pick, out) for pick in picks]
            gates = [s.table[rows, 2 + at : 3 + at] for at in range(2)]
            given = self.i.cotangent[rows].astype(F32)
            found = s.stream[2, rows, :] + gates[0] * picked[0] + gates[1] * picked[1]
            self.o.activations[rows, :] = found.astype(LOW)
            probs = s.probs[rows]
            to_probs = jnp.zeros((GROUP, 128), F32)
            for at in range(2):
                to_gate = jnp.sum(given * picked[at], -1, keepdims=True)
                expert = s.table[rows, at : at + 1].astype(jnp.int32)
                to_probs = to_probs + jnp.where(lane == expert, to_gate, 0.0)
            inner = jnp.sum(to_probs * probs, -1, keepdims=True)
            to_logits = (probs * (to_probs - inner)).astype(LOW)
            s.thin2[rows, :128] = to_logits
            back = mm(picks[0] + picks[1], s.slot_grad[:, slots, :].reshape(SLOTS, D))
            s.wide[rows, :] = back + mm(to_logits, s.router[...].astype(LOW))
            s.grad[rows, :] = given
        s.grad_router[...] = tn(s.thin2[:, :128], s.norm[3])
        self.breathe()
        self.norm_back(s.stream.at[2], s.wide, NORM4_GAIN, NORM4_BIAS)
        self.breathe()

    def run(self):
        s = self.s
        greet(partners(*place()))
        self.gather.need(A_SMALL)
        self.unpack_small()
        tokens, stream = self.i.tokens, s.stream
        first = (NORM1_GAIN, NORM1_BIAS, QUERY1, VALUE1, PROJ1_BIAS)
        second = (NORM3_GAIN, NORM3_BIAS, QUERY2, VALUE2, PROJ2_BIAS)
        self.attention(0, tokens, stream.at[0], first)
        self.breathe()
        self.feed(stream.at[0], stream.at[1])
        self.attention(1, stream.at[1], stream.at[2], second)
        self.breathe()
        self.norm(stream.at[2], s.norm.at[3], NORM4_GAIN, NORM4_BIAS)
        self.breathe()
        self.route()
        self.gather.need(A_IN)
        self.experts_first()
        self.gather.need(A_OUT)
        self.experts_then()
        self.combine()
        self.attention_back(1, stream.at[1], second)
        self.feed_back(stream.at[0])
        self.attention_back(0, tokens, first)
        self.o.input_grad[...] = s.grad[...].astype(LOW)
        self.pack_small()
        while self.scatter.step():
            pass
        self.gather.finish()
        self.scatter.finish()
        for ring in (self.ring_a, self.ring_b, self.ring_c):
            ring.settle_all()


class Plan:
    def __init__(self):
        self.tiles = [BIG[name][1] // TILE for name in BIG_NAMES] + [1]
        self.rows = [BIG[name][0] // 32 for name in BIG_NAMES] + [8]
        self.height = [tiles * rows for tiles, rows in zip(self.tiles, self.rows)]
        self.gather_items = [(A_SMALL, 0, 8)]
        for which, step in (
            (A_QKV1, 16),
            (A_PROJ1, 16),
            (A_HIDDEN, 32),
            (A_OUTPUT, 32),
            (A_QKV2, 16),
            (A_PROJ2, 16),
            (A_IN, 32),
            (A_OUT, 32),
        ):
            self.gather_items += self.parts(which, step)
        self.scatter_items = []
        for which, step in (
            (A_OUT, 32),
            (A_IN, 32),
            (A_PROJ2, 16),
            (A_QKV2, 16),
            (A_OUTPUT, 32),
            (A_HIDDEN, 32),
            (A_PROJ1, 16),
            (A_QKV1, 16),
            (A_SMALL, 8),
        ):
            self.scatter_items += self.parts(which, step)

    def parts(self, which, step):
        return [(which, first, step) for first in range(0, self.height[which], step)]

    def made_of(self, which, first, rows):
        if which == A_SMALL:
            return [0]
        if which == A_OUT:
            return list(range(EXPERTS))
        if which == A_IN:
            return [(expert, first // 128) for expert in range(EXPERTS)]
        if which == A_OUTPUT:
            return list(range(4))
        return sorted({row // self.rows[which] for row in range(first, first + rows)})


def mega_kernel(plan, trees, *refs):
    parts, at = [], 0
    for tree in trees:
        parts.append(jax.tree.unflatten(tree, refs[at : at + tree.num_leaves]))
        at += tree.num_leaves
    Step(plan, *parts).run()


def mega(tokens, cotangent, info, small, shards):
    plan = Plan()
    whole = [(4, 2, 2, 2, height, TILE) for height in plan.height[:COUNT]]
    vmem = pltpu.VMEM
    inputs = Inputs(tokens, cotangent, info, small, shards)
    outputs = Outputs(
        activations=jax.ShapeDtypeStruct((ROWS, D), LOW),
        input_grad=jax.ShapeDtypeStruct((ROWS, D), LOW),
        small=jax.ShapeDtypeStruct((8, 128), F32),
        grads=[jax.ShapeDtypeStruct(one.shape, F32) for one in shards],
        wholes=[jax.ShapeDtypeStruct(whole[which], LOW) for which in (A_IN, A_OUT)],
        made=[jax.ShapeDtypeStruct(shape, LOW) for shape in whole],
        landing=[jax.ShapeDtypeStruct((4, 2, 2, height, TILE), LOW) for height in plan.height[:COUNT]],
    )
    here = pl.BlockSpec(memory_space=pltpu.VMEM)
    anywhere = pl.BlockSpec(memory_space=pl.ANY)
    in_specs = jax.tree.map(lambda one: here, inputs)
    out_specs = Outputs(here, here, here, [here] * COUNT, [anywhere] * 2, [anywhere] * COUNT, [anywhere] * COUNT)

    def room(*lead):
        return [vmem(lead + (height, TILE), LOW) for height in plan.height[:COUNT]] + [
            vmem(lead + (8, 128), F32)
        ]

    def semaphores(items, messages):
        return pltpu.SemaphoreType.DMA((len(items), messages))

    dma = pltpu.SemaphoreType.DMA
    scratch = Scratch(
        low=room()[:COUNT],
        resident=[vmem(whole[which], LOW) for which in range(6)],
        small_whole=vmem((4, 2, 2, 2, 8, 128), F32),
        small_grad=vmem((4, 2, 2, 2, 8, 128), F32),
        flat=vmem((256, 128), F32),
        vec=vmem((16, D), F32),
        vec_ff=vmem((8, FF), F32),
        vec_out=vmem((8, D), F32),
        router=vmem((128, D), F32),
        grad_vec=vmem((16, D), F32),
        grad_ff=vmem((8, FF), F32),
        grad_out=vmem((8, D), F32),
        grad_router=vmem((128, D), F32),
        stream=vmem((3, ROWS, D), F32),
        norm=vmem((4, ROWS, D), LOW),
        packed=vmem((2, ROWS, 3 * D), LOW),
        heads=vmem((2, ROWS, D), LOW),
        probs=vmem((ROWS, 128), F32),
        side=vmem((ROWS, D), F32),
        slots=vmem((8, GROUP), F32),
        dispatched=vmem((EXPERTS, 2 * CAP, D), LOW),
        slot_grad=vmem((EXPERTS, 2 * CAP, D), LOW),
        weight_in=vmem((2, 2, 2, 256, TILE), LOW),
        weight_out=vmem((2, 2, 2, 256, TILE), LOW),
        grad=vmem((ROWS, D), F32),
        table=vmem((ROWS, 128), F32),
        wide=vmem((ROWS, D), F32),
        wide2=vmem((ROWS, D), F32),
        thin=vmem((ROWS, D), LOW),
        thin2=vmem((ROWS, D), LOW),
        grad_packed=vmem((ROWS, 3 * D), LOW),
        ring_a=vmem((2, 4, 2, 2, 2, 16, TILE), LOW),
        ring_b=vmem((2, 2, 2, 2, 64, TILE), LOW),
        ring_c=vmem((2, 2, 256, TILE), LOW),
        own=vmem((2, 4, 2, 2, 32, TILE), LOW),
        landed=vmem((1, 4, 2, 2, 32, TILE), LOW),
        pool=vmem((Scatter.slots, 4, 2, 2, 32, TILE), LOW),
        own_small=vmem((4, 2, 2, 8, 128), F32),
        landed_small=vmem((4, 2, 2, 8, 128), F32),
        pool_small=vmem((4, 2, 2, 8, 128), F32),
        landing_small=vmem((4, 2, 2, 8, 128), F32),
        halves=room(4),
        sides=room(2, 4),
        ends=room(3),
        gather_send=semaphores(plan.gather_items, Gather.messages),
        gather_recv=semaphores(plan.gather_items, Gather.messages),
        gather_local=dma((len(plan.gather_items),)),
        scatter_send=semaphores(plan.scatter_items, Scatter.messages),
        scatter_recv=semaphores(plan.scatter_items, Scatter.messages),
        scatter_local=dma((3,)),
        ring_a_sem=dma((2,)),
        ring_b_sem=dma((2,)),
        ring_c_sem=dma((2,)),
        fetch=dma((2,)),
    )
    operands, in_tree = jax.tree.flatten(inputs)
    out_shapes, out_tree = jax.tree.flatten(outputs)
    scratch_shapes, scratch_tree = jax.tree.flatten(scratch)
    found = pl.pallas_call(
        functools.partial(mega_kernel, plan, (in_tree, out_tree, scratch_tree)),
        out_shape=out_shapes,
        in_specs=jax.tree.leaves(in_specs),
        out_specs=jax.tree.leaves(out_specs),
        scratch_shapes=scratch_shapes,
        compiler_params=pltpu.CompilerParams(
            collective_id=0, has_side_effects=True, vmem_limit_bytes=64 * 1024 * 1024
        ),
    )(*operands)
    return jax.tree.unflatten(out_tree, found)


def join_small(shards):
    def zeros(count):
        return jnp.zeros((count,), F32)

    parts = [shards[name] for name in VECTORS] + [zeros(16), shards[HIDDEN_BIAS], shards[ROUTER]]
    parts += [shards[EXPERT_IN_BIAS], shards[EXPERT_OUT_BIAS], zeros(320)]
    return jnp.concatenate(parts).astype(LOW).astype(F32).reshape(8, 128)


def split_small(values):
    values = values.reshape(-1)
    found = {name: values[16 * at : 16 * at + 16] for at, name in enumerate(VECTORS)}
    for name, first, count in (
        (HIDDEN_BIAS, 256, 64),
        (ROUTER, 320, 64),
        (EXPERT_IN_BIAS, 384, 256),
        (EXPERT_OUT_BIAS, 640, 64),
    ):
        found[name] = values[first : first + count]
    return found


def on_slice(tokens, *rest):
    shards = dict(zip(NAMES, rest[: len(NAMES)]))
    routes, priority, cotangent = rest[len(NAMES) :]
    info = jnp.concatenate(
        [
            routes.reshape(-1, GROUP, 2).transpose(0, 2, 1),
            priority[:, None, :],
            jnp.zeros((priority.shape[0], 5, GROUP), jnp.int32),
        ],
        1,
    )
    found = mega(
        tokens.reshape(ROWS, D),
        cotangent.reshape(ROWS, D),
        info.astype(F32).reshape(-1, GROUP),
        join_small(shards),
        [shards[name].reshape(-1, 128) for name in BIG_NAMES],
    )
    mine = split_small(found.small)
    mine.update((name, one.reshape(-1)) for name, one in zip(BIG_NAMES, found.grads))
    outs = (found.activations.reshape(tokens.shape), found.input_grad.reshape(tokens.shape))
    return outs + tuple(mine[name] for name in NAMES)


def routed_forward(normed, weights, routes, priority):
    groups = priority.shape[0]
    normed_low = normed.astype(jnp.bfloat16)
    logits = jnp.dot(normed_low, weights[ROUTER], preferred_element_type=jnp.float32)
    row_max = jnp.max(logits, -1, keepdims=True)
    exponent = jnp.exp(logits - row_max)
    probs_all = exponent / jnp.sum(exponent, -1, keepdims=True)
    expert_ids = jnp.arange(EXPERTS, dtype=jnp.int32)
    flat_routes = routes.reshape(-1, 2)
    hots = [(flat_routes[:, k : k + 1] == expert_ids).astype(jnp.float32) for k in range(2)]
    gates = [jnp.sum(probs_all * hot, -1, keepdims=True) for hot in hots]
    first, second = routes[:, :, 0], routes[:, :, 1]
    before = priority[:, None, :] < priority[:, :, None]
    place_first = jnp.sum(before & (first[:, None, :] == first[:, :, None]), -1)
    place_second = jnp.sum(before & (second[:, None, :] == second[:, :, None]), -1)
    place_second = place_second + jnp.sum(first[:, None, :] == second[:, :, None], -1)
    slot_ids = jnp.arange(SLOTS, dtype=jnp.int32)
    picks = [
        ((which * CAP + at)[:, None, :] == slot_ids[None, :, None]) & (at < CAP)[:, None, :]
        for which, at in ((first, place_first), (second, place_second))
    ]
    picks = [pick.astype(jnp.bfloat16) for pick in picks]
    grouped = normed_low.reshape(groups, GROUP, D)
    dispatched = jnp.einsum(
        "gst,gtd->gsd", picks[0] + picks[1], grouped, preferred_element_type=jnp.float32
    ).astype(jnp.bfloat16)
    dispatched = by_expert(dispatched)
    pre_act = jnp.einsum(
        "ecd,edf->ecf", dispatched, weights[EXPERT_IN], preferred_element_type=jnp.float32
    )
    pre_act = pre_act + weights[EXPERT_IN_BIAS].astype(jnp.float32)[:, None, :]
    hidden = jax.nn.gelu(pre_act).astype(jnp.bfloat16)
    expert_out = jnp.einsum(
        "ecf,efd->ecd", hidden, weights[EXPERT_OUT], preferred_element_type=jnp.float32
    )
    expert_out = expert_out + weights[EXPERT_OUT_BIAS].astype(jnp.float32)[:, None, :]
    expert_low = by_group(expert_out.astype(jnp.bfloat16), groups)
    picked = [
        jnp.einsum("gst,gsd->gtd", pick, expert_low, preferred_element_type=jnp.float32).reshape(-1, D)
        for pick in picks
    ]
    output = gates[0] * picked[0] + gates[1] * picked[1]
    return output, (normed_low, probs_all, hots, gates, picks, dispatched, pre_act, hidden, picked)


def by_expert(slots):
    groups, width = slots.shape[0], slots.shape[2]
    slots = slots.reshape(groups, EXPERTS, CAP, width).transpose(1, 0, 2, 3)
    return slots.reshape(EXPERTS, groups * CAP, width)


def by_group(slots, groups):
    width = slots.shape[2]
    slots = slots.reshape(EXPERTS, groups, CAP, width).transpose(1, 0, 2, 3)
    return slots.reshape(groups, SLOTS, width)


def routed_backward(grad_output, saved_state, weights):
    normed_low, probs_all, hots, gates, picks, dispatched, pre_act, hidden, picked = saved_state
    groups = picks[0].shape[0]
    grad_gates = [jnp.sum(grad_output * one, -1, keepdims=True) for one in picked]
    grad_expert = sum(
        jnp.einsum(
            "gst,gtd->gsd",
            pick,
            (gate * grad_output).astype(jnp.bfloat16).reshape(groups, GROUP, D),
            preferred_element_type=jnp.float32,
        )
        for pick, gate in zip(picks, gates)
    )
    grad_expert = by_expert(grad_expert.astype(jnp.bfloat16))
    grad_out_weight = jnp.einsum(
        "ecf,ecd->efd", hidden, grad_expert, preferred_element_type=jnp.float32
    )
    grad_out_bias = jnp.sum(grad_expert.astype(jnp.float32), 1)
    grad_hidden = jnp.einsum(
        "ecd,efd->ecf", grad_expert, weights[EXPERT_OUT], preferred_element_type=jnp.float32
    )
    grad_pre = gelu_backward(pre_act, grad_hidden).astype(jnp.bfloat16)
    grad_in_weight = jnp.einsum(
        "ecd,ecf->edf", dispatched, grad_pre, preferred_element_type=jnp.float32
    )
    grad_in_bias = jnp.sum(grad_pre.astype(jnp.float32), 1)
    grad_dispatched = jnp.einsum(
        "ecf,edf->ecd", grad_pre, weights[EXPERT_IN], preferred_element_type=jnp.float32
    )
    grad_slots = by_group(grad_dispatched.astype(jnp.bfloat16), groups)
    grad_normed = jnp.einsum(
        "gst,gsd->gtd", picks[0] + picks[1], grad_slots, preferred_element_type=jnp.float32
    ).reshape(-1, D)
    grad_probs = hots[0] * grad_gates[0] + hots[1] * grad_gates[1]
    inner_sum = jnp.sum(grad_probs * probs_all, -1, keepdims=True)
    grad_logits = (probs_all * (grad_probs - inner_sum)).astype(jnp.bfloat16)
    grad_router = jnp.einsum(
        "rd,re->de", normed_low, grad_logits, preferred_element_type=jnp.float32
    )
    grad_normed = grad_normed + jnp.einsum(
        "re,de->rd", grad_logits, weights[ROUTER], preferred_element_type=jnp.float32
    )
    return grad_normed, (grad_router, grad_in_weight, grad_in_bias, grad_out_weight, grad_out_bias)


def gather_small(shards):
    lengths = [shards[name].shape[0] for name in SMALL]
    joined = jnp.concatenate([shards[name].astype(jnp.bfloat16) for name in SMALL])
    whole = lax.all_gather(joined, "fsdp", axis=0)
    found, at = {}, 0
    for name, length in zip(SMALL, lengths):
        found[name] = whole[:, at : at + length].reshape(-1)
        at += length
    found[ROUTER] = found[ROUTER].reshape(D, EXPERTS)
    found[EXPERT_IN_BIAS] = found[EXPERT_IN_BIAS].reshape(EXPERTS, EXP_FF)
    found[EXPERT_OUT_BIAS] = found[EXPERT_OUT_BIAS].reshape(EXPERTS, D)
    return found


def scatter_small(grads, devices):
    joined = jnp.concatenate([grads[name].reshape(devices, -1) for name in SMALL], 1)
    width = joined.shape[1]
    mine = lax.psum_scatter(joined.reshape(-1), "fsdp", scatter_dimension=0, tiled=True)
    found, at = {}, 0
    for name in SMALL:
        length = grads[name].size // devices
        found[name] = mine[at : at + length]
        at += length
    return found


def on_device(devices, tokens, *rest):
    shards = dict(zip(NAMES, rest[: len(NAMES)]))
    routes, priority, cotangent = rest[len(NAMES) :]
    images = tokens.shape[0]
    groups = priority.shape[0]
    weights = gather_small(shards)
    for name in BIG_NAMES:
        whole = lax.all_gather(shards[name].astype(jnp.bfloat16), "fsdp", axis=0, tiled=True)
        weights[name] = whole.reshape(BIG[name])
    weights[EXPERT_IN] = weights[EXPERT_IN].reshape(EXPERTS, D, EXP_FF)
    weights[EXPERT_OUT] = weights[EXPERT_OUT].reshape(EXPERTS, EXP_FF, D)
    wide = {name: weights[name].astype(jnp.float32) for name in GAINS}
    stream0 = tokens.reshape(images * PATCH, D).astype(jnp.float32)
    grad4 = cotangent.reshape(images * PATCH, D).astype(jnp.float32)
    normed1 = norm_forward(stream0, wide[NORM1_GAIN], wide[NORM1_BIAS])
    out, attention1 = attention_forward(
        normed1, *(weights[name] for name in (QKV1, QUERY1, VALUE1, PROJ1, PROJ1_BIAS))
    )
    stream1 = stream0 + out
    normed2 = norm_forward(stream1, wide[NORM2_GAIN], wide[NORM2_BIAS])
    out, feed = feed_forward(
        normed2, *(weights[name] for name in (HIDDEN, HIDDEN_BIAS, OUTPUT, OUTPUT_BIAS))
    )
    stream2 = stream1 + out
    normed3 = norm_forward(stream2, wide[NORM3_GAIN], wide[NORM3_BIAS])
    out, attention2 = attention_forward(
        normed3, *(weights[name] for name in (QKV2, QUERY2, VALUE2, PROJ2, PROJ2_BIAS))
    )
    stream3 = stream2 + out
    normed4 = norm_forward(stream3, wide[NORM4_GAIN], wide[NORM4_BIAS])
    out, routed = routed_forward(normed4, weights, routes.reshape(groups, GROUP, 2), priority)
    activations = (stream3 + out).astype(jnp.bfloat16).reshape(tokens.shape)

    grads = {}

    def keep(names, values):
        grads.update(zip(names, values))

    grad, found = routed_backward(grad4, routed, weights)
    keep((ROUTER, EXPERT_IN, EXPERT_IN_BIAS, EXPERT_OUT, EXPERT_OUT_BIAS), found)
    back, *found = norm_backward(stream3, wide[NORM4_GAIN], wide[NORM4_BIAS], grad)
    keep((NORM4_GAIN, NORM4_BIAS), found)
    grad3 = grad4 + back
    grad, found = attention_backward(grad3, attention2, weights[QKV2], weights[PROJ2])
    keep((QKV2, QUERY2, VALUE2, PROJ2, PROJ2_BIAS), found)
    back, *found = norm_backward(stream2, wide[NORM3_GAIN], wide[NORM3_BIAS], grad)
    keep((NORM3_GAIN, NORM3_BIAS), found)
    grad2 = grad3 + back
    grad, found = feed_backward(grad2, feed, weights[HIDDEN], weights[OUTPUT])
    keep((HIDDEN, HIDDEN_BIAS, OUTPUT, OUTPUT_BIAS), found)
    back, *found = norm_backward(stream1, wide[NORM2_GAIN], wide[NORM2_BIAS], grad)
    keep((NORM2_GAIN, NORM2_BIAS), found)
    grad1 = grad2 + back
    grad, found = attention_backward(grad1, attention1, weights[QKV1], weights[PROJ1])
    keep((QKV1, QUERY1, VALUE1, PROJ1, PROJ1_BIAS), found)
    back, *found = norm_backward(stream0, wide[NORM1_GAIN], wide[NORM1_BIAS], grad)
    keep((NORM1_GAIN, NORM1_BIAS), found)
    input_grad = (grad1 + back).astype(jnp.bfloat16).reshape(tokens.shape)

    mine = scatter_small(grads, devices)
    for name in BIG_NAMES:
        flat = grads[name].reshape(-1)
        mine[name] = lax.psum_scatter(flat, "fsdp", scatter_dimension=0, tiled=True)
    return (activations, input_grad) + tuple(mine[name] for name in NAMES)


def solution(mesh):
    rows = P("fsdp", None, None)
    flat = tuple(P("fsdp") for _ in NAMES)
    devices = mesh.shape["fsdp"]
    return jax.shard_map(
        on_slice if devices == 32 else functools.partial(on_device, devices),
        mesh=mesh,
        in_specs=(rows,) + flat + (rows, P("fsdp", None), rows),
        out_specs=(rows, rows) + flat,
        check_vma=False,
    )
```

```python
import functools
import math
from typing import Any, NamedTuple

import jax
import jax.numpy as jnp
from jax import lax
from jax.experimental import pallas as pl
from jax.experimental.pallas import tpu as pltpu
from jax.sharding import PartitionSpec as P

D = 512
HEADS = 8
HEAD_DIM = 64
FF = 2048
EXP_FF = 2048
EXPERTS = 4
PATCH = 128
GROUP = 256
CAP = 160
SLOTS = EXPERTS * CAP
MESH = pl.DeviceIdType.MESH

(
    NORM1_GAIN,
    NORM1_BIAS,
    QKV1,
    QUERY1,
    VALUE1,
    PROJ1,
    PROJ1_BIAS,
    NORM2_GAIN,
    NORM2_BIAS,
    HIDDEN,
    HIDDEN_BIAS,
    OUTPUT,
    OUTPUT_BIAS,
    NORM3_GAIN,
    NORM3_BIAS,
    QKV2,
    QUERY2,
    VALUE2,
    PROJ2,
    PROJ2_BIAS,
    NORM4_GAIN,
    NORM4_BIAS,
    ROUTER,
    EXPERT_IN,
    EXPERT_IN_BIAS,
    EXPERT_OUT,
    EXPERT_OUT_BIAS,
) = NAMES = tuple(range(27))
BIG = {
    QKV1: (D, 3 * D),
    PROJ1: (D, D),
    HIDDEN: (D, FF),
    OUTPUT: (FF, D),
    QKV2: (D, 3 * D),
    PROJ2: (D, D),
    EXPERT_IN: (EXPERTS * D, EXP_FF),
    EXPERT_OUT: (EXPERTS * EXP_FF, D),
}
SMALL = tuple(name for name in NAMES if name not in BIG)
BIG_NAMES = tuple(BIG)
GAINS = (NORM1_GAIN, NORM1_BIAS, NORM2_GAIN, NORM2_BIAS, NORM3_GAIN, NORM3_BIAS, NORM4_GAIN, NORM4_BIAS)


def norm_forward(values, norm_gain, norm_shift):
    centred = values - jnp.mean(values, -1, keepdims=True)
    variance = jnp.mean(centred * centred, -1, keepdims=True)
    return centred * lax.rsqrt(variance + 1e-06) * norm_gain + norm_shift


def norm_backward(values, norm_gain, norm_shift, grad_normed):
    unused, pullback = jax.vjp(norm_forward, values, norm_gain, norm_shift)
    return pullback(grad_normed)


def gelu_backward(pre_act, grad_act):
    unused, pullback = jax.vjp(jax.nn.gelu, pre_act)
    return pullback(grad_act)[0]


def column_sums(matrix):
    return jnp.sum(matrix.astype(jnp.float32), 0)


def attention_forward(normed, qkv_weight, query_bias, value_bias, proj_weight, proj_bias):
    row_count = normed.shape[0]
    normed_low = normed.astype(jnp.bfloat16)
    packed_bias = jnp.concatenate([query_bias, jnp.zeros_like(query_bias), value_bias]).astype(
        jnp.float32
    )
    packed = jnp.dot(normed_low, qkv_weight, preferred_element_type=jnp.float32) + packed_bias
    packed = packed.astype(jnp.bfloat16).reshape(row_count // PATCH, PATCH, 3, HEADS, HEAD_DIM)
    queries = packed[:, :, 0]
    key_block = packed[:, :, 1]
    values = packed[:, :, 2]
    score_scale = 1.0 / math.sqrt(HEAD_DIM)
    scores = (
        jnp.einsum("iqhd,ikhd->ihqk", queries, key_block, preferred_element_type=jnp.float32)
        * score_scale
    )
    row_max = jnp.max(scores, -1, keepdims=True)
    exponent = jnp.exp(scores - row_max)
    row_total = jnp.sum(exponent, -1, keepdims=True)
    weights_low = (exponent / row_total).astype(jnp.bfloat16)
    logsum = row_max + jnp.log(row_total)
    mixed_heads = jnp.einsum(
        "ihqk,ikhd->iqhd", weights_low, values, preferred_element_type=jnp.float32
    )
    mixed_heads = mixed_heads.reshape(row_count, D).astype(jnp.bfloat16)
    output = jnp.dot(
        mixed_heads, proj_weight, preferred_element_type=jnp.float32
    ) + proj_bias.astype(jnp.float32)
    return (output, (normed_low, queries, key_block, values, logsum, mixed_heads))


def attention_backward(grad_output, saved_state, qkv_weight, proj_weight):
    normed_low, queries, key_block, values, logsum, mixed_heads = saved_state
    row_count = normed_low.shape[0]
    grad_low = grad_output.astype(jnp.bfloat16)
    grad_proj_weight = jnp.einsum(
        "rd,re->de", mixed_heads, grad_low, preferred_element_type=jnp.float32
    )
    grad_proj_bias = column_sums(grad_low)
    grad_mixed = jnp.einsum("re,de->rd", grad_low, proj_weight, preferred_element_type=jnp.float32)
    grad_mixed = grad_mixed.astype(jnp.bfloat16).reshape(row_count // PATCH, PATCH, HEADS, HEAD_DIM)
    score_scale = 1.0 / math.sqrt(HEAD_DIM)
    scores = (
        jnp.einsum("iqhd,ikhd->ihqk", queries, key_block, preferred_element_type=jnp.float32)
        * score_scale
    )
    weights_full = jnp.exp(scores - logsum)
    weights_low = weights_full.astype(jnp.bfloat16)
    grad_weights = jnp.einsum(
        "iqhd,ikhd->ihqk", grad_mixed, values, preferred_element_type=jnp.float32
    )
    grad_values = jnp.einsum(
        "ihqk,iqhd->ikhd", weights_low, grad_mixed, preferred_element_type=jnp.float32
    )
    inner_sum = jnp.sum(grad_weights * weights_full, -1, keepdims=True)
    grad_scores = (weights_full * (grad_weights - inner_sum)).astype(jnp.bfloat16)
    grad_queries = (
        jnp.einsum("ihqk,ikhd->iqhd", grad_scores, key_block, preferred_element_type=jnp.float32)
        * score_scale
    )
    grad_keys = (
        jnp.einsum("ihqk,iqhd->ikhd", grad_scores, queries, preferred_element_type=jnp.float32)
        * score_scale
    )
    grad_packed = (
        jnp.stack([grad_queries, grad_keys, grad_values], 2)
        .reshape(row_count, 3 * D)
        .astype(jnp.bfloat16)
    )
    grad_qkv_weight = jnp.einsum(
        "rd,re->de", normed_low, grad_packed, preferred_element_type=jnp.float32
    )
    grad_query_bias = column_sums(grad_packed[:, :D])
    grad_value_bias = column_sums(grad_packed[:, 2 * D :])
    grad_normed = jnp.einsum(
        "re,de->rd", grad_packed, qkv_weight, preferred_element_type=jnp.float32
    )
    return (
        grad_normed,
        (grad_qkv_weight, grad_query_bias, grad_value_bias, grad_proj_weight, grad_proj_bias),
    )


def feed_forward(normed, in_weight, in_bias, out_weight, out_bias):
    normed_low = normed.astype(jnp.bfloat16)
    pre_act = jnp.dot(normed_low, in_weight, preferred_element_type=jnp.float32) + in_bias.astype(
        jnp.float32
    )
    activation = jax.nn.gelu(pre_act).astype(jnp.bfloat16)
    output = jnp.dot(activation, out_weight, preferred_element_type=jnp.float32) + out_bias.astype(
        jnp.float32
    )
    return (output, (normed_low, pre_act, activation))


def feed_backward(grad_output, saved_state, in_weight, out_weight):
    normed_low, pre_act, activation = saved_state
    grad_low = grad_output.astype(jnp.bfloat16)
    grad_out_weight = jnp.einsum(
        "rf,rd->fd", activation, grad_low, preferred_element_type=jnp.float32
    )
    grad_out_bias = column_sums(grad_low)
    grad_activation = jnp.einsum(
        "rd,fd->rf", grad_low, out_weight, preferred_element_type=jnp.float32
    )
    grad_pre = gelu_backward(pre_act, grad_activation).astype(jnp.bfloat16)
    grad_in_weight = jnp.einsum(
        "rd,rf->df", normed_low, grad_pre, preferred_element_type=jnp.float32
    )
    grad_in_bias = column_sums(grad_pre)
    grad_normed = jnp.einsum("rf,df->rd", grad_pre, in_weight, preferred_element_type=jnp.float32)
    return (grad_normed, (grad_in_weight, grad_in_bias, grad_out_weight, grad_out_bias))


TILE = 512
F32 = jnp.float32
LOW = jnp.bfloat16
ROWS = 512
CHUNK = 256
COUNT = len(BIG_NAMES)
A_QKV1, A_PROJ1, A_HIDDEN, A_OUTPUT, A_QKV2, A_PROJ2, A_IN, A_OUT, A_SMALL = range(COUNT + 1)
VECTORS = (
    NORM1_GAIN,
    NORM1_BIAS,
    QUERY1,
    VALUE1,
    PROJ1_BIAS,
    NORM2_GAIN,
    NORM2_BIAS,
    OUTPUT_BIAS,
    NORM3_GAIN,
    NORM3_BIAS,
    QUERY2,
    VALUE2,
    PROJ2_BIAS,
    NORM4_GAIN,
    NORM4_BIAS,
)
ROW_OF = {name: at for at, name in enumerate(VECTORS)}


def mm(left, right):
    return jnp.dot(left, right, preferred_element_type=F32)


def nt(left, right):
    return lax.dot_general(left, right, (((1,), (1,)), ((), ())), preferred_element_type=F32)


def tn(left, right):
    return lax.dot_general(left, right, (((0,), (0,)), ((), ())), preferred_element_type=F32)


def iota(shape, dimension):
    return lax.broadcasted_iota(jnp.int32, shape, dimension)


def chunks(body, rows=ROWS, init=0, size=CHUNK):
    def step(at, carry):
        return body(pl.ds(pl.multiple_of(at * size, size), size), carry)

    return lax.fori_loop(0, rows // size, step, init)


def normed(values):
    centred = values - jnp.mean(values, -1, keepdims=True)
    scale = lax.rsqrt(jnp.mean(centred * centred, -1, keepdims=True) + 1e-06)
    return centred * scale, scale


SQRT_2_PI = math.sqrt(2.0 / math.pi)


def gelu_parts(pre):
    squared = pre * pre
    bent = jnp.tanh(pre * (SQRT_2_PI + (SQRT_2_PI * 0.044715) * squared))
    return squared, bent, 0.5 + 0.5 * bent


def gelu_low(pre):
    return (pre * gelu_parts(pre)[2]).astype(LOW)


def gelu_and_slope(pre):
    squared, bent, half = gelu_parts(pre)
    active = pre * half
    slope = half + active * (1.0 - half) * (
        2.0 * SQRT_2_PI + (6.0 * SQRT_2_PI * 0.044715) * squared
    )
    return active.astype(LOW), slope


def column_sum(values):
    return jnp.sum(values.astype(F32), 0, keepdims=True)


def place():
    me = lax.axis_index("fsdp")
    return me // 8, (me // 4) % 2, (me // 2) % 2, me % 2


def device(z, y, x, core):
    return (((z * 2 + y) * 2 + x) * 2 + core,)


def partners(z, y, x, core):
    found = [device((z + step) % 4, y, x, core) for step in (1, 2, 3)]
    return found + [device(z, y, 1 - x, core), device(z, 1 - y, x, core), device(z, y, x, 1 - core)]


def greet(devices):
    barrier = pltpu.get_barrier_semaphore()
    for one in devices:
        pl.semaphore_signal(barrier, inc=1, device_id=one, device_id_type=MESH)
    pl.semaphore_wait(barrier, len(devices))


class Link:
    def __init__(self, items, send, recv):
        self.items, self.send, self.recv = items, send, recv
        self.z, self.y, self.x, self.core = place()

    def copy(self, item, message, source, target, to):
        return pltpu.make_async_remote_copy(
            src_ref=source,
            dst_ref=target,
            send_sem=self.send.at[item % self.turns, message],
            recv_sem=self.recv.at[item % self.turns, message],
            device_id=to,
            device_id_type=MESH,
        )

    def rows(self, item):
        which, first, rows = self.items[item]
        return which, pl.ds(first, rows)


class Gather(Link):
    messages = 12
    leads = (0, 2, 4, 6, 8, 10)
    turns = 10

    def __init__(self, items, shards, wholes, prepare, send, recv, local):
        super().__init__(items, send, recv)
        self.shards, self.wholes, self.prepare, self.local = shards, wholes, prepare, local
        self.ready, self.tick = set(), 0

    def block(self, item, zs, y, x, core):
        which, rows = self.rows(item)
        return self.wholes[which].at[zs, y, x, core, rows]

    def source(self, item):
        which, rows = self.rows(item)
        return self.shards[which].at[rows]

    def own(self, item):
        target = self.block(item, self.z, self.y, self.x, self.core)
        return pltpu.make_async_copy(self.source(item), target, self.local.at[item % self.turns])

    def along_z(self, item):
        z, y, x, core = self.z, self.y, self.x, self.core
        source = self.source(item)
        target = self.block(item, z, y, x, core)
        return [
            self.copy(item, step - 1, source, target, device((z + step) % 4, y, x, core))
            for step in (1, 2, 3)
        ]

    def same(self, item, message, zs, y, x, core, to):
        part = self.block(item, zs, y, x, core)
        return self.copy(item, message, part, part, to)

    def across(self, item):
        z, y, x, core = self.z, self.y, self.x, self.core
        return [
            self.same(item, 3, slice(None), y, x, core, device(z, y, 1 - x, core)),
            self.same(item, 4, slice(None), y, x, core, device(z, 1 - y, x, core)),
        ]

    def onward(self, item):
        z, y, x, core = self.z, self.y, self.x, self.core
        first = 2 * (z % 2)
        return [
            self.same(item, 5, first, y, 1 - x, core, device(z, 1 - y, x, core)),
            self.same(item, 6, first + 1, 1 - y, x, core, device(z, y, 1 - x, core)),
        ]

    def exchange(self, item):
        z, y, x, core = self.z, self.y, self.x, self.core
        mine, other = pl.ds(2 * (z % 2), 2), z + 1 - 2 * (z % 2)
        return self.same(item, 11, mine, 1 - y, 1 - x, core, device(other, y, x, core))

    def pair(self, item, which):
        z, y, x, core = self.z, self.y, self.x, self.core
        ys, xs = ((y, x), (y, 1 - x), (1 - y, x), (1 - y, 1 - x))[which]
        return self.same(item, 7 + which, slice(None), ys, xs, core, device(z, y, x, 1 - core))

    def stage(self, number, item):
        if number == 0:
            self.prepare(item)
            if item >= self.turns:
                self.sent(item - self.turns)
            self.own(item).start()
            for one in self.along_z(item):
                one.start()
        elif number == 1:
            self.own(item).wait()
            for one in self.along_z(item):
                one.wait_recv()
            for one in self.across(item):
                one.start()
            self.pair(item, 0).start()
        elif number == 2:
            for one in self.across(item):
                one.wait_recv()
            for one in self.onward(item):
                one.start()
            self.pair(item, 1).start()
            self.pair(item, 2).start()
        elif number == 3:
            for one in self.onward(item):
                one.wait_recv()
            self.exchange(item).start()
        elif number == 4:
            self.exchange(item).wait_recv()
            self.pair(item, 3).start()
        else:
            for which in range(4):
                self.pair(item, which).wait_recv()
            self.ready.add(item)

    def step(self):
        if len(self.ready) == len(self.items):
            return False
        for number in reversed(range(6)):
            item = self.tick - self.leads[number]
            if 0 <= item < len(self.items):
                self.stage(number, item)
        self.tick += 1
        return True

    def need(self, which):
        wanted = {at for at, item in enumerate(self.items) if item[0] == which}
        while not wanted <= self.ready:
            self.step()

    def sent(self, item):
        copies = self.along_z(item) + self.across(item) + self.onward(item) + [self.exchange(item)]
        for one in copies + [self.pair(item, which) for which in range(4)]:
            one.wait_send()

    def finish(self):
        for item in range(max(0, len(self.items) - self.turns), len(self.items)):
            self.sent(item)


class Scatter(Link):
    messages = 9
    leads = (0, 1, 2, 4, 6, 8, 10)
    turns = 9

    def __init__(self, items, grads, landing, own, landed, pool, cross, halves, sides, ends, give, send, recv, local):
        super().__init__(items, send, recv)
        self.grads, self.landing = grads, landing
        self.own, self.landed, self.pool = own, landed, pool
        self.cross, self.halves, self.sides, self.ends = cross, halves, sides, ends
        self.give, self.local = give, local
        self.tick, self.made = 0, {}

    def slot(self, kind, item):
        which, first, rows = self.items[item]
        if which == A_SMALL:
            return kind[1]
        return kind[0].at[item % kind[0].shape[0], :, :, :, pl.ds(0, rows)]

    def load_own(self, item):
        which, rows = self.rows(item)
        source = self.grads[which].at[:, :, :, self.core, rows]
        return pltpu.make_async_copy(source, self.slot(self.own, item), self.local.at[item % 2])

    def load_landed(self, item):
        which, rows = self.rows(item)
        source = self.landing[which].at[:, :, :, rows]
        return pltpu.make_async_copy(source, self.slot(self.landed, item), self.local.at[2])

    def pair(self, item):
        which, rows = self.rows(item)
        return self.copy(
            item,
            0,
            self.grads[which].at[:, :, :, 1 - self.core, rows],
            self.landing[which].at[:, :, :, rows],
            device(self.z, self.y, self.x, 1 - self.core),
        )

    def exchange(self, item):
        which, rows = self.rows(item)
        z, y, x, core = self.z, self.y, self.x, self.core
        other = z + 1 - 2 * (z % 2)
        source = self.slot(self.pool, item).at[pl.ds(2 * (other % 2), 2), 1 - y, 1 - x]
        return self.copy(item, 1, source, self.cross[which].at[:, rows], device(other, y, x, core))

    def half(self, item):
        which, rows = self.rows(item)
        z, y, x, core = self.z, self.y, self.x, self.core
        found = []
        for at, to in ((0, device(z, y, 1 - x, core)), (1, device(z, 1 - y, x, core))):
            source = self.slot(self.pool, item).at[2 * (z % 2) + at, 1 - y, 1 - x]
            found.append(self.copy(item, 2 + at, source, self.halves[which].at[at, rows], to))
        return found

    def side(self, item):
        which, rows = self.rows(item)
        z, y, x, core = self.z, self.y, self.x, self.core
        found = []
        for at, (ys, xs) in enumerate(((y, 1 - x), (1 - y, x))):
            source = self.slot(self.pool, item).at[:, ys, xs]
            target = self.sides[which].at[at, :, rows]
            found.append(self.copy(item, 4 + at, source, target, device(z, ys, xs, core)))
        return found

    def along_z(self, item):
        which, rows = self.rows(item)
        z, y, x, core = self.z, self.y, self.x, self.core
        found = []
        for step in (1, 2, 3):
            to = (z + step) % 4
            source = self.slot(self.pool, item).at[to, y, x]
            target = self.ends[which].at[step - 1, rows]
            found.append(self.copy(item, 5 + step, source, target, device(to, y, x, core)))
        return found

    def sent(self, item):
        for one in [self.exchange(item)] + self.half(item) + self.side(item) + self.along_z(item):
            one.wait_send()

    def stage(self, number, item):
        which, rows = self.rows(item)
        z, y, x = self.z, self.y, self.x
        pool = self.slot(self.pool, item)
        if number == 0:
            for one in self.made[item]:
                one()
            if item >= self.turns:
                self.pair(item - self.turns).wait_send()
            self.load_own(item).start()
            self.pair(item).start()
        elif number == 1:
            self.pair(item).wait_recv()
            self.load_landed(item).start()
        elif number == 2:
            self.load_own(item).wait()
            self.load_landed(item).wait()
            if item >= self.turns:
                self.sent(item - self.turns)
            own, landed = self.slot(self.own, item), self.slot(self.landed, item)

            def add(at, carry):
                spot = (at // 4, at // 2 % 2, at % 2)
                pool[spot] = own[spot] + landed[spot]
                return carry

            lax.fori_loop(0, 16, add, 0)
            self.exchange(item).start()
        elif number == 3:
            self.exchange(item).wait_recv()
            for at in range(2):
                spot = (2 * (z % 2) + at, 1 - y, 1 - x)
                pool[spot] = pool[spot] + self.cross[which][at, rows]
            for one in self.half(item):
                one.start()
        elif number == 4:
            for one in self.half(item):
                one.wait_recv()
            for at in range(2):
                spot = (2 * (z % 2) + at, y if at else 1 - y, 1 - x if at else x)
                pool[spot] = pool[spot] + self.halves[which][at, rows]
            for one in self.side(item):
                one.start()
        elif number == 5:
            for one in self.side(item):
                one.wait_recv()
            sides = self.sides[which]
            for at in range(4):
                total = pool[at, y, x].astype(F32) + sides[0, at, rows].astype(F32)
                pool[at, y, x] = (total + sides[1, at, rows].astype(F32)).astype(pool.dtype)
            for one in self.along_z(item):
                one.start()
        else:
            for one in self.along_z(item):
                one.wait_recv()
            total = pool[z, y, x].astype(F32)
            for step in range(3):
                total = total + self.ends[which][step, rows].astype(F32)
            self.give(self.items[item], total)

    def step(self):
        count = len(self.items)
        if self.tick >= count + self.leads[-1]:
            return False
        if self.tick < count and self.tick not in self.made:
            return False
        for number in reversed(range(7)):
            item = self.tick - self.leads[number]
            if 0 <= item < count:
                self.stage(number, item)
        self.tick += 1
        return True

    def finish(self):
        for item in range(max(0, len(self.items) - self.turns), len(self.items)):
            self.pair(item).wait_send()
            self.sent(item)


class Ring:
    def __init__(self, slots, semaphores):
        self.slots, self.semaphores = slots, semaphores
        self.count = slots.shape[0]
        self.under_way = [None] * self.count
        self.next = 0

    def copy(self, slot, target):
        return pltpu.make_async_copy(self.slots.at[slot], target, self.semaphores.at[slot])

    def settle(self, slot):
        if self.under_way[slot] is not None:
            self.under_way[slot].wait()
            self.under_way[slot] = None

    def settle_all(self):
        for slot in range(self.count):
            self.settle(slot)

    def put(self, values, target):
        slot, self.next = self.next, (self.next + 1) % self.count
        self.settle(slot)
        self.slots[slot] = values.astype(LOW).reshape(self.slots.shape[1:])
        copy = self.copy(slot, target)
        copy.start()
        self.under_way[slot] = copy

        def wait():
            if self.under_way[slot] is copy:
                self.settle(slot)

        return wait

    def fill(self, slot, values):
        self.slots[slot] = values.astype(LOW).reshape(self.slots.shape[1:])

    def start(self, targets):
        for slot, target in enumerate(targets):
            self.under_way[slot] = self.copy(slot, target)
            self.under_way[slot].start()


class Inputs(NamedTuple):
    tokens: Any
    cotangent: Any
    routes: Any
    priority: Any
    small: Any
    shards: Any


class Outputs(NamedTuple):
    activations: Any
    input_grad: Any
    small: Any
    grads: Any
    wholes: Any
    made: Any
    landing: Any


class Scratch(NamedTuple):
    low: Any
    resident: Any
    small_whole: Any
    small_grad: Any
    flat: Any
    vec: Any
    vec_ff: Any
    vec_out: Any
    router: Any
    grad_vec: Any
    grad_ff: Any
    grad_out: Any
    grad_router: Any
    stream: Any
    norm: Any
    packed: Any
    heads: Any
    probs: Any
    slots: Any
    dispatched: Any
    slot_grad: Any
    weight_in: Any
    weight_out: Any
    grad: Any
    table: Any
    wide: Any
    thin: Any
    active: Any
    gate: Any
    ring_a: Any
    ring_b: Any
    ring_c: Any
    own: Any
    landed: Any
    pool: Any
    own_small: Any
    landed_small: Any
    pool_small: Any
    landing_small: Any
    cross: Any
    halves: Any
    sides: Any
    ends: Any
    gather_send: Any
    gather_recv: Any
    gather_local: Any
    scatter_send: Any
    scatter_recv: Any
    scatter_local: Any
    ring_a_sem: Any
    ring_b_sem: Any
    ring_c_sem: Any
    fetch: Any
    shard_sem: Any
    deliver: Any


class Step:
    def __init__(self, plan, inputs, outputs, scratch):
        self.plan, self.i, self.o, self.s = plan, inputs, outputs, scratch
        s = scratch
        wholes = list(s.resident) + list(outputs.wholes) + [s.small_whole]
        made = list(outputs.made) + [s.small_grad]
        self.wholes, self.made = wholes, made
        self.prepared = set()
        self.gather = Gather(
            plan.gather_items,
            list(s.low) + [inputs.small],
            wholes,
            self.prepare,
            s.gather_send,
            s.gather_recv,
            s.gather_local,
        )
        self.scatter = Scatter(
            plan.scatter_items,
            made,
            list(outputs.landing) + [s.landing_small],
            (s.own, s.own_small),
            (s.landed, s.landed_small),
            (s.pool, s.pool_small),
            s.cross,
            s.halves,
            s.sides,
            s.ends,
            self.give,
            s.scatter_send,
            s.scatter_recv,
            s.scatter_local,
        )
        self.ring_a = Ring(s.ring_a, s.ring_a_sem)
        self.ring_b = Ring(s.ring_b, s.ring_b_sem)
        self.ring_c = Ring(s.ring_c, s.ring_c_sem)
        self.tiles_made = {}


    def prepare(self, item):
        which = self.plan.gather_items[item][0]
        if which in self.prepared or which == A_SMALL:
            return
        self.prepared.add(which)
        tiles, rows = self.plan.tiles[which], self.plan.rows[which]
        view, low = self.o.grads[which], self.s.low[which]
        self.shard(which).wait()
        for tile in range(tiles):
            for quarter in range(4):
                found = view[pl.ds(4 * tile + quarter, rows, stride=4 * tiles), :]
                low[tile * rows : (tile + 1) * rows, 128 * quarter : 128 * quarter + 128] = found.astype(LOW)

    def shard(self, which):
        return pltpu.make_async_copy(self.i.shards[which], self.o.grads[which], self.s.shard_sem.at[which])

    def give(self, item, total):
        which, first, count = item
        if which == A_SMALL:
            self.o.small[...] = total
            return
        tiles, rows = self.plan.tiles[which], self.plan.rows[which]
        view = self.o.grads[which]
        at = first
        while at < first + count:
            tile, row = at // rows, at % rows
            take = min(rows - row, first + count - at)
            part = total[at - first : at - first + take]
            for quarter in range(4):
                start = 4 * tiles * row + 4 * tile + quarter
                view[pl.ds(start, take, stride=4 * tiles), :] = part[:, 128 * quarter : 128 * quarter + 128]
            at += take


    def breathe(self):
        self.gather.step()
        self.scatter.step()

    def finished(self, which, tile, wait):
        self.tiles_made[which, tile] = wait
        for item, (one, first, rows) in enumerate(self.plan.scatter_items):
            if item in self.scatter.made or one != which:
                continue
            wanted = [(which, tile) for tile in self.plan.made_of(which, first, rows)]
            if all(key in self.tiles_made for key in wanted):
                self.scatter.made[item] = [self.tiles_made[key] for key in wanted]


    def column_tile(self, which, tile):
        rows = self.plan.rows[which]
        return self.wholes[which][:, :, :, :, pl.ds(tile * rows, rows), :].reshape(TILE, TILE)

    def whole_columns(self, which):
        tiles = [self.column_tile(which, tile) for tile in range(self.plan.tiles[which])]
        return jnp.concatenate(tiles, 1)

    def row_tile(self, which, tile):
        return self.wholes[which][tile].reshape(TILE, TILE)

    def whole_rows(self, which):
        return self.wholes[which][...].reshape(-1, TILE)

    def fetch(self, expert, out):
        source = self.o.wholes[1 if out else 0].at[expert]
        target = self.s.weight_out if out else self.s.weight_in
        return pltpu.make_async_copy(source, target, self.s.fetch.at[1 if out else 0])

    def in_tile(self, tile):
        return self.s.weight_in[:, :, :, pl.ds(tile * 64, 64), :].reshape(TILE, TILE)

    def out_tile(self, tile):
        return self.s.weight_out[tile // 2, tile % 2].reshape(TILE, TILE)

    def in_whole(self):
        return jnp.concatenate([self.in_tile(tile) for tile in range(4)], 1)

    def out_whole(self):
        return self.s.weight_out[...].reshape(EXP_FF, TILE)

    def row(self, name):
        at = ROW_OF[name]
        return self.s.vec[at : at + 1, :]

    def keep_row(self, name, values):
        at = ROW_OF[name]
        self.s.grad_vec[at : at + 1, :] = values


    def spread(self, first, each):
        lane, column = iota((128, TILE), 0), iota((128, TILE), 1)
        return jnp.where(lane == first + column % each, 1.0, 0.0).astype(LOW)

    def spread_router(self, expert):
        lane, column = iota((128, TILE), 0), iota((128, TILE), 1)
        return jnp.where(lane == 64 + 4 * (column % 16) + expert, 1.0, 0.0).astype(LOW)

    def unpack_small(self):
        s = self.s
        s.flat[...] = s.small_whole[...].reshape(256, 128).astype(LOW).astype(F32)
        device_row, column = iota((32, TILE), 0), iota((32, TILE), 1)
        found = [s.flat[pl.ds(row, 32, stride=8), :].astype(LOW) for row in (0, 1, 2, 5)]
        mine = device_row == column // 16
        for row in range(2):

            def vector(at, carry, row=row):
                wide = mm(found[row], self.spread(at * 16, 16))
                s.vec[pl.ds(8 * row + at, 1), :] = jnp.sum(jnp.where(mine, wide, 0.0), 0, keepdims=True)
                return carry

            lax.fori_loop(0, 8, vector, 0)
        router = jnp.zeros((128, TILE), F32)
        for expert in range(EXPERTS):
            wide = jnp.where(mine, mm(found[2], self.spread_router(expert)), 0.0)
            router = jnp.where(iota((128, TILE), 0) == expert, jnp.sum(wide, 0, keepdims=True), router)
        s.router[...] = router.astype(LOW)
        wide = mm(found[2], self.spread(0, 64))
        for tile in range(FF // TILE):
            part = jnp.where(device_row == 8 * tile + column // 64, wide, 0.0)
            s.vec_ff[0:1, tile * TILE : (tile + 1) * TILE] = jnp.sum(part, 0, keepdims=True)
        wide = mm(found[3], self.spread(0, 64))
        for expert in range(EXPERTS):
            part = jnp.where(device_row == 8 * expert + column // 64, wide, 0.0)
            s.vec_out[expert : expert + 1, :] = jnp.sum(part, 0, keepdims=True)
            for at in range(16):
                row = 8 * (8 * expert + at // 2) + 3 + at % 2
                s.vec_ff[1 + expert : 2 + expert, 128 * at : 128 * at + 128] = s.flat[row : row + 1, :]

    def pack_small(self):
        s = self.s
        device_row, column = iota((32, TILE), 0), iota((32, TILE), 1)
        mine = device_row == column // 16

        def back(values, one_hot):
            high = values.astype(LOW)
            rest = (values - high.astype(F32)).astype(LOW)
            return nt(high, one_hot) + nt(rest, one_hot)

        s.grad_vec[len(VECTORS) :, :] = jnp.zeros((16 - len(VECTORS), TILE), F32)
        rows = [jnp.zeros((32, 128), F32) for _ in range(4)]
        for row in range(2):

            def vector(at, carry, row=row):
                values = jnp.where(mine, s.grad_vec[pl.ds(8 * row + at, 1), :], 0.0)
                return carry + back(values, self.spread(at * 16, 16))

            rows[row] = lax.fori_loop(0, 8, vector, rows[row])
        for expert in range(EXPERTS):
            values = jnp.where(mine, s.grad_router[expert : expert + 1, :], 0.0)
            rows[2] += back(values, self.spread_router(expert))
        total = jnp.zeros((32, TILE), F32)
        for tile in range(FF // TILE):
            own = device_row == 8 * tile + column // 64
            total += jnp.where(own, s.grad_ff[0:1, tile * TILE : (tile + 1) * TILE], 0.0)
        rows[2] += back(total, self.spread(0, 64))
        total = jnp.zeros((32, TILE), F32)
        for expert in range(EXPERTS):
            own = device_row == 8 * expert + column // 64
            total += jnp.where(own, s.grad_out[expert : expert + 1, :], 0.0)
        rows[3] = back(total, self.spread(0, 64))
        s.flat[...] = jnp.zeros((256, 128), F32)
        for row, values in zip((0, 1, 2, 5), rows):
            s.flat[pl.ds(row, 32, stride=8), :] = values
        for expert in range(EXPERTS):
            for at in range(16):
                row = 8 * (8 * expert + at // 2) + 3 + at % 2
                s.flat[row : row + 1, :] = s.grad_ff[1 + expert : 2 + expert, 128 * at : 128 * at + 128]
        s.small_grad[...] = s.flat[...].reshape(4, 2, 2, 2, 8, 128)
        self.finished(A_SMALL, 0, lambda: None)


    def norm(self, source, target, gain, bias):
        gain, bias = self.row(gain), self.row(bias)

        def body(rows, carry):
            target[rows] = (normed(source[rows].astype(F32))[0] * gain + bias).astype(LOW)
            return carry

        chunks(body)

    def norm_back(self, source, back, gain, bias):
        wide, grad = self.row(gain), self.s.grad

        def body(rows, carry):
            to_gain, to_bias = carry
            unit, scale = normed(source[rows].astype(F32))
            found = back[rows]
            to_gain = to_gain + column_sum(found * unit)
            to_bias = to_bias + column_sum(found)
            found = found * wide
            mean = jnp.mean(found, -1, keepdims=True)
            along = jnp.mean(found * unit, -1, keepdims=True)
            grad[rows] = grad[rows] + scale * (found - mean - unit * along)
            return to_gain, to_bias

        zero = jnp.zeros((1, D), F32)
        to_gain, to_bias = chunks(body, init=(zero, zero))
        self.keep_row(gain, to_gain)
        self.keep_row(bias, to_bias)


    def masks(self):
        first = iota((PATCH, 128), 1) < HEAD_DIM
        return first, jnp.where(first, 1.0, 0.0).astype(LOW), jnp.where(first, 0.0, 1.0).astype(LOW)

    def scores(self, packed, rows, at, masks):
        query = packed[rows, 128 * at : 128 * at + 128]
        keys = packed[rows, D + 128 * at : D + 128 * at + 128]
        values = packed[rows, 2 * D + 128 * at : 2 * D + 128 * at + 128]
        query = jnp.concatenate([query * masks[1], query * masks[2]], 0)
        found = nt(query, keys) * (1.0 / math.sqrt(HEAD_DIM))
        found = jnp.exp(found - jnp.max(found, -1, keepdims=True))
        return query, keys, values, found / jnp.sum(found, -1, keepdims=True)

    def attention(self, block, source, target, names):
        s = self.s
        gain, bias, query, value, proj = names
        qkv_at, proj_at = (A_QKV1, A_PROJ1) if block == 0 else (A_QKV2, A_PROJ2)
        low, packed, heads = s.norm.at[0 if block == 0 else 2], s.packed.at[block], s.heads.at[block]
        self.norm(source, low, gain, bias)
        self.breathe()
        self.gather.need(qkv_at)
        for part in range(3):
            found = mm(low[...], self.column_tile(qkv_at, part))
            if part != 1:
                found = found + self.row(query if part == 0 else value)
            packed[:, part * D : (part + 1) * D] = found.astype(LOW)
        self.breathe()

        def image(number, carry):
            rows = pl.ds(pl.multiple_of(number * PATCH, PATCH), PATCH)
            masks = self.masks()
            for at in range(HEADS // 2):
                unused, unused, values, weights = self.scores(packed, rows, at, masks)
                found = mm(weights.astype(LOW), values)
                found = jnp.where(masks[0], found[:PATCH], found[PATCH:])
                heads[rows, 128 * at : 128 * at + 128] = found.astype(LOW)
            return carry

        lax.fori_loop(0, ROWS // PATCH, image, 0)
        self.breathe()
        self.gather.need(proj_at)
        found = mm(heads[...], self.column_tile(proj_at, 0)) + self.row(proj)
        target[...] = source[...].astype(F32) + found

    def low_and_sums(self, source, target):
        def body(rows, carry):
            found = source[rows].astype(LOW)
            target[rows] = found
            return carry + column_sum(found)

        return chunks(body, init=jnp.zeros((1, D), F32))

    def attention_back(self, block, source, names):
        s = self.s
        gain, bias, query_bias, value_bias, proj_bias = names
        qkv_at, proj_at = (A_QKV1, A_PROJ1) if block == 0 else (A_QKV2, A_PROJ2)
        low, packed, heads = s.norm.at[0 if block == 0 else 2], s.packed.at[block], s.heads.at[block]
        self.keep_row(proj_bias, self.low_and_sums(s.grad, s.thin))
        target = self.made[proj_at]
        self.finished(proj_at, 0, self.ring_a.put(tn(heads[...], s.thin[...]), target))
        s.gate[:, :D] = nt(s.thin[...], self.column_tile(proj_at, 0)).astype(LOW)
        self.breathe()
        scale = 1.0 / math.sqrt(HEAD_DIM)

        def image(number, carry):
            rows = pl.ds(pl.multiple_of(number * PATCH, PATCH), PATCH)
            masks = self.masks()
            for at in range(HEADS // 2):
                query, keys, values, weights = self.scores(packed, rows, at, masks)
                found = s.gate[rows, 128 * at : 128 * at + 128]
                found = jnp.concatenate([found * masks[1], found * masks[2]], 0)
                to_weights = nt(found, values)
                to_values = tn(weights.astype(LOW), found)
                inner = jnp.sum(to_weights * weights, -1, keepdims=True)
                to_scores = (weights * (to_weights - inner)).astype(LOW)
                to_query = mm(to_scores, keys) * scale
                to_query = jnp.where(masks[0], to_query[:PATCH], to_query[PATCH:])
                to_keys = tn(to_scores, query) * scale
                for part, one in enumerate((to_query, to_keys, to_values)):
                    s.active[rows, part * D + 128 * at : part * D + 128 * at + 128] = one.astype(LOW)
            return carry

        lax.fori_loop(0, 2, image, 0)
        self.breathe()
        lax.fori_loop(2, 4, image, 0)
        self.breathe()
        found = s.active[:, : 3 * D]
        self.keep_row(query_bias, column_sum(found[:, :D]))
        self.keep_row(value_bias, column_sum(found[:, 2 * D :]))
        self.ring_a.settle_all()
        for part in range(3):
            self.ring_a.fill(part, tn(low[...], found[:, part * D : (part + 1) * D]))
        s.wide[...] = nt(found, self.whole_columns(qkv_at))
        self.ring_a.start([self.made[qkv_at].at[:, :, :, :, pl.ds(16 * part, 16)] for part in range(3)])
        for part in range(3):
            self.finished(qkv_at, part, self.ring_a.settle_all)
        self.breathe()
        self.norm_back(source, s.wide, gain, bias)
        self.breathe()


    def feed(self, source, target):
        s = self.s
        low = s.norm.at[1]
        self.norm(source, low, NORM2_GAIN, NORM2_BIAS)
        self.breathe()
        self.gather.need(A_HIDDEN)
        self.gather.need(A_OUTPUT)
        for tile in range(FF // TILE):
            columns = slice(tile * TILE, (tile + 1) * TILE)
            pre = mm(low[...], self.column_tile(A_HIDDEN, tile)) + s.vec_ff[0:1, columns]
            s.active[:, columns] = gelu_low(pre)
        target[...] = source[...] + self.row(OUTPUT_BIAS) + mm(s.active[...], self.whole_rows(A_OUTPUT))
        self.breathe()

    def feed_back(self, source):
        s = self.s
        low = s.norm.at[1]
        self.keep_row(OUTPUT_BIAS, self.low_and_sums(s.grad, s.thin))
        for tile in range(FF // TILE):
            columns = slice(tile * TILE, (tile + 1) * TILE)
            pre = mm(low[...], self.column_tile(A_HIDDEN, tile)) + s.vec_ff[0:1, columns]
            active, slope = gelu_and_slope(pre)
            s.active[:, columns] = active
            found = (slope * nt(s.thin[...], self.row_tile(A_OUTPUT, tile))).astype(LOW)
            s.gate[:, columns] = found
            s.grad_ff[0:1, columns] = column_sum(found)
        self.breathe()
        self.ring_b.settle_all()
        for tile in range(FF // TILE):
            found = s.active[:, tile * TILE : (tile + 1) * TILE]
            self.ring_b.fill(tile, tn(found, s.thin[...]))
        self.ring_b.start([self.made[A_OUTPUT].at[tile] for tile in range(FF // TILE)])
        for tile in range(FF // TILE):
            self.finished(A_OUTPUT, tile, self.ring_b.settle_all)
        self.breathe()
        self.ring_a.settle_all()
        for tile in range(FF // TILE):
            found = s.gate[:, tile * TILE : (tile + 1) * TILE]
            self.ring_a.fill(tile, tn(low[...], found))
        s.wide[...] = nt(s.gate[...], self.whole_columns(A_HIDDEN))
        self.ring_a.start([self.made[A_HIDDEN].at[:, :, :, :, pl.ds(16 * tile, 16)] for tile in range(4)])
        for tile in range(FF // TILE):
            self.finished(A_HIDDEN, tile, self.ring_a.settle_all)
        self.breathe()
        self.norm_back(source, s.wide, NORM2_GAIN, NORM2_BIAS)
        self.breathe()


    def route(self):
        s = self.s
        lane = iota((ROWS, 128), 1)
        logits = jnp.where(lane < EXPERTS, nt(s.norm[3], s.router[...]), -1e30)
        found = jnp.exp(logits - jnp.max(logits, -1, keepdims=True))
        s.probs[...] = found / jnp.sum(found, -1, keepdims=True)
        same = iota((GROUP, GROUP), 0) == iota((GROUP, GROUP), 1)

        def upright(row):
            return jnp.sum(jnp.where(same, row, 0.0), 1, keepdims=True)

        def flat(column):
            return jnp.sum(jnp.where(same, column, 0.0), 0, keepdims=True)

        lane = iota((GROUP, 128), 1)
        for group in range(ROWS // GROUP):
            rows = slice(group * GROUP, (group + 1) * GROUP)
            first_up, second_up = (self.i.routes[rows, at : at + 1].astype(F32) for at in range(2))
            rank = self.i.priority[group : group + 1, :].astype(F32)
            first, second, rank_up = flat(first_up), flat(second_up), upright(rank)
            before = jnp.where(rank_up < rank, 1.0, 0.0)
            place_first = jnp.sum(jnp.where(first_up == first, before, 0.0), 0, keepdims=True)
            place_second = jnp.sum(
                jnp.where(second_up == second, before, 0.0) + jnp.where(first_up == second, 1.0, 0.0),
                0,
                keepdims=True,
            )
            kept = []
            for at, (expert, spot) in enumerate(((first, place_first), (second, place_second))):
                slot = jnp.where(spot < CAP, expert * CAP + spot, -1.0)
                s.slots[2 * group + at : 2 * group + at + 1, :] = slot
                kept.append(upright(slot))
            probs = s.probs[rows]
            gates = [
                jnp.sum(jnp.where(lane == one.astype(jnp.int32), probs, 0.0), -1, keepdims=True)
                for one in (first_up, second_up)
            ]
            columns = [first_up, second_up] + gates + kept
            table = jnp.zeros((GROUP, 128), F32)
            for at, one in enumerate(columns):
                table = jnp.where(lane == at, one, table)
            s.table[rows, :] = table
            slots = pl.ds(group * CAP, CAP)
            given = self.i.cotangent[rows].astype(F32)
            for at, gate in enumerate(gates):
                s.thin[at * GROUP : (at + 1) * GROUP, :] = (gate * given).astype(LOW)
            for expert in range(EXPERTS):
                picks = self.picks(group, expert)
                s.dispatched[expert, slots, :] = mm(picks[0] + picks[1], s.norm[3, rows, :]).astype(LOW)
                s.slot_grad[expert, slots, :] = mm(jnp.concatenate(picks, 1), s.thin[...]).astype(LOW)

    def picks(self, group, expert):
        slot = (iota((CAP, GROUP), 0) + expert * CAP).astype(F32)
        return [
            jnp.where(slot == self.s.slots[2 * group + at : 2 * group + at + 1, :], 1.0, 0.0).astype(LOW)
            for at in range(2)
        ]

    def picks_up(self, group):
        slot = iota((GROUP, SLOTS), 1).astype(F32)
        rows = slice(group * GROUP, (group + 1) * GROUP)
        return [
            jnp.where(slot == self.s.table[rows, 4 + at : 5 + at], 1.0, 0.0).astype(LOW) for at in range(2)
        ]

    def experts_first(self):
        s = self.s
        self.fetch(0, False).start()
        for expert in range(EXPERTS):
            self.fetch(expert, False).wait()
            self.ring_c.settle_all()
            rows, given = s.dispatched[expert], s.slot_grad[expert]
            for tile in range(EXP_FF // TILE):
                bias = s.vec_ff[1 + expert : 2 + expert, tile * TILE : (tile + 1) * TILE]
                hidden = gelu_low(mm(rows, self.in_tile(tile)) + bias)
                self.ring_c.fill(tile, tn(hidden, given))
            s.grad_out[expert : expert + 1, :] = column_sum(given)
            if expert + 1 < EXPERTS:
                self.fetch(expert + 1, False).start()
            self.ring_c.start([self.made[A_OUT].at[expert, tile // 2, tile % 2] for tile in range(4)])
            self.finished(A_OUT, expert, self.ring_c.settle_all)
            self.breathe()
            self.breathe()

    def experts_then(self):
        s = self.s
        count = 2 * CAP
        self.fetch(0, False).start()
        self.fetch(0, True).start()
        for expert in range(EXPERTS):
            self.fetch(expert, False).wait()
            self.fetch(expert, True).wait()
            self.ring_b.settle_all()
            rows, given = s.dispatched[expert], s.slot_grad[expert]
            for tile in range(EXP_FF // TILE):
                columns = slice(tile * TILE, (tile + 1) * TILE)
                pre = mm(rows, self.in_tile(tile)) + s.vec_ff[1 + expert : 2 + expert, columns]
                active, slope = gelu_and_slope(pre)
                s.active[:count, columns] = active
                found = (slope * nt(given, self.out_tile(tile))).astype(LOW)
                s.gate[:count, columns] = found
                s.grad_ff[1 + expert : 2 + expert, columns] = column_sum(found)
            out = mm(s.active[:count], self.out_whole()) + s.vec_out[expert : expert + 1, :]
            to_pre = s.gate[:count]
            for tile in range(EXP_FF // TILE):
                self.ring_b.fill(tile, tn(rows, to_pre[:, tile * TILE : (tile + 1) * TILE]))
            s.slot_grad[expert] = nt(to_pre, self.in_whole()).astype(LOW)
            s.dispatched[expert] = out.astype(LOW)
            if expert + 1 < EXPERTS:
                self.fetch(expert + 1, False).start()
                self.fetch(expert + 1, True).start()
            self.ring_b.start([self.made[A_IN].at[expert, :, :, :, pl.ds(64 * tile, 64)] for tile in range(4)])
            self.finished(A_IN, expert, self.ring_b.settle_all)
            self.breathe()
            self.breathe()

    def combine(self):
        s = self.s
        lane = iota((GROUP, 128), 1)
        for group in range(ROWS // GROUP):
            rows = slice(group * GROUP, (group + 1) * GROUP)
            slots = pl.ds(group * CAP, CAP)
            picks = self.picks_up(group)
            out = s.dispatched[:, slots, :].reshape(SLOTS, D)
            picked = [mm(pick, out) for pick in picks]
            gates = [s.table[rows, 2 + at : 3 + at] for at in range(2)]
            given = self.i.cotangent[rows].astype(F32)
            found = s.stream[2, rows, :] + gates[0] * picked[0] + gates[1] * picked[1]
            s.thin[rows, :] = found.astype(LOW)
            probs = s.probs[rows]
            to_probs = jnp.zeros((GROUP, 128), F32)
            for at in range(2):
                to_gate = jnp.sum(given * picked[at], -1, keepdims=True)
                expert = s.table[rows, at : at + 1].astype(jnp.int32)
                to_probs = to_probs + jnp.where(lane == expert, to_gate, 0.0)
            inner = jnp.sum(to_probs * probs, -1, keepdims=True)
            to_logits = (probs * (to_probs - inner)).astype(LOW)
            s.gate[rows, :128] = to_logits
            back = mm(picks[0] + picks[1], s.slot_grad[:, slots, :].reshape(SLOTS, D))
            s.wide[rows, :] = back + mm(to_logits, s.router[...])
            s.grad[rows, :] = given
        s.grad_router[...] = tn(s.gate[:, :128], s.norm[3])[:8]
        copy = pltpu.make_async_copy(s.thin, self.o.activations, s.deliver.at[0])
        copy.start()
        self.breathe()
        self.norm_back(s.stream.at[2], s.wide, NORM4_GAIN, NORM4_BIAS)
        copy.wait()
        self.breathe()

    def run(self):
        s = self.s
        for which in range(COUNT):
            self.shard(which).start()
        greet(partners(*place()))
        self.gather.need(A_SMALL)
        self.unpack_small()
        tokens, stream = self.i.tokens, s.stream
        first = (NORM1_GAIN, NORM1_BIAS, QUERY1, VALUE1, PROJ1_BIAS)
        second = (NORM3_GAIN, NORM3_BIAS, QUERY2, VALUE2, PROJ2_BIAS)
        self.attention(0, tokens, stream.at[0], first)
        self.breathe()
        self.feed(stream.at[0], stream.at[1])
        self.attention(1, stream.at[1], stream.at[2], second)
        self.breathe()
        self.norm(stream.at[2], s.norm.at[3], NORM4_GAIN, NORM4_BIAS)
        self.breathe()
        self.route()
        self.gather.need(A_IN)
        self.experts_first()
        self.gather.need(A_OUT)
        self.experts_then()
        self.combine()
        self.attention_back(1, stream.at[1], second)
        self.feed_back(stream.at[0])
        self.attention_back(0, tokens, first)
        s.thin[...] = s.grad[...].astype(LOW)
        copy = pltpu.make_async_copy(s.thin, self.o.input_grad, s.deliver.at[1])
        copy.start()
        self.pack_small()
        while self.scatter.step():
            pass
        self.gather.finish()
        self.scatter.finish()
        for ring in (self.ring_a, self.ring_b, self.ring_c):
            ring.settle_all()
        copy.wait()


class Plan:
    def __init__(self):
        self.tiles = [BIG[name][1] // TILE for name in BIG_NAMES] + [1]
        self.rows = [BIG[name][0] // 32 for name in BIG_NAMES] + [8]
        self.height = [tiles * rows for tiles, rows in zip(self.tiles, self.rows)]
        self.gather_items = [(A_SMALL, 0, 8)]
        for which, step in (
            (A_QKV1, 16),
            (A_PROJ1, 16),
            (A_HIDDEN, 32),
            (A_OUTPUT, 32),
            (A_QKV2, 16),
            (A_PROJ2, 16),
            (A_IN, 32),
            (A_OUT, 32),
        ):
            self.gather_items += self.parts(which, step)
        self.scatter_items = []
        for which, step in (
            (A_OUT, 32),
            (A_IN, 32),
            (A_PROJ2, 16),
            (A_QKV2, 16),
            (A_OUTPUT, 32),
            (A_HIDDEN, 32),
            (A_PROJ1, 16),
            (A_QKV1, 16),
            (A_SMALL, 8),
        ):
            self.scatter_items += self.parts(which, step)

    def parts(self, which, step):
        return [(which, first, step) for first in range(0, self.height[which], step)]

    def made_of(self, which, first, rows):
        if which == A_SMALL:
            return [0]
        if which == A_OUT:
            return list(range(EXPERTS))
        if which == A_IN:
            return list(range(EXPERTS))
        if which == A_OUTPUT:
            return list(range(4))
        return sorted({row // self.rows[which] for row in range(first, first + rows)})


def mega_kernel(plan, trees, *refs):
    parts, at = [], 0
    for tree in trees:
        parts.append(jax.tree.unflatten(tree, refs[at : at + tree.num_leaves]))
        at += tree.num_leaves
    Step(plan, *parts).run()


def mega(tokens, cotangent, routes, priority, small, shards):
    plan = Plan()
    whole = [(4, 2, 2, 2, height, TILE) for height in plan.height[:COUNT]]
    vmem = pltpu.VMEM
    inputs = Inputs(tokens, cotangent, routes, priority, small, shards)
    outputs = Outputs(
        activations=jax.ShapeDtypeStruct((ROWS, D), LOW),
        input_grad=jax.ShapeDtypeStruct((ROWS, D), LOW),
        small=jax.ShapeDtypeStruct((8, 128), F32),
        grads=[jax.ShapeDtypeStruct(one.shape, F32) for one in shards],
        wholes=[jax.ShapeDtypeStruct(whole[which], LOW) for which in (A_IN, A_OUT)],
        made=[jax.ShapeDtypeStruct(shape, LOW) for shape in whole],
        landing=[jax.ShapeDtypeStruct((4, 2, 2, height, TILE), LOW) for height in plan.height[:COUNT]],
    )
    here = pl.BlockSpec(memory_space=pltpu.VMEM)
    anywhere = pl.BlockSpec(memory_space=pl.ANY)
    in_specs = Inputs(here, here, here, here, here, [anywhere] * COUNT)
    out_specs = Outputs(anywhere, anywhere, here, [here] * COUNT, [anywhere] * 2, [anywhere] * COUNT, [anywhere] * COUNT)

    def room(*lead):
        return [vmem(lead + (height, TILE), LOW) for height in plan.height[:COUNT]] + [
            vmem(lead + (8, 128), F32)
        ]

    def semaphores(link):
        return pltpu.SemaphoreType.DMA((link.turns, link.messages))

    dma = pltpu.SemaphoreType.DMA
    scratch = Scratch(
        low=room()[:COUNT],
        resident=[vmem(whole[which], LOW) for which in range(6)],
        small_whole=vmem((4, 2, 2, 2, 8, 128), F32),
        small_grad=vmem((4, 2, 2, 2, 8, 128), F32),
        flat=vmem((256, 128), F32),
        vec=vmem((16, D), F32),
        vec_ff=vmem((8, FF), F32),
        vec_out=vmem((8, D), F32),
        router=vmem((128, D), LOW),
        grad_vec=vmem((16, D), F32),
        grad_ff=vmem((8, FF), F32),
        grad_out=vmem((8, D), F32),
        grad_router=vmem((8, D), F32),
        stream=vmem((3, ROWS, D), F32),
        norm=vmem((4, ROWS, D), LOW),
        packed=vmem((2, ROWS, 3 * D), LOW),
        heads=vmem((2, ROWS, D), LOW),
        probs=vmem((ROWS, 128), F32),
        slots=vmem((8, GROUP), F32),
        dispatched=vmem((EXPERTS, 2 * CAP, D), LOW),
        slot_grad=vmem((EXPERTS, 2 * CAP, D), LOW),
        weight_in=vmem((2, 2, 2, 256, TILE), LOW),
        weight_out=vmem((2, 2, 2, 256, TILE), LOW),
        grad=vmem((ROWS, D), F32),
        table=vmem((ROWS, 128), F32),
        wide=vmem((ROWS, D), F32),
        thin=vmem((ROWS, D), LOW),
        active=vmem((ROWS, FF), LOW),
        gate=vmem((ROWS, FF), LOW),
        ring_a=vmem((4, 4, 2, 2, 2, 16, TILE), LOW),
        ring_b=vmem((4, 2, 2, 2, 64, TILE), LOW),
        ring_c=vmem((4, 2, 256, TILE), LOW),
        own=vmem((2, 4, 2, 2, 32, TILE), LOW),
        landed=vmem((1, 4, 2, 2, 32, TILE), LOW),
        pool=vmem((Scatter.turns, 4, 2, 2, 32, TILE), LOW),
        own_small=vmem((4, 2, 2, 8, 128), F32),
        landed_small=vmem((4, 2, 2, 8, 128), F32),
        pool_small=vmem((4, 2, 2, 8, 128), F32),
        landing_small=vmem((4, 2, 2, 8, 128), F32),
        cross=room(2),
        halves=room(2),
        sides=room(2, 4),
        ends=room(3),
        gather_send=semaphores(Gather),
        gather_recv=semaphores(Gather),
        gather_local=dma((Gather.turns,)),
        scatter_send=semaphores(Scatter),
        scatter_recv=semaphores(Scatter),
        scatter_local=dma((3,)),
        ring_a_sem=dma((4,)),
        ring_b_sem=dma((4,)),
        ring_c_sem=dma((4,)),
        fetch=dma((2,)),
        shard_sem=dma((COUNT,)),
        deliver=dma((2,)),
    )
    operands, in_tree = jax.tree.flatten(inputs)
    out_shapes, out_tree = jax.tree.flatten(outputs)
    scratch_shapes, scratch_tree = jax.tree.flatten(scratch)
    found = pl.pallas_call(
        functools.partial(mega_kernel, plan, (in_tree, out_tree, scratch_tree)),
        out_shape=out_shapes,
        in_specs=jax.tree.leaves(in_specs),
        out_specs=jax.tree.leaves(out_specs),
        scratch_shapes=scratch_shapes,
        compiler_params=pltpu.CompilerParams(
            collective_id=0, has_side_effects=True, vmem_limit_bytes=64 * 1024 * 1024
        ),
    )(*operands)
    return jax.tree.unflatten(out_tree, found)


def join_small(shards):
    def zeros(count):
        return jnp.zeros((count,), F32)

    parts = [shards[name] for name in VECTORS] + [zeros(16), shards[HIDDEN_BIAS], shards[ROUTER]]
    parts += [shards[EXPERT_IN_BIAS], shards[EXPERT_OUT_BIAS], zeros(320)]
    return jnp.concatenate(parts).reshape(8, 128)


SMALL_PARTS = tuple((name, at // 8, at % 8 * 16, 16) for at, name in enumerate(VECTORS)) + (
    (HIDDEN_BIAS, 2, 0, 64),
    (ROUTER, 2, 64, 64),
    (EXPERT_IN_BIAS, 3, 0, 256),
    (EXPERT_OUT_BIAS, 5, 0, 64),
)


def deliver_kernel(count, *refs):
    small, sources = refs[0], refs[1 : 1 + count]
    targets, parts = refs[1 + count : 1 + 2 * count], refs[1 + 2 * count :]
    for source, target in zip(sources, targets):

        def body(rows, carry, source=source, target=target):
            target[rows] = source[rows]
            return carry

        chunks(body, source.shape[0], size=64)
    for part, (name, row, lane, length) in zip(parts, SMALL_PARTS):
        for at in range(0, length, 128):
            step = min(128, length)
            part[:, at : at + step] = small[row + at // 128 : row + at // 128 + 1, lane : lane + step]


def deliver(small, arrays):
    here = pl.BlockSpec(memory_space=pltpu.VMEM)
    count = len(arrays)
    shapes = [jax.ShapeDtypeStruct(one.shape, one.dtype) for one in arrays]
    shapes += [jax.ShapeDtypeStruct((1, length), F32) for name, row, lane, length in SMALL_PARTS]
    found = pl.pallas_call(
        functools.partial(deliver_kernel, count),
        out_shape=shapes,
        in_specs=[here] * (1 + count),
        out_specs=[here] * len(shapes),
        compiler_params=pltpu.CompilerParams(vmem_limit_bytes=60 * 1024 * 1024),
    )(small, *arrays)
    parts = {entry[0]: part.reshape(-1) for entry, part in zip(SMALL_PARTS, found[count:])}
    return found[:count], parts


def on_slice(tokens, *rest):
    shards = dict(zip(NAMES, rest[: len(NAMES)]))
    routes, priority, cotangent = rest[len(NAMES) :]
    found = mega(
        tokens.reshape(ROWS, D),
        cotangent.reshape(ROWS, D),
        routes.reshape(ROWS, 2),
        priority,
        join_small(shards),
        [shards[name].reshape(-1, 128) for name in BIG_NAMES],
    )
    arrays, mine = deliver(found.small, [found.activations, found.input_grad] + list(found.grads))
    mine.update((name, one.reshape(-1)) for name, one in zip(BIG_NAMES, arrays[2:]))
    outs = tuple(one.reshape(tokens.shape) for one in arrays[:2])
    return outs + tuple(mine[name] for name in NAMES)


def routed_forward(normed, weights, routes, priority):
    groups = priority.shape[0]
    normed_low = normed.astype(jnp.bfloat16)
    logits = jnp.dot(normed_low, weights[ROUTER], preferred_element_type=jnp.float32)
    row_max = jnp.max(logits, -1, keepdims=True)
    exponent = jnp.exp(logits - row_max)
    probs_all = exponent / jnp.sum(exponent, -1, keepdims=True)
    expert_ids = jnp.arange(EXPERTS, dtype=jnp.int32)
    flat_routes = routes.reshape(-1, 2)
    hots = [(flat_routes[:, k : k + 1] == expert_ids).astype(jnp.float32) for k in range(2)]
    gates = [jnp.sum(probs_all * hot, -1, keepdims=True) for hot in hots]
    first, second = routes[:, :, 0], routes[:, :, 1]
    before = priority[:, None, :] < priority[:, :, None]
    place_first = jnp.sum(before & (first[:, None, :] == first[:, :, None]), -1)
    place_second = jnp.sum(before & (second[:, None, :] == second[:, :, None]), -1)
    place_second = place_second + jnp.sum(first[:, None, :] == second[:, :, None], -1)
    slot_ids = jnp.arange(SLOTS, dtype=jnp.int32)
    picks = [
        ((which * CAP + at)[:, None, :] == slot_ids[None, :, None]) & (at < CAP)[:, None, :]
        for which, at in ((first, place_first), (second, place_second))
    ]
    picks = [pick.astype(jnp.bfloat16) for pick in picks]
    grouped = normed_low.reshape(groups, GROUP, D)
    dispatched = jnp.einsum(
        "gst,gtd->gsd", picks[0] + picks[1], grouped, preferred_element_type=jnp.float32
    ).astype(jnp.bfloat16)
    dispatched = by_expert(dispatched)
    pre_act = jnp.einsum(
        "ecd,edf->ecf", dispatched, weights[EXPERT_IN], preferred_element_type=jnp.float32
    )
    pre_act = pre_act + weights[EXPERT_IN_BIAS].astype(jnp.float32)[:, None, :]
    hidden = jax.nn.gelu(pre_act).astype(jnp.bfloat16)
    expert_out = jnp.einsum(
        "ecf,efd->ecd", hidden, weights[EXPERT_OUT], preferred_element_type=jnp.float32
    )
    expert_out = expert_out + weights[EXPERT_OUT_BIAS].astype(jnp.float32)[:, None, :]
    expert_low = by_group(expert_out.astype(jnp.bfloat16), groups)
    picked = [
        jnp.einsum("gst,gsd->gtd", pick, expert_low, preferred_element_type=jnp.float32).reshape(-1, D)
        for pick in picks
    ]
    output = gates[0] * picked[0] + gates[1] * picked[1]
    return output, (normed_low, probs_all, hots, gates, picks, dispatched, pre_act, hidden, picked)


def by_expert(slots):
    groups, width = slots.shape[0], slots.shape[2]
    slots = slots.reshape(groups, EXPERTS, CAP, width).transpose(1, 0, 2, 3)
    return slots.reshape(EXPERTS, groups * CAP, width)


def by_group(slots, groups):
    width = slots.shape[2]
    slots = slots.reshape(EXPERTS, groups, CAP, width).transpose(1, 0, 2, 3)
    return slots.reshape(groups, SLOTS, width)


def routed_backward(grad_output, saved_state, weights):
    normed_low, probs_all, hots, gates, picks, dispatched, pre_act, hidden, picked = saved_state
    groups = picks[0].shape[0]
    grad_gates = [jnp.sum(grad_output * one, -1, keepdims=True) for one in picked]
    grad_expert = sum(
        jnp.einsum(
            "gst,gtd->gsd",
            pick,
            (gate * grad_output).astype(jnp.bfloat16).reshape(groups, GROUP, D),
            preferred_element_type=jnp.float32,
        )
        for pick, gate in zip(picks, gates)
    )
    grad_expert = by_expert(grad_expert.astype(jnp.bfloat16))
    grad_out_weight = jnp.einsum(
        "ecf,ecd->efd", hidden, grad_expert, preferred_element_type=jnp.float32
    )
    grad_out_bias = jnp.sum(grad_expert.astype(jnp.float32), 1)
    grad_hidden = jnp.einsum(
        "ecd,efd->ecf", grad_expert, weights[EXPERT_OUT], preferred_element_type=jnp.float32
    )
    grad_pre = gelu_backward(pre_act, grad_hidden).astype(jnp.bfloat16)
    grad_in_weight = jnp.einsum(
        "ecd,ecf->edf", dispatched, grad_pre, preferred_element_type=jnp.float32
    )
    grad_in_bias = jnp.sum(grad_pre.astype(jnp.float32), 1)
    grad_dispatched = jnp.einsum(
        "ecf,edf->ecd", grad_pre, weights[EXPERT_IN], preferred_element_type=jnp.float32
    )
    grad_slots = by_group(grad_dispatched.astype(jnp.bfloat16), groups)
    grad_normed = jnp.einsum(
        "gst,gsd->gtd", picks[0] + picks[1], grad_slots, preferred_element_type=jnp.float32
    ).reshape(-1, D)
    grad_probs = hots[0] * grad_gates[0] + hots[1] * grad_gates[1]
    inner_sum = jnp.sum(grad_probs * probs_all, -1, keepdims=True)
    grad_logits = (probs_all * (grad_probs - inner_sum)).astype(jnp.bfloat16)
    grad_router = jnp.einsum(
        "rd,re->de", normed_low, grad_logits, preferred_element_type=jnp.float32
    )
    grad_normed = grad_normed + jnp.einsum(
        "re,de->rd", grad_logits, weights[ROUTER], preferred_element_type=jnp.float32
    )
    return grad_normed, (grad_router, grad_in_weight, grad_in_bias, grad_out_weight, grad_out_bias)


def gather_small(shards):
    lengths = [shards[name].shape[0] for name in SMALL]
    joined = jnp.concatenate([shards[name].astype(jnp.bfloat16) for name in SMALL])
    whole = lax.all_gather(joined, "fsdp", axis=0)
    found, at = {}, 0
    for name, length in zip(SMALL, lengths):
        found[name] = whole[:, at : at + length].reshape(-1)
        at += length
    found[ROUTER] = found[ROUTER].reshape(D, EXPERTS)
    found[EXPERT_IN_BIAS] = found[EXPERT_IN_BIAS].reshape(EXPERTS, EXP_FF)
    found[EXPERT_OUT_BIAS] = found[EXPERT_OUT_BIAS].reshape(EXPERTS, D)
    return found


def scatter_small(grads, devices):
    joined = jnp.concatenate([grads[name].reshape(devices, -1) for name in SMALL], 1)
    width = joined.shape[1]
    mine = lax.psum_scatter(joined.reshape(-1), "fsdp", scatter_dimension=0, tiled=True)
    found, at = {}, 0
    for name in SMALL:
        length = grads[name].size // devices
        found[name] = mine[at : at + length]
        at += length
    return found


def on_device(devices, tokens, *rest):
    shards = dict(zip(NAMES, rest[: len(NAMES)]))
    routes, priority, cotangent = rest[len(NAMES) :]
    images = tokens.shape[0]
    groups = priority.shape[0]
    weights = gather_small(shards)
    for name in BIG_NAMES:
        whole = lax.all_gather(shards[name].astype(jnp.bfloat16), "fsdp", axis=0, tiled=True)
        weights[name] = whole.reshape(BIG[name])
    weights[EXPERT_IN] = weights[EXPERT_IN].reshape(EXPERTS, D, EXP_FF)
    weights[EXPERT_OUT] = weights[EXPERT_OUT].reshape(EXPERTS, EXP_FF, D)
    wide = {name: weights[name].astype(jnp.float32) for name in GAINS}
    stream0 = tokens.reshape(images * PATCH, D).astype(jnp.float32)
    grad4 = cotangent.reshape(images * PATCH, D).astype(jnp.float32)
    normed1 = norm_forward(stream0, wide[NORM1_GAIN], wide[NORM1_BIAS])
    out, attention1 = attention_forward(
        normed1, *(weights[name] for name in (QKV1, QUERY1, VALUE1, PROJ1, PROJ1_BIAS))
    )
    stream1 = stream0 + out
    normed2 = norm_forward(stream1, wide[NORM2_GAIN], wide[NORM2_BIAS])
    out, feed = feed_forward(
        normed2, *(weights[name] for name in (HIDDEN, HIDDEN_BIAS, OUTPUT, OUTPUT_BIAS))
    )
    stream2 = stream1 + out
    normed3 = norm_forward(stream2, wide[NORM3_GAIN], wide[NORM3_BIAS])
    out, attention2 = attention_forward(
        normed3, *(weights[name] for name in (QKV2, QUERY2, VALUE2, PROJ2, PROJ2_BIAS))
    )
    stream3 = stream2 + out
    normed4 = norm_forward(stream3, wide[NORM4_GAIN], wide[NORM4_BIAS])
    out, routed = routed_forward(normed4, weights, routes.reshape(groups, GROUP, 2), priority)
    activations = (stream3 + out).astype(jnp.bfloat16).reshape(tokens.shape)

    grads = {}

    def keep(names, values):
        grads.update(zip(names, values))

    grad, found = routed_backward(grad4, routed, weights)
    keep((ROUTER, EXPERT_IN, EXPERT_IN_BIAS, EXPERT_OUT, EXPERT_OUT_BIAS), found)
    back, *found = norm_backward(stream3, wide[NORM4_GAIN], wide[NORM4_BIAS], grad)
    keep((NORM4_GAIN, NORM4_BIAS), found)
    grad3 = grad4 + back
    grad, found = attention_backward(grad3, attention2, weights[QKV2], weights[PROJ2])
    keep((QKV2, QUERY2, VALUE2, PROJ2, PROJ2_BIAS), found)
    back, *found = norm_backward(stream2, wide[NORM3_GAIN], wide[NORM3_BIAS], grad)
    keep((NORM3_GAIN, NORM3_BIAS), found)
    grad2 = grad3 + back
    grad, found = feed_backward(grad2, feed, weights[HIDDEN], weights[OUTPUT])
    keep((HIDDEN, HIDDEN_BIAS, OUTPUT, OUTPUT_BIAS), found)
    back, *found = norm_backward(stream1, wide[NORM2_GAIN], wide[NORM2_BIAS], grad)
    keep((NORM2_GAIN, NORM2_BIAS), found)
    grad1 = grad2 + back
    grad, found = attention_backward(grad1, attention1, weights[QKV1], weights[PROJ1])
    keep((QKV1, QUERY1, VALUE1, PROJ1, PROJ1_BIAS), found)
    back, *found = norm_backward(stream0, wide[NORM1_GAIN], wide[NORM1_BIAS], grad)
    keep((NORM1_GAIN, NORM1_BIAS), found)
    input_grad = (grad1 + back).astype(jnp.bfloat16).reshape(tokens.shape)

    mine = scatter_small(grads, devices)
    for name in BIG_NAMES:
        flat = grads[name].reshape(-1)
        mine[name] = lax.psum_scatter(flat, "fsdp", scatter_dimension=0, tiled=True)
    return (activations, input_grad) + tuple(mine[name] for name in NAMES)


def solution(mesh):
    rows = P("fsdp", None, None)
    flat = tuple(P("fsdp") for _ in NAMES)
    devices = mesh.shape["fsdp"]
    return jax.shard_map(
        on_slice if devices == 32 else functools.partial(on_device, devices),
        mesh=mesh,
        in_specs=(rows,) + flat + (rows, P("fsdp", None), rows),
        out_specs=(rows, rows) + flat,
        check_vma=False,
    )
```

```python
import functools
import math
from typing import Any, NamedTuple

import jax
import jax.numpy as jnp
from jax import lax
from jax.experimental import pallas as pl
from jax.experimental.pallas import tpu as pltpu
from jax.sharding import PartitionSpec as P

D = 512
HEADS = 8
HEAD_DIM = 64
FF = 2048
EXP_FF = 2048
EXPERTS = 4
PATCH = 128
GROUP = 256
CAP = 160
SLOTS = EXPERTS * CAP
MESH = pl.DeviceIdType.MESH

(
    NORM1_GAIN,
    NORM1_BIAS,
    QKV1,
    QUERY1,
    VALUE1,
    PROJ1,
    PROJ1_BIAS,
    NORM2_GAIN,
    NORM2_BIAS,
    HIDDEN,
    HIDDEN_BIAS,
    OUTPUT,
    OUTPUT_BIAS,
    NORM3_GAIN,
    NORM3_BIAS,
    QKV2,
    QUERY2,
    VALUE2,
    PROJ2,
    PROJ2_BIAS,
    NORM4_GAIN,
    NORM4_BIAS,
    ROUTER,
    EXPERT_IN,
    EXPERT_IN_BIAS,
    EXPERT_OUT,
    EXPERT_OUT_BIAS,
) = NAMES = tuple(range(27))
BIG = {
    QKV1: (D, 3 * D),
    PROJ1: (D, D),
    HIDDEN: (D, FF),
    OUTPUT: (FF, D),
    QKV2: (D, 3 * D),
    PROJ2: (D, D),
    EXPERT_IN: (EXPERTS * D, EXP_FF),
    EXPERT_OUT: (EXPERTS * EXP_FF, D),
}
SMALL = tuple(name for name in NAMES if name not in BIG)
BIG_NAMES = tuple(BIG)
GAINS = (NORM1_GAIN, NORM1_BIAS, NORM2_GAIN, NORM2_BIAS, NORM3_GAIN, NORM3_BIAS, NORM4_GAIN, NORM4_BIAS)


def norm_forward(values, norm_gain, norm_shift):
    centred = values - jnp.mean(values, -1, keepdims=True)
    variance = jnp.mean(centred * centred, -1, keepdims=True)
    return centred * lax.rsqrt(variance + 1e-06) * norm_gain + norm_shift


def norm_backward(values, norm_gain, norm_shift, grad_normed):
    unused, pullback = jax.vjp(norm_forward, values, norm_gain, norm_shift)
    return pullback(grad_normed)


def gelu_backward(pre_act, grad_act):
    unused, pullback = jax.vjp(jax.nn.gelu, pre_act)
    return pullback(grad_act)[0]


def column_sums(matrix):
    return jnp.sum(matrix.astype(jnp.float32), 0)


def attention_forward(normed, qkv_weight, query_bias, value_bias, proj_weight, proj_bias):
    row_count = normed.shape[0]
    normed_low = normed.astype(jnp.bfloat16)
    packed_bias = jnp.concatenate([query_bias, jnp.zeros_like(query_bias), value_bias]).astype(
        jnp.float32
    )
    packed = jnp.dot(normed_low, qkv_weight, preferred_element_type=jnp.float32) + packed_bias
    packed = packed.astype(jnp.bfloat16).reshape(row_count // PATCH, PATCH, 3, HEADS, HEAD_DIM)
    queries = packed[:, :, 0]
    key_block = packed[:, :, 1]
    values = packed[:, :, 2]
    score_scale = 1.0 / math.sqrt(HEAD_DIM)
    scores = (
        jnp.einsum("iqhd,ikhd->ihqk", queries, key_block, preferred_element_type=jnp.float32)
        * score_scale
    )
    row_max = jnp.max(scores, -1, keepdims=True)
    exponent = jnp.exp(scores - row_max)
    row_total = jnp.sum(exponent, -1, keepdims=True)
    weights_low = (exponent / row_total).astype(jnp.bfloat16)
    logsum = row_max + jnp.log(row_total)
    mixed_heads = jnp.einsum(
        "ihqk,ikhd->iqhd", weights_low, values, preferred_element_type=jnp.float32
    )
    mixed_heads = mixed_heads.reshape(row_count, D).astype(jnp.bfloat16)
    output = jnp.dot(
        mixed_heads, proj_weight, preferred_element_type=jnp.float32
    ) + proj_bias.astype(jnp.float32)
    return (output, (normed_low, queries, key_block, values, logsum, mixed_heads))


def attention_backward(grad_output, saved_state, qkv_weight, proj_weight):
    normed_low, queries, key_block, values, logsum, mixed_heads = saved_state
    row_count = normed_low.shape[0]
    grad_low = grad_output.astype(jnp.bfloat16)
    grad_proj_weight = jnp.einsum(
        "rd,re->de", mixed_heads, grad_low, preferred_element_type=jnp.float32
    )
    grad_proj_bias = column_sums(grad_low)
    grad_mixed = jnp.einsum("re,de->rd", grad_low, proj_weight, preferred_element_type=jnp.float32)
    grad_mixed = grad_mixed.astype(jnp.bfloat16).reshape(row_count // PATCH, PATCH, HEADS, HEAD_DIM)
    score_scale = 1.0 / math.sqrt(HEAD_DIM)
    scores = (
        jnp.einsum("iqhd,ikhd->ihqk", queries, key_block, preferred_element_type=jnp.float32)
        * score_scale
    )
    weights_full = jnp.exp(scores - logsum)
    weights_low = weights_full.astype(jnp.bfloat16)
    grad_weights = jnp.einsum(
        "iqhd,ikhd->ihqk", grad_mixed, values, preferred_element_type=jnp.float32
    )
    grad_values = jnp.einsum(
        "ihqk,iqhd->ikhd", weights_low, grad_mixed, preferred_element_type=jnp.float32
    )
    inner_sum = jnp.sum(grad_weights * weights_full, -1, keepdims=True)
    grad_scores = (weights_full * (grad_weights - inner_sum)).astype(jnp.bfloat16)
    grad_queries = (
        jnp.einsum("ihqk,ikhd->iqhd", grad_scores, key_block, preferred_element_type=jnp.float32)
        * score_scale
    )
    grad_keys = (
        jnp.einsum("ihqk,iqhd->ikhd", grad_scores, queries, preferred_element_type=jnp.float32)
        * score_scale
    )
    grad_packed = (
        jnp.stack([grad_queries, grad_keys, grad_values], 2)
        .reshape(row_count, 3 * D)
        .astype(jnp.bfloat16)
    )
    grad_qkv_weight = jnp.einsum(
        "rd,re->de", normed_low, grad_packed, preferred_element_type=jnp.float32
    )
    grad_query_bias = column_sums(grad_packed[:, :D])
    grad_value_bias = column_sums(grad_packed[:, 2 * D :])
    grad_normed = jnp.einsum(
        "re,de->rd", grad_packed, qkv_weight, preferred_element_type=jnp.float32
    )
    return (
        grad_normed,
        (grad_qkv_weight, grad_query_bias, grad_value_bias, grad_proj_weight, grad_proj_bias),
    )


def feed_forward(normed, in_weight, in_bias, out_weight, out_bias):
    normed_low = normed.astype(jnp.bfloat16)
    pre_act = jnp.dot(normed_low, in_weight, preferred_element_type=jnp.float32) + in_bias.astype(
        jnp.float32
    )
    activation = jax.nn.gelu(pre_act).astype(jnp.bfloat16)
    output = jnp.dot(activation, out_weight, preferred_element_type=jnp.float32) + out_bias.astype(
        jnp.float32
    )
    return (output, (normed_low, pre_act, activation))


def feed_backward(grad_output, saved_state, in_weight, out_weight):
    normed_low, pre_act, activation = saved_state
    grad_low = grad_output.astype(jnp.bfloat16)
    grad_out_weight = jnp.einsum(
        "rf,rd->fd", activation, grad_low, preferred_element_type=jnp.float32
    )
    grad_out_bias = column_sums(grad_low)
    grad_activation = jnp.einsum(
        "rd,fd->rf", grad_low, out_weight, preferred_element_type=jnp.float32
    )
    grad_pre = gelu_backward(pre_act, grad_activation).astype(jnp.bfloat16)
    grad_in_weight = jnp.einsum(
        "rd,rf->df", normed_low, grad_pre, preferred_element_type=jnp.float32
    )
    grad_in_bias = column_sums(grad_pre)
    grad_normed = jnp.einsum("rf,df->rd", grad_pre, in_weight, preferred_element_type=jnp.float32)
    return (grad_normed, (grad_in_weight, grad_in_bias, grad_out_weight, grad_out_bias))


TILE = 512
F32 = jnp.float32
LOW = jnp.bfloat16
ROWS = 512
CHUNK = 256
PACE = 1
ITEM = 32
COUNT = len(BIG_NAMES)
A_QKV1, A_PROJ1, A_HIDDEN, A_OUTPUT, A_QKV2, A_PROJ2, A_IN, A_OUT, A_SMALL = range(COUNT + 1)
VECTORS = (
    NORM1_GAIN,
    NORM1_BIAS,
    QUERY1,
    VALUE1,
    PROJ1_BIAS,
    NORM2_GAIN,
    NORM2_BIAS,
    OUTPUT_BIAS,
    NORM3_GAIN,
    NORM3_BIAS,
    QUERY2,
    VALUE2,
    PROJ2_BIAS,
    NORM4_GAIN,
    NORM4_BIAS,
)
ROW_OF = {name: at for at, name in enumerate(VECTORS)}


def mm(left, right):
    return jnp.dot(left, right, preferred_element_type=F32)


def nt(left, right):
    return lax.dot_general(left, right, (((1,), (1,)), ((), ())), preferred_element_type=F32)


def tn(left, right):
    return lax.dot_general(left, right, (((0,), (0,)), ((), ())), preferred_element_type=F32)


def iota(shape, dimension):
    return lax.broadcasted_iota(jnp.int32, shape, dimension)


def chunks(body, rows=ROWS, init=0, size=CHUNK):
    def step(at, carry):
        return body(pl.ds(pl.multiple_of(at * size, size), size), carry)

    return lax.fori_loop(0, rows // size, step, init)


def normed(values):
    centred = values - jnp.mean(values, -1, keepdims=True)
    scale = lax.rsqrt(jnp.mean(centred * centred, -1, keepdims=True) + 1e-06)
    return centred * scale, scale


SQRT_2_PI = math.sqrt(2.0 / math.pi)


def gelu_parts(pre):
    squared = pre * pre
    bent = jnp.tanh(pre * (SQRT_2_PI + (SQRT_2_PI * 0.044715) * squared))
    return squared, bent, 0.5 + 0.5 * bent


def gelu_low(pre):
    return (pre * gelu_parts(pre)[2]).astype(LOW)


def gelu_and_slope(pre):
    squared, bent, half = gelu_parts(pre)
    active = pre * half
    slope = half + active * (1.0 - half) * (
        2.0 * SQRT_2_PI + (6.0 * SQRT_2_PI * 0.044715) * squared
    )
    return active.astype(LOW), slope


def column_sum(values):
    return jnp.sum(values.astype(F32), 0, keepdims=True)


def place():
    me = lax.axis_index("fsdp")
    return me // 8, (me // 4) % 2, (me // 2) % 2, me % 2


def device(z, y, x, core):
    return (((z * 2 + y) * 2 + x) * 2 + core,)


def partners(z, y, x, core):
    found = [device((z + step) % 4, y, x, core) for step in (1, 2, 3)]
    return found + [device(z, y, 1 - x, core), device(z, 1 - y, x, core), device(z, y, x, 1 - core)]


def greet(devices):
    barrier = pltpu.get_barrier_semaphore()
    for one in devices:
        pl.semaphore_signal(barrier, inc=1, device_id=one, device_id_type=MESH)
    pl.semaphore_wait(barrier, len(devices))


class Link:
    def __init__(self, items, send, recv):
        self.items, self.send, self.recv = items, send, recv
        self.z, self.y, self.x, self.core = place()

    def copy(self, item, message, source, target, to):
        return pltpu.make_async_remote_copy(
            src_ref=source,
            dst_ref=target,
            send_sem=self.send.at[item % self.turns, message],
            recv_sem=self.recv.at[item % self.turns, message],
            device_id=to,
            device_id_type=MESH,
        )

    def rows(self, item):
        which, first, rows = self.items[item]
        return which, pl.ds(first, rows)


class Gather(Link):
    messages = 12
    leads = (0, 2, 4, 6, 8, 10)
    turns = 10

    def __init__(self, items, shards, wholes, prepare, send, recv, local):
        super().__init__(items, send, recv)
        self.shards, self.wholes, self.prepare, self.local = shards, wholes, prepare, local
        self.ready, self.tick = set(), 0

    def block(self, item, zs, y, x, core):
        which, rows = self.rows(item)
        return self.wholes[which].at[zs, y, x, core, rows]

    def source(self, item):
        which, rows = self.rows(item)
        return self.shards[which].at[rows]

    def own(self, item):
        target = self.block(item, self.z, self.y, self.x, self.core)
        return pltpu.make_async_copy(self.source(item), target, self.local.at[item % self.turns])

    def along_z(self, item):
        z, y, x, core = self.z, self.y, self.x, self.core
        source = self.source(item)
        target = self.block(item, z, y, x, core)
        return [
            self.copy(item, step - 1, source, target, device((z + step) % 4, y, x, core))
            for step in (1, 2, 3)
        ]

    def same(self, item, message, zs, y, x, core, to):
        part = self.block(item, zs, y, x, core)
        return self.copy(item, message, part, part, to)

    def across(self, item):
        z, y, x, core = self.z, self.y, self.x, self.core
        return [
            self.same(item, 3, slice(None), y, x, core, device(z, y, 1 - x, core)),
            self.same(item, 4, slice(None), y, x, core, device(z, 1 - y, x, core)),
        ]

    def onward(self, item):
        z, y, x, core = self.z, self.y, self.x, self.core
        first = 2 * (z % 2)
        return [
            self.same(item, 5, first, y, 1 - x, core, device(z, 1 - y, x, core)),
            self.same(item, 6, first + 1, 1 - y, x, core, device(z, y, 1 - x, core)),
        ]

    def exchange(self, item):
        z, y, x, core = self.z, self.y, self.x, self.core
        mine, other = pl.ds(2 * (z % 2), 2), z + 1 - 2 * (z % 2)
        return self.same(item, 11, mine, 1 - y, 1 - x, core, device(other, y, x, core))

    def pair(self, item, which):
        z, y, x, core = self.z, self.y, self.x, self.core
        ys, xs = ((y, x), (y, 1 - x), (1 - y, x), (1 - y, 1 - x))[which]
        return self.same(item, 7 + which, slice(None), ys, xs, core, device(z, y, x, 1 - core))

    def stage(self, number, item):
        if number == 0:
            self.prepare(item)
            if item >= self.turns:
                self.sent(item - self.turns)
            self.own(item).start()
            for one in self.along_z(item):
                one.start()
        elif number == 1:
            self.own(item).wait()
            for one in self.along_z(item):
                one.wait_recv()
            for one in self.across(item):
                one.start()
            self.pair(item, 0).start()
        elif number == 2:
            for one in self.across(item):
                one.wait_recv()
            for one in self.onward(item):
                one.start()
            self.pair(item, 1).start()
            self.pair(item, 2).start()
        elif number == 3:
            for one in self.onward(item):
                one.wait_recv()
            self.exchange(item).start()
        elif number == 4:
            self.exchange(item).wait_recv()
            self.pair(item, 3).start()
        else:
            for which in range(4):
                self.pair(item, which).wait_recv()
            self.ready.add(item)

    def step(self):
        if len(self.ready) == len(self.items):
            return False
        for number in (0, 5, 4, 3, 2, 1):
            item = self.tick - self.leads[number]
            if 0 <= item < len(self.items):
                self.stage(number, item)
        self.tick += 1
        return True

    def sent(self, item):
        copies = self.along_z(item) + self.across(item) + self.onward(item) + [self.exchange(item)]
        for one in copies + [self.pair(item, which) for which in range(4)]:
            one.wait_send()

    def finish(self):
        for item in range(max(0, len(self.items) - self.turns), len(self.items)):
            self.sent(item)


class Scatter(Link):
    messages = 9
    leads = (0, 1, 3, 5, 7, 9)
    turns = 8
    buffers = 4

    def __init__(self, items, grads, places, give, send, recv, local):
        super().__init__(items, send, recv)
        self.grads, self.give, self.local = grads, give, local
        self.own, self.landing, self.pool, self.cross, self.halves, self.sides, self.ends = places
        self.tick, self.made, self.begun = 0, {}, []

    def slot(self, kind, item):
        which, first, rows = self.items[item]
        if which == A_SMALL:
            return kind[1]
        lead = (slice(None),) * (len(kind[0].shape) - 3)
        return kind[0].at[(item % kind[0].shape[0],) + lead + (pl.ds(0, rows),)]

    def load_own(self, item):
        which, rows = self.rows(item)
        source = self.grads[which].at[:, :, :, self.core, rows]
        return pltpu.make_async_copy(source, self.slot(self.own, item), self.local.at[item % 2])

    def pair(self, item):
        which, rows = self.rows(item)
        source = self.grads[which].at[:, :, :, 1 - self.core, rows]
        target = self.slot(self.landing, item)
        return self.copy(item, 0, source, target, device(self.z, self.y, self.x, 1 - self.core))

    def exchange(self, item):
        z, y, x, core = self.z, self.y, self.x, self.core
        other = z + 1 - 2 * (z % 2)
        source = self.slot(self.pool, item).at[pl.ds(2 * (other % 2), 2), 1 - y, 1 - x]
        return self.copy(item, 1, source, self.slot(self.cross, item), device(other, y, x, core))

    def half(self, item):
        z, y, x, core = self.z, self.y, self.x, self.core
        found = []
        for at, to in ((0, device(z, y, 1 - x, core)), (1, device(z, 1 - y, x, core))):
            source = self.slot(self.pool, item).at[2 * (z % 2) + at, 1 - y, 1 - x]
            found.append(self.copy(item, 2 + at, source, self.slot(self.halves, item).at[at], to))
        return found

    def side(self, item):
        z, y, x, core = self.z, self.y, self.x, self.core
        found = []
        for at, (ys, xs) in enumerate(((y, 1 - x), (1 - y, x))):
            source = self.slot(self.pool, item).at[:, ys, xs]
            target = self.slot(self.sides, item).at[at]
            found.append(self.copy(item, 4 + at, source, target, device(z, ys, xs, core)))
        return found

    def along_z(self, item):
        z, y, x, core = self.z, self.y, self.x, self.core
        found = []
        for step in (1, 2, 3):
            to = (z + step) % 4
            source = self.slot(self.pool, item).at[to, y, x]
            target = self.slot(self.ends, item).at[step - 1]
            found.append(self.copy(item, 5 + step, source, target, device(to, y, x, core)))
        return found

    def sent(self, item):
        for one in [self.exchange(item)] + self.half(item) + self.side(item) + self.along_z(item):
            one.wait_send()

    def stage(self, number, item):
        z, y, x = self.z, self.y, self.x
        pool = self.slot(self.pool, item)
        if number == 0:
            for one in self.made[item]:
                one()
            if item >= self.turns:
                self.pair(item - self.turns).wait_send()
            self.load_own(item).start()
            self.pair(item).start()
        elif number == 1:
            self.load_own(item).wait()
            self.pair(item).wait_recv()
            if item >= self.turns:
                self.sent(item - self.turns)
            own, landed = self.slot(self.own, item), self.slot(self.landing, item)

            def add(at, carry):
                spot = (at // 4, at // 2 % 2, at % 2)
                pool[spot] = own[spot] + landed[spot]
                return carry

            lax.fori_loop(0, 16, add, 0)
            self.exchange(item).start()
        elif number == 2:
            self.exchange(item).wait_recv()
            found = self.slot(self.cross, item)
            for at in range(2):
                spot = (2 * (z % 2) + at, 1 - y, 1 - x)
                pool[spot] = pool[spot] + found[at]
            for one in self.half(item):
                one.start()
        elif number == 3:
            for one in self.half(item):
                one.wait_recv()
            found = self.slot(self.halves, item)
            for at in range(2):
                spot = (2 * (z % 2) + at, y if at else 1 - y, 1 - x if at else x)
                pool[spot] = pool[spot] + found[at]
            for one in self.side(item):
                one.start()
        elif number == 4:
            for one in self.side(item):
                one.wait_recv()
            found = self.slot(self.sides, item)

            def total(at, carry):
                values = pool[at, y, x].astype(F32) + found[0, at].astype(F32)
                pool[at, y, x] = (values + found[1, at].astype(F32)).astype(pool.dtype)
                return carry

            lax.fori_loop(0, 4, total, 0)
            for one in self.along_z(item):
                one.start()
        else:
            for one in self.along_z(item):
                one.wait_recv()
            found = self.slot(self.ends, item)
            values = pool[z, y, x].astype(F32)
            for step in range(3):
                values = values + found[step].astype(F32)
            self.give(self.items[item], values)

    def step(self):
        count, began = len(self.items), len(self.begun)
        if began < count and began in self.made:
            self.begun.append(self.tick)
        elif not self.begun or self.tick > self.begun[-1] + self.leads[-1]:
            return False
        for number in reversed(range(6)):
            for item, start in enumerate(self.begun):
                if start + self.leads[number] == self.tick:
                    self.stage(number, item)
        self.tick += 1
        return True

    def finish(self):
        for item in range(max(0, len(self.items) - self.turns), len(self.items)):
            self.pair(item).wait_send()
            self.sent(item)


class Ring:
    def __init__(self, slots, semaphores):
        self.slots, self.semaphores = slots, semaphores
        self.count = slots.shape[0]
        self.under_way = [None] * self.count
        self.next = 0

    def copy(self, slot, target):
        return pltpu.make_async_copy(self.slots.at[slot], target, self.semaphores.at[slot])

    def settle(self, slot):
        if self.under_way[slot] is not None:
            self.under_way[slot].wait()
            self.under_way[slot] = None

    def settle_all(self):
        for slot in range(self.count):
            self.settle(slot)

    def put(self, values, target):
        slot, self.next = self.next, (self.next + 1) % self.count
        self.settle(slot)
        self.slots[slot] = values.astype(LOW).reshape(self.slots.shape[1:])
        copy = self.copy(slot, target)
        copy.start()
        self.under_way[slot] = copy

        def wait():
            if self.under_way[slot] is copy:
                self.settle(slot)

        return wait

    def fill(self, slot, values):
        self.slots[slot] = values.astype(LOW).reshape(self.slots.shape[1:])

    def start(self, targets):
        for slot, target in enumerate(targets):
            self.under_way[slot] = self.copy(slot, target)
            self.under_way[slot].start()


class Inputs(NamedTuple):
    tokens: Any
    cotangent: Any
    routes: Any
    priority: Any
    small: Any
    shards: Any


class Outputs(NamedTuple):
    activations: Any
    input_grad: Any
    small: Any
    grads: Any
    wholes: Any
    made: Any


class Scratch(NamedTuple):
    low: Any
    resident: Any
    small_whole: Any
    small_grad: Any
    flat: Any
    vec: Any
    vec_ff: Any
    vec_out: Any
    router: Any
    grad_vec: Any
    grad_ff: Any
    grad_out: Any
    grad_router: Any
    stream: Any
    norm: Any
    packed: Any
    heads: Any
    probs: Any
    slots: Any
    dispatched: Any
    slot_grad: Any
    weight_in: Any
    weight_out: Any
    slot_sums: Any
    grad: Any
    table: Any
    wide: Any
    thin: Any
    active: Any
    gate: Any
    ring_a: Any
    ring_b: Any
    ring_c: Any
    turn: Any
    turn_small: Any
    gather_send: Any
    gather_recv: Any
    gather_local: Any
    scatter_send: Any
    scatter_recv: Any
    scatter_local: Any
    ring_a_sem: Any
    ring_b_sem: Any
    ring_c_sem: Any
    fetch: Any
    shard_sem: Any
    deliver: Any


class Step:
    def __init__(self, plan, inputs, outputs, scratch):
        self.plan, self.i, self.o, self.s = plan, inputs, outputs, scratch
        s = scratch
        wholes = list(s.resident) + list(outputs.wholes) + [s.small_whole]
        made = list(outputs.made) + [s.small_grad]
        self.wholes, self.made = wholes, made
        self.prepared = set()
        self.pace = 1
        self.gather = Gather(
            plan.gather_items,
            list(s.low) + [inputs.small],
            wholes,
            self.prepare,
            s.gather_send,
            s.gather_recv,
            s.gather_local,
        )
        self.scatter = Scatter(
            plan.scatter_items,
            made,
            list(zip(s.turn, s.turn_small)),
            self.give,
            s.scatter_send,
            s.scatter_recv,
            s.scatter_local,
        )
        self.ring_a = Ring(s.ring_a, s.ring_a_sem)
        self.ring_b = Ring(s.ring_b, s.ring_b_sem)
        self.ring_c = Ring(s.ring_c, s.ring_c_sem)
        self.tiles_made = {}


    def prepare(self, item):
        which = self.plan.gather_items[item][0]
        if which in self.prepared or which == A_SMALL:
            return
        self.prepared.add(which)
        tiles, rows = self.plan.tiles[which], self.plan.rows[which]
        view, low = self.o.grads[which], self.s.low[which]
        self.shard(which).wait()
        for tile in range(tiles):
            for quarter in range(4):
                found = view[pl.ds(chunk_of(which, tiles, tile, quarter), rows, stride=4 * tiles), :]
                low[tile * rows : (tile + 1) * rows, 128 * quarter : 128 * quarter + 128] = found.astype(LOW)

    def shard(self, which):
        return pltpu.make_async_copy(self.i.shards[which], self.o.grads[which], self.s.shard_sem.at[which])

    def give(self, item, total):
        which, first, count = item
        if which == A_SMALL:
            self.o.small[...] = total
            return
        tiles, rows = self.plan.tiles[which], self.plan.rows[which]
        view = self.o.grads[which]
        at = first
        while at < first + count:
            tile, row = at // rows, at % rows
            take = min(rows - row, first + count - at)
            part = total[at - first : at - first + take]
            for quarter in range(4):
                start = 4 * tiles * row + chunk_of(which, tiles, tile, quarter)
                view[pl.ds(start, take, stride=4 * tiles), :] = part[:, 128 * quarter : 128 * quarter + 128]
            at += take


    def breathe(self):
        self.gather.step()
        for _ in range(self.pace):
            self.scatter.step()

    def need(self, which, rows=None):
        wanted = {
            at
            for at, (one, first, count) in enumerate(self.plan.gather_items)
            if one == which and (rows is None or first < rows)
        }
        while not wanted <= self.gather.ready:
            self.breathe()

    def finished(self, which, tile, wait):
        self.tiles_made[which, tile] = wait
        for item, (one, first, rows) in enumerate(self.plan.scatter_items):
            if item in self.scatter.made or one != which:
                continue
            wanted = [(which, tile) for tile in self.plan.made_of(which, first, rows)]
            if all(key in self.tiles_made for key in wanted):
                self.scatter.made[item] = [self.tiles_made[key] for key in wanted]


    def column_tile(self, which, tile):
        rows = self.plan.rows[which]
        return self.wholes[which][:, :, :, :, pl.ds(tile * rows, rows), :].reshape(TILE, TILE)

    def whole_columns(self, which):
        tiles = [self.column_tile(which, tile) for tile in range(self.plan.tiles[which])]
        return jnp.concatenate(tiles, 1)

    def row_tile(self, which, tile):
        return self.wholes[which][tile].reshape(TILE, TILE)

    def whole_rows(self, which):
        return self.wholes[which][...].reshape(-1, TILE)

    def fetch_in(self, tile):
        return pltpu.make_async_copy(
            self.o.wholes[0].at[:, :, :, :, pl.ds(64 * tile, 64)],
            self.s.weight_in.at[tile % 2],
            self.s.fetch.at[tile % 2, 0],
        )

    def fetch_out(self, tile):
        return pltpu.make_async_copy(
            self.o.wholes[1].at[:, tile % 2, :, :, pl.ds(128 * (tile // 2), 128)],
            self.s.weight_out.at[tile % 2],
            self.s.fetch.at[tile % 2, 1],
        )

    def row(self, name):
        at = ROW_OF[name]
        return self.s.vec[at : at + 1, :]

    def keep_row(self, name, values):
        at = ROW_OF[name]
        self.s.grad_vec[at : at + 1, :] = values


    def spread(self, first, each):
        lane, column = iota((128, TILE), 0), iota((128, TILE), 1)
        return jnp.where(lane == first + column % each, 1.0, 0.0).astype(LOW)

    def spread_router(self, expert):
        lane, column = iota((128, TILE), 0), iota((128, TILE), 1)
        return jnp.where(lane == 64 + 4 * (column % 16) + expert, 1.0, 0.0).astype(LOW)

    def unpack_small(self):
        s = self.s
        s.flat[...] = s.small_whole[...].reshape(256, 128).astype(LOW).astype(F32)
        device_row, column = iota((32, TILE), 0), iota((32, TILE), 1)
        found = [s.flat[pl.ds(row, 32, stride=8), :].astype(LOW) for row in (0, 1, 2, 5)]
        mine = device_row == column // 16
        for row in range(2):

            def vector(at, carry, row=row):
                wide = mm(found[row], self.spread(at * 16, 16))
                s.vec[pl.ds(8 * row + at, 1), :] = jnp.sum(jnp.where(mine, wide, 0.0), 0, keepdims=True)
                return carry

            lax.fori_loop(0, 8, vector, 0)
        router = jnp.zeros((128, TILE), F32)
        for expert in range(EXPERTS):
            wide = jnp.where(mine, mm(found[2], self.spread_router(expert)), 0.0)
            router = jnp.where(iota((128, TILE), 0) == expert, jnp.sum(wide, 0, keepdims=True), router)
        s.router[...] = router.astype(LOW)
        wide = mm(found[2], self.spread(0, 64))
        for tile in range(FF // TILE):
            part = jnp.where(device_row == 8 * tile + column // 64, wide, 0.0)
            s.vec_ff[0:1, tile * TILE : (tile + 1) * TILE] = jnp.sum(part, 0, keepdims=True)
        wide = mm(found[3], self.spread(0, 64))
        for expert in range(EXPERTS):
            part = jnp.where(device_row == 8 * expert + column // 64, wide, 0.0)
            s.vec_out[expert : expert + 1, :] = jnp.sum(part, 0, keepdims=True)
            for at in range(16):
                chunk = chunk_of(A_IN, 4, at // 4, at % 4)
                row = 8 * (8 * expert + chunk // 2) + 3 + chunk % 2
                s.vec_ff[1 + expert : 2 + expert, 128 * at : 128 * at + 128] = s.flat[row : row + 1, :]

    def pack_vectors(self, row):
        s = self.s
        mine = iota((32, TILE), 0) == iota((32, TILE), 1) // 16

        def vector(at, carry):
            values = jnp.where(mine, s.grad_vec[pl.ds(8 * row + at, 1), :], 0.0)
            return carry + self.pack(values, self.spread(at * 16, 16))

        s.flat[pl.ds(row, 32, stride=8), :] = lax.fori_loop(0, 8, vector, jnp.zeros((32, 128), F32))

    def pack(self, values, one_hot):
        high = values.astype(LOW)
        rest = (values - high.astype(F32)).astype(LOW)
        return nt(high, one_hot) + nt(rest, one_hot)

    def pack_early(self):
        s = self.s
        device_row, column = iota((32, TILE), 0), iota((32, TILE), 1)
        mine = device_row == column // 16
        s.flat[...] = jnp.zeros((256, 128), F32)
        s.grad_vec[len(VECTORS) :, :] = jnp.zeros((16 - len(VECTORS), TILE), F32)
        self.pack_vectors(1)
        found = jnp.zeros((32, 128), F32)
        for expert in range(EXPERTS):
            values = jnp.where(mine, s.grad_router[expert : expert + 1, :], 0.0)
            found += self.pack(values, self.spread_router(expert))
        total = jnp.zeros((32, TILE), F32)
        for tile in range(FF // TILE):
            own = device_row == 8 * tile + column // 64
            total += jnp.where(own, s.grad_ff[0:1, tile * TILE : (tile + 1) * TILE], 0.0)
        s.flat[pl.ds(2, 32, stride=8), :] = found + self.pack(total, self.spread(0, 64))
        total = jnp.zeros((32, TILE), F32)
        for expert in range(EXPERTS):
            own = device_row == 8 * expert + column // 64
            total += jnp.where(own, s.grad_out[expert : expert + 1, :], 0.0)
        s.flat[pl.ds(5, 32, stride=8), :] = self.pack(total, self.spread(0, 64))
        for expert in range(EXPERTS):
            for at in range(16):
                chunk = chunk_of(A_IN, 4, at // 4, at % 4)
                row = 8 * (8 * expert + chunk // 2) + 3 + chunk % 2
                s.flat[row : row + 1, :] = s.grad_ff[1 + expert : 2 + expert, 128 * at : 128 * at + 128]

    def pack_late(self):
        s = self.s
        self.pack_vectors(0)
        s.small_grad[...] = s.flat[...].reshape(4, 2, 2, 2, 8, 128)
        self.finished(A_SMALL, 0, lambda: None)


    def norm(self, source, target, gain, bias):
        gain, bias = self.row(gain), self.row(bias)

        def body(rows, carry):
            target[rows] = (normed(source[rows].astype(F32))[0] * gain + bias).astype(LOW)
            return carry

        chunks(body)

    def norm_back(self, source, back, gain, bias):
        wide, grad = self.row(gain), self.s.grad

        def body(rows, carry):
            to_gain, to_bias = carry
            unit, scale = normed(source[rows].astype(F32))
            found = back[rows]
            to_gain = to_gain + column_sum(found * unit)
            to_bias = to_bias + column_sum(found)
            found = found * wide
            mean = jnp.mean(found, -1, keepdims=True)
            along = jnp.mean(found * unit, -1, keepdims=True)
            grad[rows] = grad[rows] + scale * (found - mean - unit * along)
            return to_gain, to_bias

        zero = jnp.zeros((1, D), F32)
        to_gain, to_bias = chunks(body, init=(zero, zero))
        self.keep_row(gain, to_gain)
        self.keep_row(bias, to_bias)


    def masks(self):
        first = iota((PATCH, 128), 1) < HEAD_DIM
        return first, jnp.where(first, 1.0, 0.0).astype(LOW), jnp.where(first, 0.0, 1.0).astype(LOW)

    def scores(self, packed, rows, at, masks):
        query = packed[rows, 128 * at : 128 * at + 128]
        keys = packed[rows, D + 128 * at : D + 128 * at + 128]
        values = packed[rows, 2 * D + 128 * at : 2 * D + 128 * at + 128]
        query = jnp.concatenate([query * masks[1], query * masks[2]], 0)
        return query, keys, values, nt(query, keys) * (1.0 / math.sqrt(HEAD_DIM))

    def exponent(self, scores):
        found = jnp.exp(scores - jnp.max(scores, -1, keepdims=True))
        return found, jnp.sum(found, -1, keepdims=True)

    def pairs(self, first, images):
        for image in range(images):
            rows = pl.ds(pl.multiple_of((first + image) * PATCH, PATCH), PATCH)
            for at in range(HEADS // 2):
                yield rows, at

    def attention(self, block, source, target, names):
        s = self.s
        gain, bias, query, value, proj = names
        qkv_at, proj_at = (A_QKV1, A_PROJ1) if block == 0 else (A_QKV2, A_PROJ2)
        low, packed, heads = s.norm.at[0 if block == 0 else 2], s.packed.at[block], s.heads.at[block]
        self.norm(source, low, gain, bias)
        self.breathe()
        self.need(qkv_at)
        for part in range(3):
            found = mm(low[...], self.column_tile(qkv_at, part))
            if part != 1:
                found = found + self.row(query if part == 0 else value)
            packed[:, part * D : (part + 1) * D] = found.astype(LOW)
        self.breathe()

        def images(number, carry):
            masks = self.masks()
            work = list(self.pairs(2 * number, 2))
            parts = [self.scores(packed, rows, at, masks) for rows, at in work]
            parts = [(values, *self.exponent(scores)) for query, keys, values, scores in parts]
            for (rows, at), (values, weights, total) in zip(work, parts):
                found = mm((weights / total).astype(LOW), values)
                found = jnp.where(masks[0], found[:PATCH], found[PATCH:])
                heads[rows, 128 * at : 128 * at + 128] = found.astype(LOW)
            return carry

        lax.fori_loop(0, 2, images, 0)
        self.breathe()
        self.need(proj_at)
        found = mm(heads[...], self.column_tile(proj_at, 0)) + self.row(proj)
        target[...] = source[...].astype(F32) + found

    def low_and_sums(self, source, target):
        def body(rows, carry):
            found = source[rows].astype(LOW)
            target[rows] = found
            return carry + column_sum(found)

        return chunks(body, init=jnp.zeros((1, D), F32))

    def attention_back(self, block, source, names):
        s = self.s
        gain, bias, query_bias, value_bias, proj_bias = names
        qkv_at, proj_at = (A_QKV1, A_PROJ1) if block == 0 else (A_QKV2, A_PROJ2)
        low, packed, heads = s.norm.at[0 if block == 0 else 2], s.packed.at[block], s.heads.at[block]
        self.keep_row(proj_bias, self.low_and_sums(s.grad, s.thin))
        target = self.made[proj_at]
        self.finished(proj_at, 0, self.ring_a.put(tn(heads[...], s.thin[...]), target))
        s.gate[:, :D] = nt(s.thin[...], self.column_tile(proj_at, 0)).astype(LOW)
        self.breathe()
        scale = 1.0 / math.sqrt(HEAD_DIM)

        def image(number, carry):
            masks = self.masks()
            work = list(self.pairs(number, 1))
            parts = []
            for rows, at in work:
                query, keys, values, scores = self.scores(packed, rows, at, masks)
                found = s.gate[rows, 128 * at : 128 * at + 128]
                found = jnp.concatenate([found * masks[1], found * masks[2]], 0)
                parts.append((query, keys, found, scores, nt(found, values)))
            parts = [(query, keys, found, *self.exponent(scores), back) for query, keys, found, scores, back in parts]
            parts = [(query, keys, found, up / total, back) for query, keys, found, up, total, back in parts]
            inner = [jnp.sum(back * weights, -1, keepdims=True) for query, keys, found, weights, back in parts]
            parts = [
                (query, keys, tn(weights.astype(LOW), found), (weights * (back - one)).astype(LOW))
                for (query, keys, found, weights, back), one in zip(parts, inner)
            ]
            for (rows, at), (query, keys, to_values, to_scores) in zip(work, parts):
                to_query = mm(to_scores, keys) * scale
                to_query = jnp.where(masks[0], to_query[:PATCH], to_query[PATCH:])
                to_keys = tn(to_scores, query) * scale
                for part, one in enumerate((to_query, to_keys, to_values)):
                    s.active[rows, part * D + 128 * at : part * D + 128 * at + 128] = one.astype(LOW)
            return carry

        lax.fori_loop(0, 2, image, 0)
        self.breathe()
        lax.fori_loop(2, 4, image, 0)
        self.breathe()
        found = s.active[:, : 3 * D]
        self.keep_row(query_bias, column_sum(found[:, :D]))
        self.keep_row(value_bias, column_sum(found[:, 2 * D :]))
        self.ring_a.settle_all()
        for part in range(3):
            self.ring_a.fill(part, tn(low[...], found[:, part * D : (part + 1) * D]))
        s.wide[...] = nt(found, self.whole_columns(qkv_at))
        self.ring_a.start([self.made[qkv_at].at[:, :, :, :, pl.ds(16 * part, 16)] for part in range(3)])
        for part in range(3):
            self.finished(qkv_at, part, self.ring_a.settle_all)
        self.breathe()
        self.norm_back(source, s.wide, gain, bias)
        self.breathe()


    def feed(self, source, target):
        s = self.s
        low = s.norm.at[1]
        self.norm(source, low, NORM2_GAIN, NORM2_BIAS)
        self.breathe()
        self.need(A_HIDDEN)
        self.need(A_OUTPUT)
        for tile in range(FF // TILE):
            columns = slice(tile * TILE, (tile + 1) * TILE)
            pre = mm(low[...], self.column_tile(A_HIDDEN, tile)) + s.vec_ff[0:1, columns]
            s.active[:, columns] = gelu_low(pre)
        target[...] = source[...] + self.row(OUTPUT_BIAS) + mm(s.active[...], self.whole_rows(A_OUTPUT))
        self.breathe()

    def feed_back(self, source):
        s = self.s
        low = s.norm.at[1]
        self.keep_row(OUTPUT_BIAS, self.low_and_sums(s.grad, s.thin))
        for tile in range(FF // TILE):
            columns = slice(tile * TILE, (tile + 1) * TILE)
            pre = mm(low[...], self.column_tile(A_HIDDEN, tile)) + s.vec_ff[0:1, columns]
            active, slope = gelu_and_slope(pre)
            s.active[:, columns] = active
            found = (slope * nt(s.thin[...], self.row_tile(A_OUTPUT, tile))).astype(LOW)
            s.gate[:, columns] = found
            s.grad_ff[0:1, columns] = column_sum(found)
        self.breathe()
        self.ring_b.settle_all()
        for tile in range(FF // TILE):
            found = s.active[:, tile * TILE : (tile + 1) * TILE]
            self.ring_b.fill(tile, tn(found, s.thin[...]))
        self.ring_b.start([self.made[A_OUTPUT].at[tile] for tile in range(FF // TILE)])
        for tile in range(FF // TILE):
            self.finished(A_OUTPUT, tile, self.ring_b.settle_all)
        self.breathe()
        self.ring_a.settle_all()
        for tile in range(FF // TILE):
            found = s.gate[:, tile * TILE : (tile + 1) * TILE]
            self.ring_a.fill(tile, tn(low[...], found))
        s.wide[...] = nt(s.gate[...], self.whole_columns(A_HIDDEN))
        self.ring_a.start([self.made[A_HIDDEN].at[:, :, :, :, pl.ds(16 * tile, 16)] for tile in range(4)])
        for tile in range(FF // TILE):
            self.finished(A_HIDDEN, tile, self.ring_a.settle_all)
        self.breathe()
        self.norm_back(source, s.wide, NORM2_GAIN, NORM2_BIAS)
        self.breathe()


    def route(self):
        s = self.s
        lane = iota((ROWS, 128), 1)
        logits = jnp.where(lane < EXPERTS, nt(s.norm[3], s.router[...]), -1e30)
        found = jnp.exp(logits - jnp.max(logits, -1, keepdims=True))
        s.probs[...] = found / jnp.sum(found, -1, keepdims=True)
        same = iota((GROUP, GROUP), 0) == iota((GROUP, GROUP), 1)

        def upright(row):
            return jnp.sum(jnp.where(same, row, 0.0), 1, keepdims=True)

        lane = iota((GROUP, 128), 1)
        for group in range(ROWS // GROUP):
            rows = slice(group * GROUP, (group + 1) * GROUP)
            first, second = (
                jnp.concatenate([self.i.routes[2 * group + image, at : at + 1, :] for image in range(2)], 1)
                .astype(F32)
                for at in range(2)
            )
            rank = self.i.priority[group : group + 1, :].astype(F32)
            first_up, second_up, rank_up = upright(first), upright(second), upright(rank)
            before = jnp.where(rank_up < rank, 1.0, 0.0)
            place_first = jnp.sum(jnp.where(first_up == first, before, 0.0), 0, keepdims=True)
            place_second = jnp.sum(
                jnp.where(second_up == second, before, 0.0) + jnp.where(first_up == second, 1.0, 0.0),
                0,
                keepdims=True,
            )
            kept = []
            for at, (expert, spot) in enumerate(((first, place_first), (second, place_second))):
                slot = jnp.where(spot < CAP, expert * CAP + spot, -1.0)
                s.slots[2 * group + at : 2 * group + at + 1, :] = slot
                kept.append(upright(slot))
            probs = s.probs[rows]
            gates = [
                jnp.sum(jnp.where(lane == one.astype(jnp.int32), probs, 0.0), -1, keepdims=True)
                for one in (first_up, second_up)
            ]
            columns = [first_up, second_up] + gates + kept
            table = jnp.zeros((GROUP, 128), F32)
            for at, one in enumerate(columns):
                table = jnp.where(lane == at, one, table)
            s.table[rows, :] = table
            slots = pl.ds(group * CAP, CAP)
            given = self.i.cotangent[rows].astype(F32)
            for at, gate in enumerate(gates):
                s.thin[at * GROUP : (at + 1) * GROUP, :] = (gate * given).astype(LOW)
            for expert in range(EXPERTS):
                picks = self.picks(group, expert)
                s.dispatched[expert, slots, :] = mm(picks[0] + picks[1], s.norm[3, rows, :]).astype(LOW)
                s.slot_grad[expert, slots, :] = mm(jnp.concatenate(picks, 1), s.thin[...]).astype(LOW)

    def picks(self, group, expert):
        slot = (iota((CAP, GROUP), 0) + expert * CAP).astype(F32)
        return [
            jnp.where(slot == self.s.slots[2 * group + at : 2 * group + at + 1, :], 1.0, 0.0).astype(LOW)
            for at in range(2)
        ]

    def picks_up(self, group):
        slot = iota((GROUP, SLOTS), 1).astype(F32)
        rows = slice(group * GROUP, (group + 1) * GROUP)
        return [
            jnp.where(slot == self.s.table[rows, 4 + at : 5 + at], 1.0, 0.0).astype(LOW) for at in range(2)
        ]

    def experts_first(self, tiles):
        s = self.s
        for tile in tiles:
            self.need(A_IN, 64 * (tile + 1))
            self.fetch_in(tile).start()
            self.ring_c.settle_all()
            self.fetch_in(tile).wait()
            for expert in range(EXPERTS):
                weight = s.weight_in[tile % 2, expert].reshape(TILE, TILE)
                bias = s.vec_ff[1 + expert : 2 + expert, tile * TILE : (tile + 1) * TILE]
                hidden = gelu_low(mm(s.dispatched[expert], weight) + bias)
                self.ring_c.fill(expert, tn(hidden, s.slot_grad[expert]))
            half = pl.ds(128 * (tile // 2), 128)
            self.ring_c.start([self.made[A_OUT].at[expert, tile % 2, :, :, half] for expert in range(EXPERTS)])
            self.finished(A_OUT, tile, self.ring_c.settle_all)
            self.breathe()

    def experts_then(self, tiles):
        s = self.s
        self.need(A_OUT, 64 * tiles[-1] + 64)
        self.fetch_in(tiles[0]).start()
        self.fetch_out(tiles[0]).start()
        for tile in tiles:
            if tile + 1 in tiles:
                self.fetch_in(tile + 1).start()
                self.fetch_out(tile + 1).start()
            self.fetch_in(tile).wait()
            self.fetch_out(tile).wait()
            self.ring_b.settle_all()
            columns = slice(tile * TILE, (tile + 1) * TILE)
            for expert in range(EXPERTS):
                rows, given = s.dispatched[expert], s.slot_grad[expert]
                to_hidden = s.weight_in[tile % 2, expert].reshape(TILE, TILE)
                to_out = s.weight_out[tile % 2, expert].reshape(TILE, TILE)
                pre = mm(rows, to_hidden) + s.vec_ff[1 + expert : 2 + expert, columns]
                active, slope = gelu_and_slope(pre)
                found = (slope * nt(given, to_out)).astype(LOW)
                s.grad_ff[1 + expert : 2 + expert, columns] = column_sum(found)
                out, back = mm(active, to_out), nt(found, to_hidden)
                self.ring_b.fill(expert, tn(rows, found))
                if tile == 0:
                    s.slot_sums[0, expert] = out + s.vec_out[expert : expert + 1, :]
                    s.slot_sums[1, expert] = back
                else:
                    s.slot_sums[0, expert] = s.slot_sums[0, expert] + out
                    s.slot_sums[1, expert] = s.slot_sums[1, expert] + back
                if expert == 1:
                    self.breathe()
            self.ring_b.start(
                [self.made[A_IN].at[expert, :, :, :, pl.ds(64 * tile, 64)] for expert in range(EXPERTS)]
            )
            self.finished(A_IN, tile, self.ring_b.settle_all)
            self.breathe()

    def experts_end(self):
        s = self.s
        for expert in range(EXPERTS):
            s.grad_out[expert : expert + 1, :] = column_sum(s.slot_grad[expert])
            s.dispatched[expert] = s.slot_sums[0, expert].astype(LOW)
            s.slot_grad[expert] = s.slot_sums[1, expert].astype(LOW)

    def combine(self):
        s = self.s
        lane = iota((GROUP, 128), 1)
        for group in range(ROWS // GROUP):
            rows = slice(group * GROUP, (group + 1) * GROUP)
            slots = pl.ds(group * CAP, CAP)
            picks = self.picks_up(group)
            out = s.dispatched[:, slots, :].reshape(SLOTS, D)
            picked = [mm(pick, out) for pick in picks]
            gates = [s.table[rows, 2 + at : 3 + at] for at in range(2)]
            given = self.i.cotangent[rows].astype(F32)
            found = s.stream[2, rows, :] + gates[0] * picked[0] + gates[1] * picked[1]
            s.thin[rows, :] = found.astype(LOW)
            probs = s.probs[rows]
            to_probs = jnp.zeros((GROUP, 128), F32)
            for at in range(2):
                to_gate = jnp.sum(given * picked[at], -1, keepdims=True)
                expert = s.table[rows, at : at + 1].astype(jnp.int32)
                to_probs = to_probs + jnp.where(lane == expert, to_gate, 0.0)
            inner = jnp.sum(to_probs * probs, -1, keepdims=True)
            to_logits = (probs * (to_probs - inner)).astype(LOW)
            s.gate[rows, :128] = to_logits
            back = mm(picks[0] + picks[1], s.slot_grad[:, slots, :].reshape(SLOTS, D))
            s.wide[rows, :] = back + mm(to_logits, s.router[...])
            s.grad[rows, :] = given
        s.grad_router[...] = tn(s.gate[:, :128], s.norm[3])[:8]
        copy = pltpu.make_async_copy(s.thin, self.o.activations, s.deliver.at[0])
        copy.start()
        self.breathe()
        self.norm_back(s.stream.at[2], s.wide, NORM4_GAIN, NORM4_BIAS)
        copy.wait()
        self.breathe()

    def run(self):
        s = self.s
        for which in range(COUNT):
            self.shard(which).start()
        greet(partners(*place()))
        self.need(A_SMALL)
        self.unpack_small()
        tokens, stream = self.i.tokens, s.stream
        first = (NORM1_GAIN, NORM1_BIAS, QUERY1, VALUE1, PROJ1_BIAS)
        second = (NORM3_GAIN, NORM3_BIAS, QUERY2, VALUE2, PROJ2_BIAS)
        self.attention(0, tokens, stream.at[0], first)
        self.breathe()
        self.feed(stream.at[0], stream.at[1])
        self.attention(1, stream.at[1], stream.at[2], second)
        self.breathe()
        self.norm(stream.at[2], s.norm.at[3], NORM4_GAIN, NORM4_BIAS)
        self.breathe()
        self.route()
        for half in ((0, 1), (2, 3)):
            self.experts_first(half)
            self.experts_then(half)
        self.experts_end()
        self.pace = PACE
        self.combine()
        self.attention_back(1, stream.at[1], second)
        self.feed_back(stream.at[0])
        self.pack_early()
        self.breathe()
        self.attention_back(0, tokens, first)
        s.thin[...] = s.grad[...].astype(LOW)
        copy = pltpu.make_async_copy(s.thin, self.o.input_grad, s.deliver.at[1])
        copy.start()
        self.pack_late()
        while self.scatter.step():
            pass
        self.gather.finish()
        self.scatter.finish()
        for ring in (self.ring_a, self.ring_b, self.ring_c):
            ring.settle_all()
        copy.wait()


def chunk_of(which, tiles, tile, quarter):
    if which == A_IN:
        return 8 * (tile % 2) + 2 * quarter + tile // 2
    return 4 * tile + quarter


class Plan:
    def __init__(self):
        self.tiles = [BIG[name][1] // TILE for name in BIG_NAMES] + [1]
        self.rows = [BIG[name][0] // 32 for name in BIG_NAMES] + [8]
        self.height = [tiles * rows for tiles, rows in zip(self.tiles, self.rows)]
        self.gather_items = [(A_SMALL, 0, 8)]
        for which, step in (
            (A_QKV1, 16),
            (A_PROJ1, 16),
            (A_HIDDEN, 32),
            (A_OUTPUT, 32),
            (A_QKV2, 16),
            (A_PROJ2, 16),
        ):
            self.gather_items += self.parts(which, step)
        for half in (0, 128):
            for which in (A_IN, A_OUT):
                self.gather_items += [(which, first, 32) for first in range(half, half + 128, 32)]
        self.scatter_items = []
        for half in (0, 128):
            for which in (A_OUT, A_IN):
                self.scatter_items += [(which, first, ITEM) for first in range(half, half + 128, ITEM)]
        for which, step in (
            (A_PROJ2, 16),
            (A_QKV2, 16),
            (A_OUTPUT, ITEM),
            (A_HIDDEN, ITEM),
            (A_PROJ1, 16),
            (A_QKV1, 16),
            (A_SMALL, 8),
        ):
            self.scatter_items += self.parts(which, step)

    def parts(self, which, step):
        return [(which, first, step) for first in range(0, self.height[which], step)]

    def made_of(self, which, first, rows):
        if which == A_SMALL:
            return [0]
        if which == A_OUT:
            return [0, 1] if first < 128 else [2, 3]
        if which == A_IN:
            return [first // 64]
        if which == A_OUTPUT:
            return list(range(4))
        return sorted({row // self.rows[which] for row in range(first, first + rows)})


def mega_kernel(plan, trees, *refs):
    parts, at = [], 0
    for tree in trees:
        parts.append(jax.tree.unflatten(tree, refs[at : at + tree.num_leaves]))
        at += tree.num_leaves
    Step(plan, *parts).run()


def mega(tokens, cotangent, routes, priority, small, shards):
    plan = Plan()
    whole = [(4, 2, 2, 2, height, TILE) for height in plan.height[:COUNT]]
    vmem = pltpu.VMEM
    inputs = Inputs(tokens, cotangent, routes, priority, small, shards)
    outputs = Outputs(
        activations=jax.ShapeDtypeStruct((ROWS, D), LOW),
        input_grad=jax.ShapeDtypeStruct((ROWS, D), LOW),
        small=jax.ShapeDtypeStruct((8, 128), F32),
        grads=[jax.ShapeDtypeStruct(one.shape, F32) for one in shards],
        wholes=[jax.ShapeDtypeStruct(whole[which], LOW) for which in (A_IN, A_OUT)],
        made=[jax.ShapeDtypeStruct(shape, LOW) for shape in whole],
    )
    here = pl.BlockSpec(memory_space=pltpu.VMEM)
    anywhere = pl.BlockSpec(memory_space=pl.ANY)
    in_specs = Inputs(here, here, here, here, here, [anywhere] * COUNT)
    out_specs = Outputs(anywhere, anywhere, here, [here] * COUNT, [anywhere] * 2, [anywhere] * COUNT)

    leads = ((4, 2, 2), (4, 2, 2), (4, 2, 2), (2,), (2,), (2, 4), (3,))

    def semaphores(link):
        return pltpu.SemaphoreType.DMA((link.turns, link.messages))

    dma = pltpu.SemaphoreType.DMA
    scratch = Scratch(
        low=[vmem((height, TILE), LOW) for height in plan.height[:COUNT]],
        resident=[vmem(whole[which], LOW) for which in range(6)],
        small_whole=vmem((4, 2, 2, 2, 8, 128), F32),
        small_grad=vmem((4, 2, 2, 2, 8, 128), F32),
        flat=vmem((256, 128), F32),
        vec=vmem((16, D), F32),
        vec_ff=vmem((8, FF), F32),
        vec_out=vmem((8, D), F32),
        router=vmem((128, D), LOW),
        grad_vec=vmem((16, D), F32),
        grad_ff=vmem((8, FF), F32),
        grad_out=vmem((8, D), F32),
        grad_router=vmem((8, D), F32),
        stream=vmem((3, ROWS, D), F32),
        norm=vmem((4, ROWS, D), LOW),
        packed=vmem((2, ROWS, 3 * D), LOW),
        heads=vmem((2, ROWS, D), LOW),
        probs=vmem((ROWS, 128), F32),
        slots=vmem((8, GROUP), F32),
        dispatched=vmem((EXPERTS, 2 * CAP, D), LOW),
        slot_grad=vmem((EXPERTS, 2 * CAP, D), LOW),
        weight_in=vmem((2, 4, 2, 2, 2, 64, TILE), LOW),
        weight_out=vmem((2, 4, 2, 2, 128, TILE), LOW),
        slot_sums=vmem((2, EXPERTS, 2 * CAP, D), F32),
        grad=vmem((ROWS, D), F32),
        table=vmem((ROWS, 128), F32),
        wide=vmem((ROWS, D), F32),
        thin=vmem((ROWS, D), LOW),
        active=vmem((ROWS, FF), LOW),
        gate=vmem((ROWS, FF), LOW),
        ring_a=vmem((4, 4, 2, 2, 2, 16, TILE), LOW),
        ring_b=vmem((4, 2, 2, 2, 64, TILE), LOW),
        ring_c=vmem((4, 2, 2, 128, TILE), LOW),
        turn=[
            vmem((count,) + lead + (ITEM, TILE), LOW)
            for count, lead in zip((2, 2, Scatter.turns) + (Scatter.buffers,) * 4, leads)
        ],
        turn_small=[vmem(lead + (8, 128), F32) for lead in leads],
        gather_send=semaphores(Gather),
        gather_recv=semaphores(Gather),
        gather_local=dma((Gather.turns,)),
        scatter_send=semaphores(Scatter),
        scatter_recv=semaphores(Scatter),
        scatter_local=dma((2,)),
        ring_a_sem=dma((4,)),
        ring_b_sem=dma((4,)),
        ring_c_sem=dma((4,)),
        fetch=dma((2, 2)),
        shard_sem=dma((COUNT,)),
        deliver=dma((2,)),
    )
    operands, in_tree = jax.tree.flatten(inputs)
    out_shapes, out_tree = jax.tree.flatten(outputs)
    scratch_shapes, scratch_tree = jax.tree.flatten(scratch)
    found = pl.pallas_call(
        functools.partial(mega_kernel, plan, (in_tree, out_tree, scratch_tree)),
        out_shape=out_shapes,
        in_specs=jax.tree.leaves(in_specs),
        out_specs=jax.tree.leaves(out_specs),
        scratch_shapes=scratch_shapes,
        compiler_params=pltpu.CompilerParams(
            collective_id=0, has_side_effects=True, vmem_limit_bytes=64 * 1024 * 1024
        ),
    )(*operands)
    return jax.tree.unflatten(out_tree, found)


def join_small(shards):
    def zeros(count):
        return jnp.zeros((count,), F32)

    parts = [shards[name] for name in VECTORS] + [zeros(16), shards[HIDDEN_BIAS], shards[ROUTER]]
    parts += [shards[EXPERT_IN_BIAS], shards[EXPERT_OUT_BIAS], zeros(320)]
    return jnp.concatenate(parts).reshape(8, 128)


SMALL_PARTS = tuple((name, at // 8, at % 8 * 16, 16) for at, name in enumerate(VECTORS)) + (
    (HIDDEN_BIAS, 2, 0, 64),
    (ROUTER, 2, 64, 64),
    (EXPERT_IN_BIAS, 3, 0, 256),
    (EXPERT_OUT_BIAS, 5, 0, 64),
)


def deliver_kernel(count, *refs):
    small, sources = refs[0], refs[1 : 1 + count]
    targets, parts = refs[1 + count : 1 + 2 * count], refs[1 + 2 * count :]
    for source, target in zip(sources, targets):

        def body(rows, carry, source=source, target=target):
            target[rows] = source[rows]
            return carry

        chunks(body, source.shape[0], size=64)
    for part, (name, row, lane, length) in zip(parts, SMALL_PARTS):
        for at in range(0, length, 128):
            step = min(128, length)
            part[:, at : at + step] = small[row + at // 128 : row + at // 128 + 1, lane : lane + step]


def deliver(small, arrays):
    here = pl.BlockSpec(memory_space=pltpu.VMEM)
    count = len(arrays)
    shapes = [jax.ShapeDtypeStruct(one.shape, one.dtype) for one in arrays]
    shapes += [jax.ShapeDtypeStruct((1, length), F32) for name, row, lane, length in SMALL_PARTS]
    found = pl.pallas_call(
        functools.partial(deliver_kernel, count),
        out_shape=shapes,
        in_specs=[here] * (1 + count),
        out_specs=[here] * len(shapes),
        compiler_params=pltpu.CompilerParams(vmem_limit_bytes=60 * 1024 * 1024),
    )(small, *arrays)
    parts = {entry[0]: part.reshape(-1) for entry, part in zip(SMALL_PARTS, found[count:])}
    return found[:count], parts


def on_slice(tokens, *rest):
    shards = dict(zip(NAMES, rest[: len(NAMES)]))
    routes, priority, cotangent = rest[len(NAMES) :]
    found = mega(
        tokens.reshape(ROWS, D),
        cotangent.reshape(ROWS, D),
        routes.transpose(0, 2, 1),
        priority,
        join_small(shards),
        [shards[name].reshape(-1, 128) for name in BIG_NAMES],
    )
    arrays, mine = deliver(found.small, [found.activations, found.input_grad] + list(found.grads))
    mine.update((name, one.reshape(-1)) for name, one in zip(BIG_NAMES, arrays[2:]))
    outs = tuple(one.reshape(tokens.shape) for one in arrays[:2])
    return outs + tuple(mine[name] for name in NAMES)


def routed_forward(normed, weights, routes, priority):
    groups = priority.shape[0]
    normed_low = normed.astype(jnp.bfloat16)
    logits = jnp.dot(normed_low, weights[ROUTER], preferred_element_type=jnp.float32)
    row_max = jnp.max(logits, -1, keepdims=True)
    exponent = jnp.exp(logits - row_max)
    probs_all = exponent / jnp.sum(exponent, -1, keepdims=True)
    expert_ids = jnp.arange(EXPERTS, dtype=jnp.int32)
    flat_routes = routes.reshape(-1, 2)
    hots = [(flat_routes[:, k : k + 1] == expert_ids).astype(jnp.float32) for k in range(2)]
    gates = [jnp.sum(probs_all * hot, -1, keepdims=True) for hot in hots]
    first, second = routes[:, :, 0], routes[:, :, 1]
    before = priority[:, None, :] < priority[:, :, None]
    place_first = jnp.sum(before & (first[:, None, :] == first[:, :, None]), -1)
    place_second = jnp.sum(before & (second[:, None, :] == second[:, :, None]), -1)
    place_second = place_second + jnp.sum(first[:, None, :] == second[:, :, None], -1)
    slot_ids = jnp.arange(SLOTS, dtype=jnp.int32)
    picks = [
        ((which * CAP + at)[:, None, :] == slot_ids[None, :, None]) & (at < CAP)[:, None, :]
        for which, at in ((first, place_first), (second, place_second))
    ]
    picks = [pick.astype(jnp.bfloat16) for pick in picks]
    grouped = normed_low.reshape(groups, GROUP, D)
    dispatched = jnp.einsum(
        "gst,gtd->gsd", picks[0] + picks[1], grouped, preferred_element_type=jnp.float32
    ).astype(jnp.bfloat16)
    dispatched = by_expert(dispatched)
    pre_act = jnp.einsum(
        "ecd,edf->ecf", dispatched, weights[EXPERT_IN], preferred_element_type=jnp.float32
    )
    pre_act = pre_act + weights[EXPERT_IN_BIAS].astype(jnp.float32)[:, None, :]
    hidden = jax.nn.gelu(pre_act).astype(jnp.bfloat16)
    expert_out = jnp.einsum(
        "ecf,efd->ecd", hidden, weights[EXPERT_OUT], preferred_element_type=jnp.float32
    )
    expert_out = expert_out + weights[EXPERT_OUT_BIAS].astype(jnp.float32)[:, None, :]
    expert_low = by_group(expert_out.astype(jnp.bfloat16), groups)
    picked = [
        jnp.einsum("gst,gsd->gtd", pick, expert_low, preferred_element_type=jnp.float32).reshape(-1, D)
        for pick in picks
    ]
    output = gates[0] * picked[0] + gates[1] * picked[1]
    return output, (normed_low, probs_all, hots, gates, picks, dispatched, pre_act, hidden, picked)


def by_expert(slots):
    groups, width = slots.shape[0], slots.shape[2]
    slots = slots.reshape(groups, EXPERTS, CAP, width).transpose(1, 0, 2, 3)
    return slots.reshape(EXPERTS, groups * CAP, width)


def by_group(slots, groups):
    width = slots.shape[2]
    slots = slots.reshape(EXPERTS, groups, CAP, width).transpose(1, 0, 2, 3)
    return slots.reshape(groups, SLOTS, width)


def routed_backward(grad_output, saved_state, weights):
    normed_low, probs_all, hots, gates, picks, dispatched, pre_act, hidden, picked = saved_state
    groups = picks[0].shape[0]
    grad_gates = [jnp.sum(grad_output * one, -1, keepdims=True) for one in picked]
    grad_expert = sum(
        jnp.einsum(
            "gst,gtd->gsd",
            pick,
            (gate * grad_output).astype(jnp.bfloat16).reshape(groups, GROUP, D),
            preferred_element_type=jnp.float32,
        )
        for pick, gate in zip(picks, gates)
    )
    grad_expert = by_expert(grad_expert.astype(jnp.bfloat16))
    grad_out_weight = jnp.einsum(
        "ecf,ecd->efd", hidden, grad_expert, preferred_element_type=jnp.float32
    )
    grad_out_bias = jnp.sum(grad_expert.astype(jnp.float32), 1)
    grad_hidden = jnp.einsum(
        "ecd,efd->ecf", grad_expert, weights[EXPERT_OUT], preferred_element_type=jnp.float32
    )
    grad_pre = gelu_backward(pre_act, grad_hidden).astype(jnp.bfloat16)
    grad_in_weight = jnp.einsum(
        "ecd,ecf->edf", dispatched, grad_pre, preferred_element_type=jnp.float32
    )
    grad_in_bias = jnp.sum(grad_pre.astype(jnp.float32), 1)
    grad_dispatched = jnp.einsum(
        "ecf,edf->ecd", grad_pre, weights[EXPERT_IN], preferred_element_type=jnp.float32
    )
    grad_slots = by_group(grad_dispatched.astype(jnp.bfloat16), groups)
    grad_normed = jnp.einsum(
        "gst,gsd->gtd", picks[0] + picks[1], grad_slots, preferred_element_type=jnp.float32
    ).reshape(-1, D)
    grad_probs = hots[0] * grad_gates[0] + hots[1] * grad_gates[1]
    inner_sum = jnp.sum(grad_probs * probs_all, -1, keepdims=True)
    grad_logits = (probs_all * (grad_probs - inner_sum)).astype(jnp.bfloat16)
    grad_router = jnp.einsum(
        "rd,re->de", normed_low, grad_logits, preferred_element_type=jnp.float32
    )
    grad_normed = grad_normed + jnp.einsum(
        "re,de->rd", grad_logits, weights[ROUTER], preferred_element_type=jnp.float32
    )
    return grad_normed, (grad_router, grad_in_weight, grad_in_bias, grad_out_weight, grad_out_bias)


def gather_small(shards):
    lengths = [shards[name].shape[0] for name in SMALL]
    joined = jnp.concatenate([shards[name].astype(jnp.bfloat16) for name in SMALL])
    whole = lax.all_gather(joined, "fsdp", axis=0)
    found, at = {}, 0
    for name, length in zip(SMALL, lengths):
        found[name] = whole[:, at : at + length].reshape(-1)
        at += length
    found[ROUTER] = found[ROUTER].reshape(D, EXPERTS)
    found[EXPERT_IN_BIAS] = found[EXPERT_IN_BIAS].reshape(EXPERTS, EXP_FF)
    found[EXPERT_OUT_BIAS] = found[EXPERT_OUT_BIAS].reshape(EXPERTS, D)
    return found


def scatter_small(grads, devices):
    joined = jnp.concatenate([grads[name].reshape(devices, -1) for name in SMALL], 1)
    width = joined.shape[1]
    mine = lax.psum_scatter(joined.reshape(-1), "fsdp", scatter_dimension=0, tiled=True)
    found, at = {}, 0
    for name in SMALL:
        length = grads[name].size // devices
        found[name] = mine[at : at + length]
        at += length
    return found


def on_device(devices, tokens, *rest):
    shards = dict(zip(NAMES, rest[: len(NAMES)]))
    routes, priority, cotangent = rest[len(NAMES) :]
    images = tokens.shape[0]
    groups = priority.shape[0]
    weights = gather_small(shards)
    for name in BIG_NAMES:
        whole = lax.all_gather(shards[name].astype(jnp.bfloat16), "fsdp", axis=0, tiled=True)
        weights[name] = whole.reshape(BIG[name])
    weights[EXPERT_IN] = weights[EXPERT_IN].reshape(EXPERTS, D, EXP_FF)
    weights[EXPERT_OUT] = weights[EXPERT_OUT].reshape(EXPERTS, EXP_FF, D)
    wide = {name: weights[name].astype(jnp.float32) for name in GAINS}
    stream0 = tokens.reshape(images * PATCH, D).astype(jnp.float32)
    grad4 = cotangent.reshape(images * PATCH, D).astype(jnp.float32)
    normed1 = norm_forward(stream0, wide[NORM1_GAIN], wide[NORM1_BIAS])
    out, attention1 = attention_forward(
        normed1, *(weights[name] for name in (QKV1, QUERY1, VALUE1, PROJ1, PROJ1_BIAS))
    )
    stream1 = stream0 + out
    normed2 = norm_forward(stream1, wide[NORM2_GAIN], wide[NORM2_BIAS])
    out, feed = feed_forward(
        normed2, *(weights[name] for name in (HIDDEN, HIDDEN_BIAS, OUTPUT, OUTPUT_BIAS))
    )
    stream2 = stream1 + out
    normed3 = norm_forward(stream2, wide[NORM3_GAIN], wide[NORM3_BIAS])
    out, attention2 = attention_forward(
        normed3, *(weights[name] for name in (QKV2, QUERY2, VALUE2, PROJ2, PROJ2_BIAS))
    )
    stream3 = stream2 + out
    normed4 = norm_forward(stream3, wide[NORM4_GAIN], wide[NORM4_BIAS])
    out, routed = routed_forward(normed4, weights, routes.reshape(groups, GROUP, 2), priority)
    activations = (stream3 + out).astype(jnp.bfloat16).reshape(tokens.shape)

    grads = {}

    def keep(names, values):
        grads.update(zip(names, values))

    grad, found = routed_backward(grad4, routed, weights)
    keep((ROUTER, EXPERT_IN, EXPERT_IN_BIAS, EXPERT_OUT, EXPERT_OUT_BIAS), found)
    back, *found = norm_backward(stream3, wide[NORM4_GAIN], wide[NORM4_BIAS], grad)
    keep((NORM4_GAIN, NORM4_BIAS), found)
    grad3 = grad4 + back
    grad, found = attention_backward(grad3, attention2, weights[QKV2], weights[PROJ2])
    keep((QKV2, QUERY2, VALUE2, PROJ2, PROJ2_BIAS), found)
    back, *found = norm_backward(stream2, wide[NORM3_GAIN], wide[NORM3_BIAS], grad)
    keep((NORM3_GAIN, NORM3_BIAS), found)
    grad2 = grad3 + back
    grad, found = feed_backward(grad2, feed, weights[HIDDEN], weights[OUTPUT])
    keep((HIDDEN, HIDDEN_BIAS, OUTPUT, OUTPUT_BIAS), found)
    back, *found = norm_backward(stream1, wide[NORM2_GAIN], wide[NORM2_BIAS], grad)
    keep((NORM2_GAIN, NORM2_BIAS), found)
    grad1 = grad2 + back
    grad, found = attention_backward(grad1, attention1, weights[QKV1], weights[PROJ1])
    keep((QKV1, QUERY1, VALUE1, PROJ1, PROJ1_BIAS), found)
    back, *found = norm_backward(stream0, wide[NORM1_GAIN], wide[NORM1_BIAS], grad)
    keep((NORM1_GAIN, NORM1_BIAS), found)
    input_grad = (grad1 + back).astype(jnp.bfloat16).reshape(tokens.shape)

    mine = scatter_small(grads, devices)
    for name in BIG_NAMES:
        flat = grads[name].reshape(-1)
        mine[name] = lax.psum_scatter(flat, "fsdp", scatter_dimension=0, tiled=True)
    return (activations, input_grad) + tuple(mine[name] for name in NAMES)


def solution(mesh):
    rows = P("fsdp", None, None)
    flat = tuple(P("fsdp") for _ in NAMES)
    devices = mesh.shape["fsdp"]
    return jax.shard_map(
        on_slice if devices == 32 else functools.partial(on_device, devices),
        mesh=mesh,
        in_specs=(rows,) + flat + (rows, P("fsdp", None), rows),
        out_specs=(rows, rows) + flat,
        check_vma=False,
    )
```
